32 devices in a mesh: dp: 8 (over y, x, core), fsdp: 4 (over z).
Axes of the slice: x: 2, y: 2, z: 4, core: 2. Of those that a mesh axis runs over, the one named last changes fastest.
Arguments:
- tokens: bfloat16 [32768, 768], P(('dp', 'fsdp')), may hold values from -6 to 6
- qkv_weight: float32 [768, 2304], P('fsdp', 'dp'), may hold values from -0.21875 to 0.21875
- out_weight: float32 [768, 768], P('fsdp', 'dp'), may hold values from -2.5 to 2.5
- fc_weight: float32 [768, 3072], P('fsdp', 'dp'), may hold values from -0.21875 to 0.21875
- proj_weight: float32 [3072, 768], P('fsdp', 'dp'), may hold values from -0.109375 to 0.109375
- fc_bias: float32 [3072], P('dp'), may hold values from -1.2 to 1.2
- vectors: float32 [8, 768], P(None, 'dp'), may hold values from -0.8 to 1.4, as said below
- cotangent: bfloat16 [32768, 768], P(('dp', 'fsdp')), may hold values from -6 to 6
- lengths: int32 [32], P(('dp', 'fsdp')), may hold values from 64 to 1024, as said below
- clip_norm: float32 [], replicated, may hold values from 12000 to 24000
- noise_qkv: float32 [768, 2304], P('fsdp', 'dp'), may hold values from -4 to 4
- noise_out: float32 [768, 768], P('fsdp', 'dp'), may hold values from -4 to 4
- noise_fc: float32 [768, 3072], P('fsdp', 'dp'), may hold values from -4 to 4
- noise_proj: float32 [3072, 768], P('fsdp', 'dp'), may hold values from -4 to 4
- noise_fc_bias: float32 [3072], P('dp'), may hold values from -4 to 4
- noise_vectors: float32 [8, 768], P(None, 'dp'), may hold values from -4 to 4
Outputs:
- block_out: bfloat16 [32768, 768], P(('dp', 'fsdp'))
- input_grad: bfloat16 [32768, 768], P(('dp', 'fsdp'))
- norm_ratio: float32 [32], P(('dp', 'fsdp'))
- grad_qkv: float32 [768, 2304], P('fsdp', 'dp')
- grad_out: float32 [768, 768], P('fsdp', 'dp')
- grad_fc: float32 [768, 3072], P('fsdp', 'dp')
- grad_proj: float32 [3072, 768], P('fsdp', 'dp')
- grad_fc_bias: float32 [3072], P('dp')
- grad_vectors: float32 [8, 768], P(None, 'dp')
The draws below stay inside these ranges and needn't reach their ends.
Inputs may be any that keep to these rules, and one draw needn't show every extreme that they name: `lengths`: each sequence's real length; at least one sequence has exactly 1024. `vectors`: gain rows near 1, bias rows of order a tenth.
All inputs are finite; a program needn't handle non-finite values.
Results may differ from the reference program's by a relative error of at most 0.014.
Values may be sent and summed in bfloat16 or wider, within the bound.
A program may use at most 320 MiB of HBM per device.

```python
import math
import jax
import jax.numpy as jnp
from jax import lax

D = 768
H = 12
HD = 64
FF = 3072
NVEC = 8
L = 1024
LMIN = 64
SEQS = 32
TOKENS = 32768
QB = 512


def draw_lengths(key, part):
    key = jax.random.fold_in(key, 11)
    first_key, second_key = jax.random.split(key)
    drawn = jax.random.randint(first_key, (SEQS,), LMIN, L + 1)
    chosen = jax.random.randint(second_key, (), 0, SEQS)
    return jnp.where(jnp.arange(SEQS) == chosen, L, drawn).astype(jnp.int32)


def draw_vectors(key, part):
    key = jax.random.fold_in(key, 23)
    scales = jnp.array([0.0, 0.1, 0.1, 0.05, 0.3, 0.0, 0.1, 0.3], jnp.float32)[:, None]
    gains = jnp.array([1.0, 0.0, 0.0, 0.0, 0.0, 1.0, 0.0, 0.0], jnp.float32)[:, None]
    noise = jax.random.truncated_normal(key, -2.5, 2.5, (NVEC, D), jnp.float32)
    return gains + (scales + 0.12 * gains) * noise


def levels(key, shape, cuts, least, top_value):
    level = 1.0
    for dim, parts in cuts:
        steps = jax.random.uniform(jax.random.fold_in(jax.random.fold_in(key, 6), dim), (parts,), jnp.float32, least / len(cuts), top_value / len(cuts))
        level = level * jnp.repeat(jnp.exp(steps), shape[dim] // parts).reshape((-1,) + (1,) * (len(shape) - 1 - dim))
    return level


def scatter_about(own_key, shape, width, most, cuts=(), held_as=jnp.bfloat16):
    gain = levels(own_key, shape, cuts, -0.22, 0.18) if cuts else 1.0
    values = jax.random.normal(own_key, shape, jnp.float32) * width * gain
    return jnp.minimum(jnp.maximum(values, -most), most).astype(held_as)


def setup_inputs(seed: int = 0) -> dict:
    streams_of = jax.random.split(jax.random.key(seed), 17)
    return {
        "tokens": scatter_about(streams_of[0], (TOKENS, D), 1.0, 6.0, ((0, 32),)),
        "qkv_weight": scatter_about(streams_of[1], (D, 3 * D), D ** -0.5, 0.21875, ((0, 4), (1, 8)), jnp.float32),
        "out_weight": scatter_about(streams_of[2], (D, D), (D * 8 // L) ** -0.5, 2.5, ((0, 4), (1, 8)), jnp.float32),
        "fc_weight": scatter_about(streams_of[3], (D, FF), D ** -0.5, 0.21875, ((0, 4), (1, 8)), jnp.float32),
        "proj_weight": scatter_about(streams_of[4], (FF, D), FF ** -0.5, 0.109375, ((0, 4), (1, 8)), jnp.float32),
        "fc_bias": scatter_about(streams_of[5], (FF,), 0.3, 1.2, ((0, 8),), jnp.float32),
        "vectors": draw_vectors(jax.random.fold_in(streams_of[16], 71), 0),
        "cotangent": scatter_about(streams_of[7], (TOKENS, D), 1.0, 6.0, ((0, 32),)),
        "lengths": draw_lengths(jax.random.fold_in(streams_of[16], 71), 0),
        "clip_norm": jnp.clip(jnp.exp(jax.random.uniform(streams_of[9], (), jnp.float32, math.log(12000.0), math.log(24000.0))), 12000.0, 24000.0),
        "noise_qkv": scatter_about(streams_of[10], (D, 3 * D), 0.5, 4.0, ((0, 4), (1, 8)), jnp.float32),
        "noise_out": scatter_about(streams_of[11], (D, D), 0.5, 4.0, ((0, 4), (1, 8)), jnp.float32),
        "noise_fc": scatter_about(streams_of[12], (D, FF), 0.5, 4.0, ((0, 4), (1, 8)), jnp.float32),
        "noise_proj": scatter_about(streams_of[13], (FF, D), 0.5, 4.0, ((0, 4), (1, 8)), jnp.float32),
        "noise_fc_bias": scatter_about(streams_of[14], (FF,), 0.5, 4.0, ((0, 8),), jnp.float32),
        "noise_vectors": scatter_about(streams_of[15], (NVEC, D), 0.5, 4.0, ((1, 8),), jnp.float32),
    }


@jax.custom_vjp
def low(v):
    return lax.optimization_barrier(v.astype(jnp.bfloat16)).astype(jnp.float32)

@jax.custom_vjp
def low_back(v):
    return v

def low_keep(v):
    return (low(v), None)

def low_pass(kept, grad):
    return (grad,)

def back_keep(v):
    return (v, None)

def back_low(kept, grad):
    return (low(grad),)
low.defvjp(low_keep, low_pass)
low_back.defvjp(back_keep, back_low)
epsilon = 1e-05
highest = lax.Precision.HIGHEST

def norm_layer(values, gain_row, shift_row):
    center = values - lax.optimization_barrier(jnp.mean(values, axis=-1, keepdims=True))
    spread = lax.optimization_barrier(jnp.mean(center * center, axis=-1, keepdims=True))
    return center * lax.rsqrt(spread + epsilon) * gain_row + shift_row

def product(left, right):
    return jnp.dot(left, right, precision=highest, preferred_element_type=jnp.float32)

def attention(queries, key_rows, value_rows, length):
    scaling = HD ** (-0.5)
    block_count = L // QB

    def one_block(position):
        offset = position * QB
        query_rows = lax.dynamic_slice_in_dim(queries, offset, QB, 0)
        scores = jnp.einsum('qhd,khd->hqk', query_rows, key_rows, precision=highest) * scaling
        scores = low_back(scores)
        places = offset + jnp.arange(QB, dtype=jnp.int32)
        key_places = jnp.arange(L, dtype=jnp.int32)
        allowed = (key_places[None, :] <= places[:, None]) & (key_places[None, :] < length)
        scores = jnp.where(allowed[None], scores, -1e+30)
        row_peak = lax.optimization_barrier(jnp.max(scores, axis=-1, keepdims=True))
        powers = jnp.exp(scores - row_peak)
        chances = low(powers / lax.optimization_barrier(jnp.sum(powers, axis=-1, keepdims=True)))
        return jnp.einsum('hqk,khd->qhd', chances, value_rows, precision=highest)
    blocks = lax.map(jax.checkpoint(one_block), jnp.arange(block_count, dtype=jnp.int32))
    return blocks.reshape(L, D)

def layer_forward(inputs, weight_qkv, weight_out, weight_fc, weight_proj, fc_shift, vector_rows, length):
    weight_qkv = low(weight_qkv)
    weight_out = low(weight_out)
    weight_fc = low(weight_fc)
    weight_proj = low(weight_proj)
    fc_shift = low(fc_shift)
    vector_rows = low(vector_rows)
    gain_one, shift_one, query_shift, value_shift = (vector_rows[0], vector_rows[1], vector_rows[2], vector_rows[3])
    out_shift, gain_two, shift_two, proj_shift = (vector_rows[4], vector_rows[5], vector_rows[6], vector_rows[7])
    normed_one = low(norm_layer(inputs, gain_one, shift_one))
    qkv_shift = jnp.concatenate([query_shift, jnp.zeros_like(query_shift), value_shift])
    mixed = low_back(low(product(normed_one, weight_qkv) + qkv_shift))
    heads_view = mixed.reshape(L, 3, H, HD)
    attended = attention(heads_view[:, 0], heads_view[:, 1], heads_view[:, 2], length)
    attended = low_back(low(attended))
    middle = inputs + low_back(product(attended, weight_out) + out_shift)
    normed_two = low(norm_layer(middle, gain_two, shift_two))
    hidden = low_back(product(normed_two, weight_fc) + fc_shift)
    activated = low(jax.nn.gelu(hidden, approximate=True))
    return middle + low_back(product(activated, weight_proj) + proj_shift)

def reference(tokens, qkv_weight, out_weight, fc_weight, proj_weight, fc_bias, vectors, cotangent, lengths, clip_norm, noise_qkv, noise_out, noise_fc, noise_proj, noise_fc_bias, noise_vectors):
    parameters = (qkv_weight, out_weight, fc_weight, proj_weight, fc_bias, vectors)

    def per_sequence(totals, position):
        inputs = lax.dynamic_slice_in_dim(tokens, position * L, L, 0).astype(jnp.float32)
        cot_rows = lax.dynamic_slice_in_dim(cotangent, position * L, L, 0).astype(jnp.float32)
        length = lengths[position]
        real_rows = (jnp.arange(L, dtype=jnp.int32) < length).astype(jnp.float32)

        def forward(inputs_in, params_in):
            return layer_forward(inputs_in, *params_in, length)
        output, pullback = jax.vjp(forward, inputs, parameters)
        grad_inputs, grads = pullback(cot_rows * real_rows[:, None])
        squares = sum((jnp.sum(member * member) for member in grads))
        grad_norm = jnp.sqrt(squares)
        factor = jnp.minimum(1.0, clip_norm / grad_norm)
        totals = jax.tree.map(lambda total_in, member: total_in + factor * member, totals, grads)
        return (totals, (output.astype(jnp.bfloat16), grad_inputs.astype(jnp.bfloat16), grad_norm / clip_norm))
    initial = jax.tree.map(jnp.zeros_like, parameters)
    totals, (outputs, input_grads, ratios) = lax.scan(per_sequence, initial, jnp.arange(SEQS, dtype=jnp.int32))
    noises = (noise_qkv, noise_out, noise_fc, noise_proj, noise_fc_bias, noise_vectors)
    finals = [total_in / SEQS + noise for total_in, noise in zip(totals, noises)]
    return (outputs.reshape(TOKENS, D), input_grads.reshape(TOKENS, D), ratios, finals[0], finals[1], finals[2], finals[3], finals[4], finals[5])
```

```python
import jax, jax.numpy as jnp
from jax import lax
from jax.experimental import pallas as pl
from jax.experimental.pallas import tpu as pltpu
P = jax.sharding.PartitionSpec
MESH = pl.DeviceIdType.MESH
bf16=jnp.bfloat16; f32=jnp.float32

def place():
    d = lax.axis_index("dp"); z = lax.axis_index("fsdp")
    core = d % 2; xx = (d // 2) % 2; yy = d // 4
    return d, z, d + 1 - 2*core, d + 2 - 4*xx, d + 4 - 8*yy

def greet(partners):
    bar = pltpu.get_barrier_semaphore()
    for dev in partners:
        pl.semaphore_signal(bar, inc=1, device_id=dev, device_id_type=MESH)
    pl.semaphore_wait(bar, len(partners))

class Gather:
    def __init__(self, shards, zq, zo, full, send, recv):
        self.sh = shards; self.zb = (zq, zo); self.full = full
        self.send = send; self.recv = recv
        self.d, self.z, self.sib, self.xn, self.yn = place()
        self.dg = self.xn + self.yn - self.d
        self.nz = lax.axis_size("fsdp")
    def cp(self, src, dst, w, slot, dev):
        return pltpu.make_async_remote_copy(src_ref=src, dst_ref=dst, send_sem=self.send.at[w, slot], recv_sem=self.recv.at[w, slot], device_id=dev, device_id_type=MESH)
    def block(self, w, d, half=None):
        ref = self.full[w]
        if w == 4:
            return ref.at[d] if half is None else ref.at[d, pl.ds(half * 8, 8)]
        if w == 2:
            cols = ref.shape[1] // 8
            cs = pl.ds(pl.multiple_of(d * cols, 128), cols)
            n = ref.shape[0]
            rs = pl.ds(0, n) if half is None else pl.ds(half * (n // 2), n // 2)
            return ref.at[rs, cs]
        rows = ref.shape[0] // 8
        if half is None:
            return ref.at[pl.ds(pl.multiple_of(d * rows, 16), rows), :]
        return ref.at[pl.ds(pl.multiple_of(d * rows + half * (rows // 2), 16), rows // 2), :]
    def zslot(self, w, z):
        if w < 2:
            return self.zb[w].at[z]
        ref = self.full[w]
        if w == 2:
            r, c = ref.shape[0] // self.nz, ref.shape[1] // 8
            return ref.at[pl.ds(pl.multiple_of(z * r, 16), r), pl.ds(pl.multiple_of(self.d * c, 128), c)]
        r, c = ref.shape[0] // 8, ref.shape[1] // self.nz
        return ref.at[pl.ds(pl.multiple_of(self.d * r, 16), r), pl.ds(pl.multiple_of(z * c, 128), c)]
    def partners(self):
        return [(self.d, (self.z + j) % self.nz) for j in range(1, self.nz)] + [(self.sib, self.z), (self.xn, self.z), (self.yn, self.z)]
    def zc(self, w, j, recv=False):
        other = (self.z - j + self.nz) % self.nz if recv else (self.z + j) % self.nz
        src = self.sh[w]
        dst = self.zslot(w, other if recv else self.z)
        return self.cp(src, dst, w, j - 1, (self.d, other))
    def start(self, w):
        if w == 4:
            self.block(w, self.d)[...] = self.sh[w][...]
            return
        for j in range(1, self.nz):
            self.zc(w, j).start()
        self.zslot(w, self.z)[...] = self.sh[w][...]
    def sibc(self, w, i, d):
        return self.cp(self.block(w, d), self.block(w, d), w, 7 + i, (self.sib, self.z))
    def bx(self, w, b, dev, slot, half=None):
        return self.cp(self.block(w, b, half), self.block(w, b, half), w, slot, (dev, self.z))
    def e1(self, w):
        if w < 4:
            for j in range(1, self.nz):
                self.zc(w, j, True).wait_recv()
        if w < 2:
            self.block(w, self.d)[...] = jnp.concatenate([self.zb[w][k] for k in range(self.nz)], axis=1)
        self.bx(w, self.d, self.xn, 3).start()
        self.bx(w, self.d, self.yn, 4).start()
        self.sibc(w, 0, self.d).start()
    def e2(self, w):
        self.bx(w, self.xn, self.xn, 3).wait_recv()
        self.bx(w, self.xn, self.yn, 5, 0).start()
        self.sibc(w, 1, self.xn).start()
    def e3(self, w):
        self.bx(w, self.yn, self.yn, 4).wait_recv()
        self.bx(w, self.yn, self.xn, 6, 1).start()
        self.sibc(w, 2, self.yn).start()
    def e4(self, w):
        self.bx(w, self.dg, self.yn, 5, 0).wait_recv()
        self.bx(w, self.dg, self.xn, 6, 1).wait_recv()
        self.sibc(w, 3, self.dg).start()
    def e5(self, w):
        o = self.sib - self.d
        for i, b in enumerate((self.d, self.xn, self.yn, self.dg)):
            self.sibc(w, i, b + o).wait_recv()
    def finish(self, w):
        if w < 4:
            for j in range(1, self.nz):
                self.zc(w, j).wait_send()
        self.bx(w, self.d, self.xn, 3).wait_send()
        self.bx(w, self.d, self.yn, 4).wait_send()
        self.bx(w, self.xn, self.yn, 5, 0).wait_send()
        self.bx(w, self.yn, self.xn, 6, 1).wait_send()
        for i, b in enumerate((self.d, self.xn, self.yn, self.dg)):
            self.sibc(w, i, b).wait_send()

def ag_kernel(sq, so, sf, sp, sv, QT, OT, F, PT, V, zq, zo, send, recv):
    g = Gather((sq, so, sf, sp, sv), zq, zo, (QT, OT, F, PT, V), send, recv)
    greet(g.partners())
    for w in (4, 0, 1, 2, 3): g.start(w)
    g.e1(4); g.e2(4); g.e3(4); g.e4(4)
    g.e1(0); g.e1(1); g.e2(0); g.e3(0); g.e1(2); g.e2(1); g.e3(1); g.e4(0); g.e4(1); g.e1(3)
    g.e2(2); g.e3(2); g.e4(2); g.e2(3); g.e3(3); g.e4(3)
    for w in range(5): g.e5(w)
    for w in range(5): g.finish(w)

def gather_all(sq, so, sf, sp, sv):
    ndp, nz = lax.axis_size("dp"), lax.axis_size("fsdp")
    D = sq.shape[1] * nz
    shapes = [(sq.shape[0]*ndp, D), (so.shape[0]*ndp, D), (D, sf.shape[1]*ndp), (sp.shape[0]*ndp, sp.shape[1]*nz)]
    vm = pl.BlockSpec(memory_space=pltpu.VMEM)
    return pl.pallas_call(ag_kernel, out_shape=[jax.ShapeDtypeStruct(s, bf16) for s in shapes] + [jax.ShapeDtypeStruct((ndp,) + sv.shape, f32)],
        in_specs=[vm]*5, out_specs=[vm]*5,
        scratch_shapes=[pltpu.VMEM((nz,)+sq.shape, bf16), pltpu.VMEM((nz,)+so.shape, bf16),
            pltpu.SemaphoreType.DMA((5, 11)), pltpu.SemaphoreType.DMA((5, 11))],
        compiler_params=pltpu.CompilerParams(collective_id=0, has_side_effects=True, vmem_limit_bytes=60<<20))(sq, so, sf, sp, sv)

class Scatter:
    def __init__(self, grads, sibs, ras, rbs, rxs, rys, zss, zrs, outs, cs, csend, crecv, send, recv):
        self.g = grads; self.sb = sibs; self.ra = ras; self.rb = rbs; self.rx = rxs; self.ry = rys
        self.zs = zss; self.zr = zrs; self.out = outs; self.send = send; self.recv = recv
        self.cs = cs; self.csend = csend; self.crecv = crecv
        self.d, self.z, self.sib, self.xn, self.yn = place()
        self.dg = self.xn + self.yn - self.d
        self.nz = lax.axis_size("fsdp")
    def partners(self):
        return [(self.d, (self.z + j) % self.nz) for j in range(1, self.nz)] + [(self.sib, self.z), (self.xn, self.z), (self.yn, self.z)]
    def cp(self, src, dst, w, slot, dev):
        return pltpu.make_async_remote_copy(src_ref=src, dst_ref=dst, send_sem=self.send.at[w, slot], recv_sem=self.recv.at[w, slot], device_id=dev, device_id_type=MESH)
    def block(self, w, d):
        ref = self.g[w]
        if w == 4:
            return ref.at[d]
        if w == 2:
            cols = ref.shape[1] // 8
            return ref.at[:, pl.ds(pl.multiple_of(d * cols, 128), cols)]
        rows = ref.shape[0] // 8
        return ref.at[pl.ds(pl.multiple_of(d * rows, 16), rows), :]
    def half(self, ref, h):
        n = ref.shape[0] // 2
        return ref.at[pl.ds(h * n, n)]
    def chips(self): return (self.dg, self.xn, self.yn, self.d)
    def sibc(self, w, i):
        o = self.sib - self.d
        return self.cp(self.block(w, self.chips()[i] + o), self.sb[w].at[i], w, i, (self.sib, self.z))
    def start_c(self, c):
        self.cs[0] = jnp.full((8, 128), c, f32)
        self.cc().start()
    def cc(self):
        return pltpu.make_async_remote_copy(src_ref=self.cs.at[0], dst_ref=self.cs.at[1], send_sem=self.csend, recv_sem=self.crecv, device_id=(self.sib, self.z), device_id_type=MESH)
    def s0(self, w):
        for i in range(4): self.sibc(w, i).start()
    def hsend(self, w, i, h, slot, dev, dst):
        return self.cp(self.half(self.sb[w].at[i], h), dst, w, slot, (dev, self.z))
    def ca(self, w): return self.hsend(w, 0, 0, 4, self.xn, self.ra[w])
    def cb(self, w): return self.hsend(w, 0, 1, 5, self.yn, self.rb[w])
    def cx(self, w, h): return self.hsend(w, 1, h, 6 + h, self.xn, self.half(self.rx[w], h))
    def cy(self, w, h): return self.hsend(w, 2, h, 8 + h, self.yn, self.half(self.ry[w], h))
    def mix(self, w, i):
        c0 = self.cs[0, 0:1, 0:1]; c1 = self.cs[1, 0:1, 0:1]
        ref = self.sb[w].at[i]
        ref[...] = (c0 * self.block(w, self.chips()[i])[...].astype(f32) + c1 * ref[...].astype(f32)).astype(ref.dtype)
    def a(self, w):
        self.sibc(w, 0).wait_recv(); self.mix(w, 0); self.ca(w).start(); self.cb(w).start()
        self.sibc(w, 1).wait_recv(); self.mix(w, 1); self.cx(w, 0).start()
        self.sibc(w, 2).wait_recv(); self.mix(w, 2); self.cy(w, 1).start()
    def r(self, w):
        self.ca(w).wait_recv()
        ref = self.half(self.sb[w].at[2], 0)
        ref[...] = (ref[...].astype(f32) + self.ra[w][...].astype(f32)).astype(ref.dtype)
        self.cy(w, 0).start()
        self.cb(w).wait_recv()
        ref = self.half(self.sb[w].at[1], 1)
        ref[...] = (ref[...].astype(f32) + self.rb[w][...].astype(f32)).astype(ref.dtype)
        self.cx(w, 1).start()
    def zpiece(self, w, k):
        if w in (0, 1): return self.zs[w].at[k]
        own = self.zs[w]
        if w == 4: return own
        if w == 2:
            r = own.shape[0] // self.nz
            return own.at[pl.ds(pl.multiple_of(k * r, 16), r)]
        c = own.shape[1] // self.nz
        return own.at[:, pl.ds(pl.multiple_of(k * c, 128), c)]
    def zc(self, w, j):
        to = (self.z + j) % self.nz
        return self.cp(self.zpiece(w, to), self.zr[w].at[j - 1], w, 9 + j, (self.d, to))
    def f(self, w):
        self.sibc(w, 3).wait_recv()
        for h in (0, 1):
            self.cx(w, h).wait_recv(); self.cy(w, h).wait_recv()
        c0 = self.cs[0, 0:1, 0:1]; c1 = self.cs[1, 0:1, 0:1]
        t = c0 * self.block(w, self.d)[...].astype(f32) + c1 * self.sb[w][3].astype(f32)
        t = t + self.rx[w][...].astype(f32) + self.ry[w][...].astype(f32)
        if w in (0, 1):
            c = t.shape[1] // self.nz
            for k in range(self.nz): self.zs[w][k] = t[:, k * c:(k + 1) * c].astype(bf16)
        else:
            self.zs[w][...] = t.astype(self.zs[w].dtype)
        for j in range(1, self.nz): self.zc(w, j).start()
    def zf(self, w):
        for j in range(1, self.nz): self.zc(w, j).wait_recv()
        t = self.zpiece(w, self.z)[...].astype(f32)
        for j in range(self.nz - 1): t = t + self.zr[w][j].astype(f32)
        self.out[w][...] = t
    def finish(self, w):
        for i in range(4): self.sibc(w, i).wait_send()
        self.ca(w).wait_send(); self.cb(w).wait_send()
        for h in (0, 1): self.cx(w, h).wait_send(); self.cy(w, h).wait_send()
        for j in range(1, self.nz): self.zc(w, j).wait_send()

def rs_kernel(*refs):
    c, *refs = refs
    take = lambda n: [refs.pop(0) for _ in range(n)]
    grads = take(5); outs = take(5)
    sibs, ras, rbs, rxs, rys, zss, zrs = (take(5) for _ in range(7))
    cs, csend, crecv, send, recv = refs
    s = Scatter(grads, sibs, ras, rbs, rxs, rys, zss, zrs, outs, cs, csend, crecv, send, recv)
    greet(s.partners())
    s.start_c(c[0, 0])
    for w in (1, 0, 2, 3, 4): s.s0(w)
    s.cc().wait_recv()
    q, o, f, p, v = range(5)
    s.a(o); s.a(v); s.a(q); s.r(o); s.r(v); s.a(f); s.r(q); s.f(o); s.f(v); s.a(p); s.r(f); s.f(q); s.r(p); s.f(f)
    s.zf(o); s.zf(v); s.zf(q); s.f(p); s.zf(f); s.zf(p)
    s.cc().wait_send()
    for w in range(5): s.finish(w)

def scatter_all(c, gq, go, gf, gp, gv):
    nz = lax.axis_size("fsdp")
    grads = (gq, go, gf, gp, gv)
    blocks = [(gq.shape[0]//8, gq.shape[1]), (go.shape[0]//8, go.shape[1]), (gf.shape[0], gf.shape[1]//8), (gp.shape[0]//8, gp.shape[1]), gv.shape[1:]]
    dt = [bf16]*4 + [f32]
    hb = [(r//2, c_) for r, c_ in blocks]
    piece = [(r, c_//nz) for r, c_ in blocks[:2]] + [(blocks[2][0]//nz, blocks[2][1]), (blocks[3][0], blocks[3][1]//nz), blocks[4]]
    zs = [(nz,)+piece[0], (nz,)+piece[1]] + blocks[2:]
    zr = [(nz-1,)+s for s in piece]
    V = lambda ss: [pltpu.VMEM(s, t) for s, t in zip(ss, dt)]
    vm = pl.BlockSpec(memory_space=pltpu.VMEM)
    return pl.pallas_call(rs_kernel, out_shape=[jax.ShapeDtypeStruct(s, f32) for s in piece],
        in_specs=[pl.BlockSpec(memory_space=pltpu.SMEM)] + [vm]*5, out_specs=[vm]*5,
        scratch_shapes=V([(4,)+b for b in blocks]) + V(hb) + V(hb) + V(blocks) + V(blocks) + V(zs) + V(zr)
            + [pltpu.VMEM((2, 8, 128), f32), pltpu.SemaphoreType.DMA, pltpu.SemaphoreType.DMA, pltpu.SemaphoreType.DMA((5, 13)), pltpu.SemaphoreType.DMA((5, 13))],
        compiler_params=pltpu.CompilerParams(collective_id=1, has_side_effects=True, vmem_limit_bytes=60<<20))(c, *grads)


HD = 64


epsilon = 1e-05


def norm_layer(values, gain_row, shift_row):
    center = values - jnp.mean(values, axis=-1, keepdims=True)
    spread = jnp.mean(center * center, axis=-1, keepdims=True)
    return center * lax.rsqrt(spread + epsilon) * gain_row + shift_row


def gelu_tanh(values):
    return jax.nn.gelu(values, approximate=True)


def masked_scores(query_rows, key_rows, offset, length, scaling):
    scores = (
        jnp.einsum("qhd,khd->hqk", query_rows, key_rows, preferred_element_type=jnp.float32)
        * scaling
    )
    places = offset + jnp.arange(query_rows.shape[0], dtype=jnp.int32)
    key_places = jnp.arange(key_rows.shape[0], dtype=jnp.int32)
    allowed = (key_places[None, :] <= places[:, None]) & (key_places[None, :] < length)
    return jnp.where(allowed[None], scores, -1e30)


def attend(queries, key_rows, value_rows, length, block_rows, scaling):
    results = []
    log_parts = []
    for offset in range(0, queries.shape[0], block_rows):
        scores = masked_scores(
            queries[offset : offset + block_rows], key_rows, offset, length, scaling
        )
        row_peak = jnp.max(scores, axis=-1, keepdims=True)
        powers = jnp.exp(scores - row_peak)
        row_total = jnp.sum(powers, axis=-1, keepdims=True)
        chances = (powers / row_total).astype(jnp.bfloat16)
        results.append(
            jnp.einsum("hqk,khd->qhd", chances, value_rows, preferred_element_type=jnp.float32)
        )
        log_parts.append(row_peak + jnp.log(row_total))
    return (jnp.concatenate(results, axis=0), jnp.concatenate(log_parts, axis=1))


def attend_back(queries, key_rows, value_rows, grad_rows, log_sums, length, block_rows, scaling):
    grad_query = []
    grad_key = jnp.zeros(key_rows.shape, jnp.float32)
    grad_value = jnp.zeros(value_rows.shape, jnp.float32)
    for offset in range(0, queries.shape[0], block_rows):
        query_rows = queries[offset : offset + block_rows]
        scores = masked_scores(query_rows, key_rows, offset, length, scaling)
        chances = jnp.exp(scores - log_sums[:, offset : offset + block_rows])
        grad_block = grad_rows[offset : offset + block_rows]
        grad_value = grad_value + jnp.einsum(
            "hqk,qhd->khd",
            chances.astype(jnp.bfloat16),
            grad_block,
            preferred_element_type=jnp.float32,
        )
        grad_chances = jnp.einsum(
            "qhd,khd->hqk", grad_block, value_rows, preferred_element_type=jnp.float32
        )
        inner = jnp.sum(chances * grad_chances, axis=-1, keepdims=True)
        grad_scores = (chances * (grad_chances - inner)).astype(jnp.bfloat16)
        grad_query.append(
            jnp.einsum("hqk,khd->qhd", grad_scores, key_rows, preferred_element_type=jnp.float32)
            * scaling
        )
        grad_key = (
            grad_key
            + jnp.einsum(
                "hqk,qhd->khd", grad_scores, query_rows, preferred_element_type=jnp.float32
            )
            * scaling
        )
    return (jnp.concatenate(grad_query, axis=0), grad_key, grad_value)


def shards(
    tokens,
    qkv_weight,
    out_weight,
    fc_weight,
    proj_weight,
    fc_bias,
    vectors,
    cotangent,
    lengths,
    clip_norm,
    noise_qkv,
    noise_out,
    noise_fc,
    noise_proj,
    noise_fc_bias,
    noise_vectors,
):
    seq_count = lengths.shape[0]
    seq_len = tokens.shape[0] // seq_count
    width = tokens.shape[1]
    head_size = HD
    head_count = width // head_size
    block_rows = min(512, seq_len)
    scaling = head_size ** (-0.5)
    ndp = lax.axis_size("dp")
    rows = fc_bias.shape[0] // 128 + vectors.size // 128 if ndp == 8 else 0
    if ndp == 8:
        small = jnp.concatenate([fc_bias.reshape(-1, 128), vectors.reshape(-1, 128)], axis=0)
        small = jnp.pad(small, ((0, 16 - small.shape[0]), (0, 0)))
        QT, OT, weight_fc, PT, small = gather_all(
            qkv_weight.astype(bf16).T, out_weight.astype(bf16).T, fc_weight.astype(bf16), proj_weight.astype(bf16).T, small)
        nb = fc_bias.shape[0] // 128
        fc_shift = small[:, :nb].reshape(-1).astype(bf16).astype(f32)
        vector_rows = small[:, nb:rows].reshape(ndp, vectors.shape[0], vectors.shape[1]).transpose(1, 0, 2).reshape(vectors.shape[0], -1)
        vector_rows = vector_rows.astype(bf16).astype(f32)
        weight_qkv, weight_out, weight_proj = QT.T, OT.T, PT.T
    else:
        g = lambda a: lax.all_gather(lax.all_gather(a.astype(bf16), "dp", axis=1, tiled=True), "fsdp", axis=0, tiled=True)
        weight_qkv, weight_out, weight_fc, weight_proj = g(qkv_weight), g(out_weight), g(fc_weight), g(proj_weight)
        vector_rows = lax.all_gather(vectors.astype(bf16), "dp", axis=1, tiled=True).astype(f32)
        fc_shift = lax.all_gather(fc_bias.astype(bf16), "dp", axis=0, tiled=True).astype(f32)
    gain_one, shift_one, query_shift, value_shift, out_shift, gain_two, shift_two, proj_shift = vector_rows
    qkv_shift = jnp.concatenate([query_shift, jnp.zeros_like(query_shift), value_shift])
    seq = 0
    inputs = tokens.astype(jnp.float32)
    length = lengths[seq]
    normed_one = norm_layer(inputs, gain_one, shift_one).astype(jnp.bfloat16)
    mixed = (
        jnp.dot(normed_one, weight_qkv, preferred_element_type=jnp.float32) + qkv_shift
    ).astype(jnp.bfloat16)
    heads_view = mixed.reshape(seq_len, 3, head_count, head_size)
    attended, log_sums = attend(
        heads_view[:, 0], heads_view[:, 1], heads_view[:, 2], length, block_rows, scaling
    )
    attended = attended.reshape(seq_len, width).astype(jnp.bfloat16)
    middle = inputs + jnp.dot(attended, weight_out, preferred_element_type=jnp.float32) + out_shift
    normed_two = norm_layer(middle, gain_two, shift_two).astype(jnp.bfloat16)
    hidden = jnp.dot(normed_two, weight_fc, preferred_element_type=jnp.float32) + fc_shift
    activated = gelu_tanh(hidden).astype(jnp.bfloat16)
    result = (
        middle + jnp.dot(activated, weight_proj, preferred_element_type=jnp.float32) + proj_shift
    )
    outputs = result.astype(jnp.bfloat16)
    saved = [
        (inputs, normed_one, heads_view, log_sums, attended, middle, normed_two, hidden, activated)
    ]
    back_fc, back_proj, back_qkv, back_out = weight_fc, weight_proj, weight_qkv, weight_out
    seq = 0
    inputs, normed_one, heads_view, log_sums, attended, middle, normed_two, hidden, activated = (
        saved[seq]
    )
    length = lengths[seq]
    real_rows = (jnp.arange(seq_len, dtype=jnp.int32) < length).astype(jnp.float32)[:, None]
    grad_y = cotangent.astype(jnp.float32) * real_rows
    grad_branch = grad_y.astype(jnp.bfloat16)
    grad_proj = jnp.dot(activated.T, grad_branch, preferred_element_type=jnp.float32)
    grad_pshift = jnp.sum(grad_branch.astype(jnp.float32), axis=0)
    grad_act = jnp.dot(grad_branch, back_proj.T, preferred_element_type=jnp.float32)
    gelu_out, gelu_pull = jax.vjp(gelu_tanh, hidden)
    grad_hidden = gelu_pull(grad_act)[0].astype(jnp.bfloat16)
    grad_fc = jnp.dot(normed_two.T, grad_hidden, preferred_element_type=jnp.float32)
    grad_fshift = jnp.sum(grad_hidden.astype(jnp.float32), axis=0)
    grad_normed_two = jnp.dot(grad_hidden, back_fc.T, preferred_element_type=jnp.float32)
    norm_out, second_pull = jax.vjp(norm_layer, middle, gain_two, shift_two)
    grad_mid, grad_gain_two, grad_shift_two = second_pull(grad_normed_two)
    grad_mid = grad_y + grad_mid
    grad_attn = grad_mid.astype(jnp.bfloat16)
    grad_out = jnp.dot(attended.T, grad_attn, preferred_element_type=jnp.float32)
    grad_oshift = jnp.sum(grad_attn.astype(jnp.float32), axis=0)
    grad_heads = jnp.dot(grad_attn, back_out.T, preferred_element_type=jnp.float32).astype(
        jnp.bfloat16
    )
    grad_heads = grad_heads.reshape(seq_len, head_count, head_size)
    grad_query, grad_key, grad_value = attend_back(
        heads_view[:, 0],
        heads_view[:, 1],
        heads_view[:, 2],
        grad_heads,
        log_sums,
        length,
        block_rows,
        scaling,
    )
    grad_mixed = (
        jnp.stack([grad_query, grad_key, grad_value], axis=1)
        .reshape(seq_len, 3 * width)
        .astype(jnp.bfloat16)
    )
    grad_qkv = jnp.dot(normed_one.T, grad_mixed, preferred_element_type=jnp.float32)
    grad_mshift = jnp.sum(grad_mixed.astype(jnp.float32), axis=0)
    grad_normed_one = jnp.dot(grad_mixed, back_qkv.T, preferred_element_type=jnp.float32)
    first_out, first_pull = jax.vjp(norm_layer, inputs, gain_one, shift_one)
    grad_in, grad_gain_one, grad_shift_one = first_pull(grad_normed_one)
    input_grads = (grad_mid + grad_in).astype(jnp.bfloat16)
    grad_vec = jnp.stack(
        [
            grad_gain_one,
            grad_shift_one,
            grad_mshift[:width],
            grad_mshift[2 * width :],
            grad_oshift,
            grad_gain_two,
            grad_shift_two,
            grad_pshift,
        ]
    )
    per_seq = (grad_qkv, grad_out, grad_fc, grad_proj, grad_fshift, grad_vec)
    squares = sum((jnp.sum(member * member) for member in per_seq))
    grad_norm = jnp.sqrt(squares)
    factor = jnp.minimum(1.0, clip_norm / grad_norm)
    ratios = [grad_norm / clip_norm]
    if ndp == 8:
        nb = fc_bias.shape[0] // 128
        gv = jnp.concatenate([grad_fshift.reshape(ndp, nb, 128), grad_vec.reshape(8, ndp, -1).transpose(1, 0, 2).reshape(ndp, -1, 128)], axis=1)
        gv = jnp.pad(gv, ((0, 0), (0, 16 - gv.shape[1]), (0, 0)))
        sq, so, sf, sp, sv = scatter_all(factor.reshape(1, 1), grad_qkv.T.astype(bf16), grad_out.T.astype(bf16), grad_fc.astype(bf16), grad_proj.T.astype(bf16), gv)
        finals = (sq.T, so.T, sf, sp.T, sv[:nb].reshape(-1), sv[nb:rows].reshape(vectors.shape))
    else:
        ps = lambda a, dim: lax.psum_scatter(factor * a, "dp", scatter_dimension=dim, tiled=True)
        pz = lambda a: lax.psum_scatter(a.astype(bf16), "fsdp", scatter_dimension=0, tiled=True).astype(f32)
        finals = tuple(pz(ps(a, 1)) for a in per_seq[:4]) + lax.psum((ps(per_seq[4], 0), ps(per_seq[5], 1)), "fsdp")
    examples = lax.axis_size("dp") * lax.axis_size("fsdp") * seq_count
    return (
        outputs,
        input_grads,
        jnp.stack(ratios),
        finals[0] / examples + noise_qkv,
        finals[1] / examples + noise_out,
        finals[2] / examples + noise_fc,
        finals[3] / examples + noise_proj,
        finals[4] / examples + noise_fc_bias,
        finals[5] / examples + noise_vectors,
    )


def solution(mesh):
    placed = (
        P(("dp", "fsdp"), None),
        P("fsdp", "dp"),
        P("fsdp", "dp"),
        P("fsdp", "dp"),
        P("fsdp", "dp"),
        P("dp"),
        P(None, "dp"),
        P(("dp", "fsdp"), None),
        P(("dp", "fsdp")),
        P(),
        P("fsdp", "dp"),
        P("fsdp", "dp"),
        P("fsdp", "dp"),
        P("fsdp", "dp"),
        P("dp"),
        P(None, "dp"),
    )
    return jax.shard_map(
        shards,
        mesh=mesh,
        in_specs=placed,
        out_specs=(
            P(("dp", "fsdp"), None),
            P(("dp", "fsdp"), None),
            P(("dp", "fsdp")),
            P("fsdp", "dp"),
            P("fsdp", "dp"),
            P("fsdp", "dp"),
            P("fsdp", "dp"),
            P("dp"),
            P(None, "dp"),
        ),
        check_vma=False,
    )
```

```python
import functools
import jax
import jax.numpy as jnp
from jax import lax
from jax.experimental import pallas as pl
from jax.experimental.pallas import tpu as pltpu
from jax.sharding import PartitionSpec as P

MESH = pl.DeviceIdType.MESH
f32 = jnp.float32
bf16 = jnp.bfloat16
HD=64; T=256; QB=256
EPS=1e-05
GC=0.7978845608028654
GA=0.044715

def nn(a, b): return lax.dot_general(a, b, (((1,), (0,)), ((), ())), preferred_element_type=f32)
def nt(a, b): return lax.dot_general(a, b, (((1,), (1,)), ((), ())), preferred_element_type=f32)
def at(i, n): return pl.ds(pl.multiple_of(i * n, n), n)
def loop(n, body): lax.fori_loop(0, n, lambda i, c: (body(i), c)[1], 0)

class Block:
    def __init__(s, **refs): s.__dict__.update(refs)
    def unpack(s):
        V = s.V
        n = V.shape[0]; w = s.x.shape[1] // n; k = s.bf.shape[1] // n // 128
        s.vec[...] = jnp.concatenate([V[d][0:8, 0:w] for d in range(n)], axis=1).astype(bf16).astype(f32)
        s.bf[...] = jnp.concatenate([V[d][8 + j:9 + j, :] for d in range(n) for j in range(k)], axis=1).astype(bf16).astype(f32)
        s.clear()
    def clear(s):
        s.col[...] = jnp.zeros_like(s.col); s.ssq[...] = jnp.zeros_like(s.ssq)
        L = s.x.shape[0]
        kp = lax.broadcasted_iota(jnp.int32, (L, 128), 0)
        s.kb[...] = jnp.where(kp < s.length, 0.0, -1e30).astype(bf16)
    def row(s, i): return s.vec[i:i + 1, :]
    def ln1(s):
        def body(i):
            x = s.x[at(i, T), :].astype(f32)
            c = x - jnp.mean(x, axis=1, keepdims=True)
            v = jnp.mean(c * c, axis=1, keepdims=True)
            s.n1[at(i, T), :] = (c * lax.rsqrt(v + EPS) * s.row(0) + s.row(1)).astype(bf16)
        loop(s.x.shape[0] // T, body)
    def qkv(s):
        D = s.x.shape[1]
        for part, b in ((0, 2), (1, None), (2, 3)):
            def body(i):
                o = nt(s.n1[...], s.QT[pl.ds(pl.multiple_of(part * D + i * T, T), T), :])
                if b is not None: o = o + s.vec[b:b + 1, at(i, T)]
                s.m[:, pl.ds(pl.multiple_of(part * D + i * T, T), T)] = o.astype(bf16)
            loop(D // T, body)
    def heads(s, hp):
        D = s.x.shape[1]
        q = s.m[:, at(hp, 128)] * bf16(HD ** -0.5)
        k = s.m[:, pl.ds(pl.multiple_of(D + hp * 128, 128), 128)]
        v = s.m[:, pl.ds(pl.multiple_of(2 * D + hp * 128, 128), 128)]
        return q, k, v
    def masked(s, q, k, h):
        lane = lax.broadcasted_iota(jnp.int32, q.shape, 1)
        mine = (lane // HD) == h
        free = lane == (1 - h) * HD
        zero = jnp.zeros_like(q)
        return jnp.where(mine, q, jnp.where(free, jnp.ones_like(q), zero)), jnp.where(mine, k, jnp.where(free, s.kb[...], zero))
    def scores(s, kh, qh, b):
        qq = qh[b * QB:(b + 1) * QB]
        parts = []
        if b: parts.append(nt(kh[:b * QB], qq))
        o = nt(kh[b * QB:(b + 1) * QB], qq)
        r = lax.broadcasted_iota(jnp.int32, o.shape, 0); c = lax.broadcasted_iota(jnp.int32, o.shape, 1)
        parts.append(jnp.where(r <= c, o, -1e30))
        return parts
    def attend(s, hp):
        L = s.x.shape[0]
        q, k, v = s.heads(hp)
        vt = v.T
        outs = []
        for h in (0, 1):
            qh, kh = s.masked(q, k, h)
            for b in range(L // QB):
                parts = s.scores(kh, qh, b)
                mx = jnp.max(parts[-1], axis=0, keepdims=True)
                if b: mx = jnp.maximum(mx, jnp.max(parts[0], axis=0, keepdims=True))
                es = [jnp.exp(p - mx) for p in parts]
                l = sum(jnp.sum(e, axis=0, keepdims=True) for e in es)
                o = nn(vt[h * HD:(h + 1) * HD, b * QB:(b + 1) * QB], es[-1].astype(bf16))
                if b: o = o + nn(vt[h * HD:(h + 1) * HD, :b * QB], es[0].astype(bf16))
                s.lse[hp, h:h + 1, b * QB:(b + 1) * QB] = mx + jnp.log(l)
                s.ot[h * HD:(h + 1) * HD, b * QB:(b + 1) * QB] = o / l
        s.A[:, at(hp, 128)] = s.ot[...].T.astype(bf16)
    def out(s):
        def body(i):
            o = nt(s.A[...], s.OT[at(i, T), :])
            s.r[:, at(i, T)] = s.x[:, at(i, T)].astype(f32) + o + s.vec[4:5, at(i, T)]
        loop(s.x.shape[1] // T, body)
    def ln2(s):
        def body(i):
            x = s.r[at(i, T), :]
            c = x - jnp.mean(x, axis=1, keepdims=True)
            v = jnp.mean(c * c, axis=1, keepdims=True)
            s.n2[at(i, T), :] = (c * lax.rsqrt(v + EPS) * s.row(5) + s.row(6)).astype(bf16)
        loop(s.x.shape[0] // T, body)
    def fc(s):
        def body(i):
            f = nn(s.n2[...], s.F[:, at(i, T)]) + s.bf[:, at(i, T)]
            f2 = f * f
            t = jnp.tanh(f * (GC + GC * GA * f2))
            p = 0.5 * t + 0.5
            u = f * p
            s.u[:, at(i, T)] = u.astype(bf16)
            s.gp[:, at(i, T)] = (p + u * (1.0 - p) * (2 * GC + 6 * GC * GA * f2)).astype(bf16)
        loop(s.u.shape[1] // T, body)
    def ey_mask(s):
        def body(i):
            rp = i * T + lax.broadcasted_iota(jnp.int32, (T, s.x.shape[1]), 0)
            e = jnp.where(rp < s.length, s.ey[at(i, T), :].astype(f32), 0.0)
            s.ey[at(i, T), :] = e.astype(bf16)
            s.col[7:8, :] += jnp.sum(e, axis=0, keepdims=True)
        loop(s.x.shape[0] // T, body)
    def wgrad(s, lhs, rhs, out, nw, cols, first=0):
        N = cols; M = out.shape[0]
        def cp(i): return pltpu.make_async_copy(s.stage.at[i % 2, :, pl.ds(0, N)], out.at[at(i, T), :], s.dsem.at[i % 2])
        def body(i):
            s.lt[...] = lhs[:, at(i, T)].T
            @pl.when(i >= 2)
            def _(): cp(i - 2).wait()
            def inner(j):
                o = nn(s.lt[...], rhs[:, at(j, nw)])
                s.ssq[:, 0:nw] += jnp.sum(o * o, axis=0, keepdims=True)
                s.stage[i % 2, :, at(j, nw)] = o.astype(bf16)
            loop(N // nw, inner)
            cp(i).start()
        n = M // T
        loop(n, body)
        cp(n - 2).wait(); cp(n - 1).wait()
    def y(s):
        def body(i):
            o = nt(s.u[...], s.PT[at(i, T), :])
            s.er[:, at(i, T)] = (s.r[:, at(i, T)] + o + s.vec[7:8, at(i, T)]).astype(bf16)
        loop(s.x.shape[1] // T, body)
    def ef(s):
        def body(i):
            g = nn(s.ey[...], s.PT[:, at(i, T)]) * s.gp[:, at(i, T)].astype(f32)
            e = g.astype(bf16)
            s.gp[:, at(i, T)] = e
            s.dbf[:, at(i, T)] = jnp.sum(e.astype(f32), axis=0, keepdims=True)
        loop(s.u.shape[1] // T, body)
    def gn2(s):
        def body(i):
            s.G[:, at(i, T)] = nt(s.gp[...], s.F[at(i, T), :])
        loop(s.x.shape[1] // T, body)
    def lnb(s, x, gn, gain):
        c = x - jnp.mean(x, axis=1, keepdims=True)
        v = jnp.mean(c * c, axis=1, keepdims=True)
        rs = lax.rsqrt(v + EPS)
        h = c * rs
        a = gn * gain
        return h, rs * (a - jnp.mean(a, axis=1, keepdims=True) - h * jnp.mean(a * h, axis=1, keepdims=True))
    def ln2b(s):
        def body(i):
            gn = s.G[at(i, T), :]
            h, g = s.lnb(s.r[at(i, T), :], gn, s.row(5))
            s.col[5:6, :] += jnp.sum(gn * h, axis=0, keepdims=True)
            s.col[6:7, :] += jnp.sum(gn, axis=0, keepdims=True)
            g = g + s.ey[at(i, T), :].astype(f32)
            s.r[at(i, T), :] = g
            e = g.astype(bf16)
            s.er[at(i, T), :] = e
            s.col[4:5, :] += jnp.sum(e.astype(f32), axis=0, keepdims=True)
        loop(s.x.shape[0] // T, body)
    def eA(s):
        def body(i):
            s.n2[:, at(i, T)] = nn(s.er[...], s.OT[:, at(i, T)]).astype(bf16)
        loop(s.x.shape[1] // T, body)
    def attend_back(s, hp):
        L, D = s.x.shape
        q, k, v = s.heads(hp)
        e = s.n2[:, at(hp, 128)]
        kt = k.T
        ea = (e.astype(f32) * s.A[:, at(hp, 128)].astype(f32)).T
        lane = lax.broadcasted_iota(jnp.int32, e.shape, 1)
        s.dk[...] = jnp.zeros_like(s.dk); s.dv[...] = jnp.zeros_like(s.dv)
        for h in (0, 1):
            qh, kh = s.masked(q, k, h)
            mine = (lane // HD) == h
            eh = jnp.where(mine, e, jnp.zeros_like(e))
            qz = jnp.where(mine, q, jnp.zeros_like(q))
            delta = jnp.sum(ea[h * HD:(h + 1) * HD, :], axis=0, keepdims=True)
            for b in range(L // QB):
                cols = slice(b * QB, (b + 1) * QB)
                n = (b + 1) * QB
                parts = s.scores(kh, qh, b)
                lse = s.lse[hp, h:h + 1, cols]
                P = [jnp.exp(p - lse) for p in parts]
                dP = nt(v[:n], eh[cols])
                dl = delta[:, cols]
                dS = [(P[-1] * (dP[n - QB:] - dl)).astype(bf16)]
                if b: dS = [(P[0] * (dP[:n - QB] - dl)).astype(bf16)] + dS
                for i, (p, ds) in enumerate(zip(P, dS)):
                    rows = slice(n - QB, n) if i == len(P) - 1 else slice(0, n - QB)
                    s.dv[rows, :] += nn(p.astype(bf16), eh[cols])
                    s.dk[rows, :] += nn(ds, qz[cols])
                o = nn(kt[h * HD:(h + 1) * HD, n - QB:n], dS[-1])
                if b: o = o + nn(kt[h * HD:(h + 1) * HD, :n - QB], dS[0])
                s.ot[h * HD:(h + 1) * HD, cols] = o * (HD ** -0.5)
        s.u[:, at(hp, 128)] = s.ot[...].T.astype(bf16)
        s.u[:, pl.ds(pl.multiple_of(D + hp * 128, 128), 128)] = s.dk[...].astype(bf16)
        s.u[:, pl.ds(pl.multiple_of(2 * D + hp * 128, 128), 128)] = s.dv[...].astype(bf16)
    def bias_cols(s):
        D = s.x.shape[1]
        def body(i):
            s.col[2:3, :] += jnp.sum(s.u[at(i, T), 0:D].astype(f32), axis=0, keepdims=True)
            s.col[3:4, :] += jnp.sum(s.u[at(i, T), 2 * D:3 * D].astype(f32), axis=0, keepdims=True)
        loop(s.x.shape[0] // T, body)
    def gn1(s):
        D = s.x.shape[1]
        def body(i):
            s.G[:, at(i, T)] = nn(s.u[:, 0:3 * D], s.QT[:, at(i, T)])
        loop(D // T, body)
    def ln1b(s):
        def body(i):
            gn = s.G[at(i, T), :]
            h, g = s.lnb(s.x[at(i, T), :].astype(f32), gn, s.row(0))
            s.col[0:1, :] += jnp.sum(gn * h, axis=0, keepdims=True)
            s.col[1:2, :] += jnp.sum(gn, axis=0, keepdims=True)
            s.er[at(i, T), :] = (s.r[at(i, T), :] + g).astype(bf16)
        loop(s.x.shape[0] // T, body)
    def norm(s):
        t = jnp.sum(s.ssq[...]) + jnp.sum(s.dbf[...] * s.dbf[...]) + jnp.sum(s.col[...] * s.col[...])
        return t

def scratch(L, D, FF, rows=None):
    return dict(
        vec=pltpu.VMEM((8, D), f32), bf=pltpu.VMEM((1, FF), f32), col=pltpu.VMEM((8, D), f32), dbf=pltpu.VMEM((1, FF), f32),
        ssq=pltpu.VMEM((1, 512), f32), kb=pltpu.VMEM((L, 128), bf16),
        n1=pltpu.VMEM((L, D), bf16), m=pltpu.VMEM((L, 3 * D), bf16), A=pltpu.VMEM((L, D), bf16), r=pltpu.VMEM((L, D), f32),
        n2=pltpu.VMEM((L, D), bf16), u=pltpu.VMEM((L, FF), bf16), gp=pltpu.VMEM((L, FF), bf16), er=pltpu.VMEM((L, D), bf16),
        G=pltpu.VMEM((L, D), f32), stage=pltpu.VMEM((2, T, FF), bf16), lt=pltpu.VMEM((T, L), bf16),
        lse=pltpu.VMEM((D // 128, 2, L), f32), ot=pltpu.VMEM((128, L), f32), dk=pltpu.VMEM((L, 128), f32), dv=pltpu.VMEM((L, 128), f32),
        x=pltpu.VMEM((L, D), bf16), ey=pltpu.VMEM((L, D), bf16),
        dsem=pltpu.SemaphoreType.DMA((2,)), isem=pltpu.SemaphoreType.DMA((4,)))


def place():
    d = lax.axis_index("dp"); z = lax.axis_index("fsdp")
    core = d % 2; xx = (d // 2) % 2; yy = d // 4
    return d, z, d + 1 - 2 * core, d + 2 - 4 * xx, d + 4 - 8 * yy


def greet(partners):
    bar = pltpu.get_barrier_semaphore()
    for dev in partners:
        pl.semaphore_signal(bar, inc=1, device_id=dev, device_id_type=MESH)
    pl.semaphore_wait(bar, len(partners))


def split(n):
    return n // 32 * 16 if n >= 32 else n // 2


class Comm:
    def __init__(s):
        s.d, s.z, s.sib, s.xn, s.yn = place()
        s.dg = s.xn + s.yn - s.d
        s.nz = lax.axis_size("fsdp")
        s.partners = [(s.d, (s.z + j) % s.nz) for j in range(1, s.nz)] + [(s.sib, s.z), (s.xn, s.z), (s.yn, s.z)]


class Gather(Comm):
    def __init__(s, items, shards, zb, full, send, recv):
        super().__init__()
        s.items = items; s.sh = shards; s.zb = zb; s.full = full; s.send = send; s.recv = recv
    def cp(s, src, dst, i, slot, dev):
        return pltpu.make_async_remote_copy(src_ref=src, dst_ref=dst, send_sem=s.send.at[i, slot], recv_sem=s.recv.at[i, slot], device_id=dev, device_id_type=MESH)
    def block(s, i, d, half=None):
        w, r0, n = s.items[i]
        ref = s.full[w]
        a, m = (0, n) if half is None else ((0, split(n)) if half == 0 else (split(n), n - split(n)))
        if w == 4:
            return ref.at[d, pl.ds(r0 + a, m)]
        if w == 2:
            cols = ref.shape[1] // 8
            return ref.at[pl.ds(r0 + a, m), pl.ds(pl.multiple_of(d * cols, 128), cols)]
        rows = ref.shape[0] // 8
        return ref.at[pl.ds(pl.multiple_of(d * rows + (r0 + a), 16), m), :]
    def shard(s, i):
        w, r0, n = s.items[i]
        return s.sh[w] if w in (2, 4) else s.sh[w].at[pl.ds(r0, n), :]
    def zslot(s, i, z):
        w, r0, n = s.items[i]
        if w < 2:
            return s.zb[w].at[z, pl.ds(r0, n)]
        ref = s.full[w]
        if w == 2:
            r, c = ref.shape[0] // s.nz, ref.shape[1] // 8
            return ref.at[pl.ds(pl.multiple_of(z * r, 16), r), pl.ds(pl.multiple_of(s.d * c, 128), c)]
        r, c = ref.shape[0] // 8, ref.shape[1] // s.nz
        return ref.at[pl.ds(pl.multiple_of(s.d * r + r0, 16), n), pl.ds(pl.multiple_of(z * c, 128), c)]
    def zc(s, i, j, recv=False):
        other = (s.z - j + s.nz) % s.nz if recv else (s.z + j) % s.nz
        return s.cp(s.shard(i), s.zslot(i, other if recv else s.z), i, j - 1, (s.d, other))
    def start(s, i):
        if s.items[i][0] == 4:
            s.block(i, s.d)[...] = s.shard(i)[...]
            return
        for j in range(1, s.nz):
            s.zc(i, j).start()
        s.zslot(i, s.z)[...] = s.shard(i)[...]
    def sibc(s, i, k, d):
        return s.cp(s.block(i, d), s.block(i, d), i, 7 + k, (s.sib, s.z))
    def bx(s, i, b, dev, slot, half=None):
        return s.cp(s.block(i, b, half), s.block(i, b, half), i, slot, (dev, s.z))
    def e1(s, i):
        w = s.items[i][0]
        if w < 4:
            for j in range(1, s.nz):
                s.zc(i, j, True).wait_recv()
        if w < 2:
            s.block(i, s.d)[...] = jnp.concatenate([s.zslot(i, k)[...] for k in range(s.nz)], axis=1)
        s.bx(i, s.d, s.xn, 3).start()
        s.bx(i, s.d, s.yn, 4).start()
        s.sibc(i, 0, s.d).start()
    def e2(s, i):
        s.bx(i, s.xn, s.xn, 3).wait_recv()
        s.bx(i, s.xn, s.yn, 5, 0).start()
        s.sibc(i, 1, s.xn).start()
    def e3(s, i):
        s.bx(i, s.yn, s.yn, 4).wait_recv()
        s.bx(i, s.yn, s.xn, 6, 1).start()
        s.sibc(i, 2, s.yn).start()
    def e4(s, i):
        s.bx(i, s.dg, s.yn, 5, 0).wait_recv()
        s.bx(i, s.dg, s.xn, 6, 1).wait_recv()
        s.sibc(i, 3, s.dg).start()
    def e5(s, i):
        o = s.sib - s.d
        for k, b in enumerate((s.d, s.xn, s.yn, s.dg)):
            s.sibc(i, k, b + o).wait_recv()
    def finish(s, i):
        if s.items[i][0] < 4:
            for j in range(1, s.nz):
                s.zc(i, j).wait_send()
        s.bx(i, s.d, s.xn, 3).wait_send()
        s.bx(i, s.d, s.yn, 4).wait_send()
        s.bx(i, s.xn, s.yn, 5, 0).wait_send()
        s.bx(i, s.yn, s.xn, 6, 1).wait_send()
        for k, b in enumerate((s.d, s.xn, s.yn, s.dg)):
            s.sibc(i, k, b).wait_send()


class Scatter(Comm):
    def __init__(s, grads, own, sb, ra, rb, rx, ry, zs, zr, out, cs, csem, osem, send, recv):
        super().__init__()
        s.g = grads; s.own = own; s.sb = sb; s.ra = ra; s.rb = rb; s.rx = rx; s.ry = ry; s.zs = zs; s.zr = zr
        s.out = out; s.cs = cs; s.csem = csem; s.osem = osem; s.send = send; s.recv = recv
        s.chips = (s.dg, s.xn, s.yn, s.d)
    def cp(s, src, dst, w, slot, dev):
        return pltpu.make_async_remote_copy(src_ref=src, dst_ref=dst, send_sem=s.send.at[w, slot], recv_sem=s.recv.at[w, slot], device_id=dev, device_id_type=MESH)
    def block(s, w, d):
        ref = s.g[w]
        if w == 4:
            return ref.at[d]
        if w == 2:
            cols = ref.shape[1] // 8
            return ref.at[:, pl.ds(pl.multiple_of(d * cols, 128), cols)]
        rows = ref.shape[0] // 8
        return ref.at[pl.ds(pl.multiple_of(d * rows, 16), rows), :]
    def half(s, ref, h):
        n = ref.shape[0]; k = split(n)
        return ref.at[pl.ds(0, k)] if h == 0 else ref.at[pl.ds(k, n - k)]
    def sibc(s, w, i):
        return s.cp(s.block(w, s.chips[i] + s.sib - s.d), s.sb[w].at[i], w, i, (s.sib, s.z))
    def load(s, w, i):
        return pltpu.make_async_copy(s.block(w, s.chips[i]), s.own[w].at[i], s.osem.at[w, i])
    def cc(s):
        return pltpu.make_async_remote_copy(src_ref=s.cs.at[0], dst_ref=s.cs.at[1], send_sem=s.csem.at[0], recv_sem=s.csem.at[1], device_id=(s.sib, s.z), device_id_type=MESH)
    def s0(s, w):
        for i in range(4):
            s.sibc(w, i).start()
            s.load(w, i).start()
    def ca(s, w): return s.cp(s.half(s.sb[w].at[0], 0), s.ra[w], w, 4, (s.xn, s.z))
    def cb(s, w): return s.cp(s.half(s.sb[w].at[0], 1), s.rb[w], w, 5, (s.yn, s.z))
    def cx(s, w, h): return s.cp(s.half(s.sb[w].at[1], h), s.half(s.rx[w], h), w, 6 + h, (s.xn, s.z))
    def cy(s, w, h): return s.cp(s.half(s.sb[w].at[2], h), s.half(s.ry[w], h), w, 8 + h, (s.yn, s.z))
    def mixed(s, w, i):
        s.sibc(w, i).wait_recv(); s.load(w, i).wait()
        return s.cs[0, 0:1, 0:1] * s.own[w][i].astype(f32) + s.cs[1, 0:1, 0:1] * s.sb[w][i].astype(f32)
    def a(s, w):
        t = s.sb[w]
        t[0] = s.mixed(w, 0).astype(t.dtype); s.ca(w).start(); s.cb(w).start()
        t[1] = s.mixed(w, 1).astype(t.dtype); s.cx(w, 0).start()
        t[2] = s.mixed(w, 2).astype(t.dtype); s.cy(w, 1).start()
    def r(s, w):
        s.ca(w).wait_recv()
        t = s.half(s.sb[w].at[2], 0)
        t[...] = (t[...].astype(f32) + s.ra[w][...].astype(f32)).astype(t.dtype)
        s.cy(w, 0).start()
        s.cb(w).wait_recv()
        t = s.half(s.sb[w].at[1], 1)
        t[...] = (t[...].astype(f32) + s.rb[w][...].astype(f32)).astype(t.dtype)
        s.cx(w, 1).start()
    def zpiece(s, w, k):
        ref = s.zs[w]
        if w in (0, 1): return ref.at[k]
        if w == 4: return ref
        if w == 2:
            r = ref.shape[0] // s.nz
            return ref.at[pl.ds(pl.multiple_of(k * r, 16), r)]
        c = ref.shape[1] // s.nz
        return ref.at[:, pl.ds(pl.multiple_of(k * c, 128), c)]
    def zc(s, w, j):
        to = (s.z + j) % s.nz
        return s.cp(s.zpiece(w, to), s.zr[w].at[j - 1], w, 9 + j, (s.d, to))
    def f(s, w):
        t = s.mixed(w, 3)
        for h in (0, 1):
            s.cx(w, h).wait_recv(); s.cy(w, h).wait_recv()
        t = t + s.rx[w][...].astype(f32) + s.ry[w][...].astype(f32)
        if w in (0, 1):
            c = t.shape[1] // s.nz
            for k in range(s.nz): s.zs[w][k] = t[:, k * c:(k + 1) * c].astype(bf16)
        else:
            s.zs[w][...] = t.astype(s.zs[w].dtype)
        for j in range(1, s.nz): s.zc(w, j).start()
    def zf(s, w):
        for j in range(1, s.nz): s.zc(w, j).wait_recv()
        t = s.zpiece(w, s.z)[...].astype(f32)
        for j in range(s.nz - 1): t = t + s.zr[w][j].astype(f32)
        s.out[w][...] = t
    def finish(s, w):
        for i in range(4): s.sibc(w, i).wait_send()
        s.ca(w).wait_send(); s.cb(w).wait_send()
        for h in (0, 1): s.cx(w, h).wait_send(); s.cy(w, h).wait_send()
        for j in range(1, s.nz): s.zc(w, j).wait_send()


def rs_kernel(c, *refs):
    refs = list(refs)
    take = lambda n: [refs.pop(0) for _ in range(n)]
    grads = take(5); outs = take(5)
    parts = [take(5) for _ in range(8)]
    s = Scatter(grads, *parts, outs, *refs)
    greet(s.partners)
    q, o, f, p, v = range(5)
    for w in (o, v, q, f, p): s.s0(w)
    s.cs[0] = jnp.full(s.cs.shape[1:], c[0], f32)
    s.cc().start(); s.cc().wait_recv()
    s.a(o); s.a(v); s.a(q); s.r(o); s.r(v); s.a(f); s.r(q); s.f(o); s.f(v); s.a(p); s.r(f); s.f(q); s.r(p); s.f(f)
    s.zf(o); s.zf(v); s.zf(q); s.f(p); s.zf(f); s.zf(p)
    s.cc().wait_send()
    for w in range(5): s.finish(w)


def scatter_all(c, gq, go, gf, gp, gv):
    nz = lax.axis_size("fsdp")
    grads = (gq, go, gf, gp, gv)
    blocks = [(gq.shape[0] // 8, gq.shape[1]), (go.shape[0] // 8, go.shape[1]), (gf.shape[0], gf.shape[1] // 8), (gp.shape[0] // 8, gp.shape[1]), gv.shape[1:]]
    dt = [bf16] * 4 + [f32]
    ha = [(split(r), c_) for r, c_ in blocks]
    hb = [(r - split(r), c_) for r, c_ in blocks]
    piece = [(r, c_ // nz) for r, c_ in blocks[:2]] + [(blocks[2][0] // nz, blocks[2][1]), (blocks[3][0], blocks[3][1] // nz), blocks[4]]
    zs = [(nz,) + piece[0], (nz,) + piece[1]] + blocks[2:]
    zr = [(nz - 1,) + s for s in piece]
    V = lambda ss: [pltpu.VMEM(s, t) for s, t in zip(ss, dt)]
    four = [(4,) + b for b in blocks]
    vm = pl.BlockSpec(memory_space=pltpu.VMEM)
    an = pl.BlockSpec(memory_space=pl.ANY)
    dma = pltpu.SemaphoreType.DMA
    return pl.pallas_call(rs_kernel, out_shape=[jax.ShapeDtypeStruct(s, f32) for s in piece],
        in_specs=[pl.BlockSpec(memory_space=pltpu.SMEM)] + [an] * 5, out_specs=[vm] * 5,
        scratch_shapes=V(four) + V(four) + V(ha) + V(hb) + V(blocks) + V(blocks) + V(zs) + V(zr)
            + [pltpu.VMEM((2, 8, 128), f32), dma((2,)), dma((5, 4)), dma((5, 13)), dma((5, 13))],
        compiler_params=pltpu.CompilerParams(collective_id=1, has_side_effects=True, vmem_limit_bytes=60 << 20))(c, *grads)


def block_kernel(names, remote, length, tok, cot, *refs):
    refs = list(refs)
    take = lambda n: [refs.pop(0) for _ in range(n)]
    if remote:
        raw = take(5)
        y, gx, gq, go, gf, gp, gv, ss = take(8)
        QT, OT, F, PT, V, sq, so, sf, sp, zq, zo, send, recv = take(13)
    else:
        QT, OT, F, PT, vec, bf = take(6)
        y, gx, gq, go, gf, gp, col, dbf, ss = take(9)
        V = None
    s = Block(length=length[0], QT=QT, OT=OT, F=F, PT=PT, V=V, **dict(zip(names, refs)))
    D = s.x.shape[1]; FF = s.u.shape[1]
    cx = pltpu.make_async_copy(tok, s.x, s.isem.at[0]); cx.start()
    ce = pltpu.make_async_copy(cot, s.ey, s.isem.at[1]); ce.start()
    if remote:
        rows = sq.shape[0]
        items = [(4, 0, 16), (0, 0, rows // 2), (0, rows // 2, rows - rows // 2), (1, 0, so.shape[0]), (2, 0, F.shape[0]), (3, 0, sp.shape[0])]
        g = Gather(items, (sq, so, sf, sp, raw[4]), (zq, zo), (QT, OT, F, PT, V), send, recv)
        sq[...] = raw[0][...].astype(bf16).T
        so[...] = raw[1][...].astype(bf16).T
        sf[...] = raw[2][...].astype(bf16)
        sp[...] = raw[3][...].astype(bf16).T
        greet(g.partners)
        v, q1, q2, o, f, p = range(6)
        for i in range(6): g.start(i)
        g.e1(v); g.e2(v); g.e3(v); g.e4(v)
        g.e1(q1); g.e5(v); s.unpack(); cx.wait(); s.ln1()
        g.e1(q2); g.e2(q1); g.e3(q1); g.e1(o); g.e2(q2); g.e3(q2); g.e4(q1); g.e1(f); g.e2(o); g.e3(o); g.e4(q2)
        g.e5(q1); g.e5(q2)
        s.qkv()
        def pair(hp):
            @pl.when(hp == 0)
            def _(): g.e4(o); g.e1(p)
            @pl.when(hp == 3)
            def _(): g.e2(f); g.e3(f)
            s.attend(hp)
        loop(D // 128, pair)
        g.e4(f); g.e5(o)
        s.out(); s.ln2(); g.e2(p); g.e3(p); g.e5(f); s.fc()
    else:
        s.vec[...] = vec[...]; s.bf[...] = bf[...]
        s.clear(); cx.wait()
        s.ln1(); s.qkv()
        loop(D // 128, s.attend)
        s.out(); s.ln2(); s.fc()
    ce.wait(); s.ey_mask()
    if remote: g.e4(p)
    s.wgrad(s.ey, s.u, gp, 512, FF)
    if remote: g.e5(p)
    s.y()
    cy = pltpu.make_async_copy(s.er, y, s.isem.at[2]); cy.start()
    s.ef(); s.wgrad(s.n2, s.gp, gf, 512, FF); s.gn2()
    cy.wait()
    s.ln2b(); s.wgrad(s.er, s.A, go, 256, D); s.eA()
    loop(D // 128, s.attend_back)
    s.bias_cols(); s.gn1(); s.ln1b()
    cg = pltpu.make_async_copy(s.er, gx, s.isem.at[3]); cg.start()
    s.wgrad(s.u, s.n1, gq, 256, D)
    cg.wait()
    ss[0] = s.norm()
    if remote:
        w = D // 8; nb = FF // 8 // 128
        for d in range(8):
            gv[d, 0:8, 0:w] = s.col[:, d * w:(d + 1) * w]
            gv[d, 0:8, w:128] = jnp.zeros((8, 128 - w), f32)
            for j in range(8):
                k = d * nb + j
                gv[d, 8 + j:9 + j, :] = s.dbf[:, k * 128:(k + 1) * 128] if j < nb else jnp.zeros((1, 128), f32)
        for i in range(6): g.finish(i)
    else:
        col[...] = s.col[...]; dbf[...] = s.dbf[...]


def run_block(remote, length, tok, cot, *ws):
    L, D = tok.shape
    sd = jax.ShapeDtypeStruct
    dma = pltpu.SemaphoreType.DMA
    vm = pl.BlockSpec(memory_space=pltpu.VMEM); an = pl.BlockSpec(memory_space=pl.ANY); sm = pl.BlockSpec(memory_space=pltpu.SMEM)
    extra = []
    if remote:
        nz = lax.axis_size("fsdp")
        q, o, f, p, v = ws
        FF = f.shape[1] * 8
        qt, ot, pt = q.shape[::-1], o.shape[::-1], p.shape[::-1]
        extra = [pltpu.VMEM((3 * D, D), bf16), pltpu.VMEM((D, D), bf16), pltpu.VMEM((D, FF), bf16), pltpu.VMEM((D, FF), bf16), pltpu.VMEM((8,) + v.shape, f32),
            pltpu.VMEM(qt, bf16), pltpu.VMEM(ot, bf16), pltpu.VMEM(f.shape, bf16), pltpu.VMEM(pt, bf16),
            pltpu.VMEM((nz,) + qt, bf16), pltpu.VMEM((nz,) + ot, bf16), dma((6, 11)), dma((6, 11))]
        tail = [sd((8,) + v.shape, f32)]
    else:
        FF = ws[2].shape[1]
        tail = [sd((8, D), f32), sd((1, FF), f32)]
    scr = scratch(L, D, FF)
    params = dict(collective_id=0, has_side_effects=True) if remote else {}
    return pl.pallas_call(functools.partial(block_kernel, list(scr), remote),
        out_shape=[sd((L, D), bf16), sd((L, D), bf16), sd((3 * D, D), bf16), sd((D, D), bf16), sd((D, FF), bf16), sd((D, FF), bf16)] + tail + [sd((1,), f32)],
        in_specs=[sm, an, an] + [vm] * len(ws), out_specs=[an] * 6 + [vm] * len(tail) + [sm], scratch_shapes=extra + list(scr.values()),
        compiler_params=pltpu.CompilerParams(vmem_limit_bytes=VLIM, **params))(length, tok, cot, *ws)


VLIM = 63 << 20


def shards(tokens, qkv_weight, out_weight, fc_weight, proj_weight, fc_bias, vectors, cotangent, lengths, clip_norm,
           noise_qkv, noise_out, noise_fc, noise_proj, noise_fc_bias, noise_vectors):
    ndp, nz = lax.axis_size("dp"), lax.axis_size("fsdp")
    if ndp == 8:
        nb = fc_bias.shape[0] // 128
        small = jnp.concatenate([jnp.pad(vectors, ((0, 0), (0, 128 - vectors.shape[1]))), jnp.pad(fc_bias.reshape(nb, 128), ((0, 8 - nb), (0, 0)))], axis=0)
        y, gx, gq, go, gf, gp, gv, ss = run_block(True, lengths, tokens, cotangent, qkv_weight, out_weight, fc_weight, proj_weight, small)
    else:
        g = lambda a: lax.all_gather(lax.all_gather(a.astype(bf16), "dp", axis=1, tiled=True), "fsdp", axis=0, tiled=True)
        vec = lax.all_gather(vectors.astype(bf16), "dp", axis=1, tiled=True).astype(f32)
        bf = lax.all_gather(fc_bias.astype(bf16), "dp", axis=0, tiled=True).astype(f32).reshape(1, -1)
        y, gx, gq, go, gf, gp, col, dbf, ss = run_block(False, lengths, tokens, cotangent, g(qkv_weight).T, g(out_weight).T, g(fc_weight), g(proj_weight).T, vec, bf)
    norm = jnp.sqrt(ss)
    factor = jnp.minimum(1.0, clip_norm / norm)
    if ndp == 8:
        sq, so, sf, sp, sv = scatter_all(factor, gq, go, gf, gp, gv)
        finals = (sq.T, so.T, sf, sp.T, sv[8:8 + nb].reshape(-1), sv[:8, :vectors.shape[1]])
    else:
        ps = lambda a, dim: lax.psum_scatter(factor * a.astype(f32), "dp", scatter_dimension=dim, tiled=True)
        pz = lambda a: lax.psum_scatter(a.astype(bf16), "fsdp", scatter_dimension=0, tiled=True).astype(f32)
        finals = tuple(pz(ps(a, 1)) for a in (gq.T, go.T, gf, gp.T)) + lax.psum((ps(dbf[0], 0), ps(col, 1)), "fsdp")
    examples = ndp * nz
    noises = (noise_qkv, noise_out, noise_fc, noise_proj, noise_fc_bias, noise_vectors)
    return (y, gx, norm / clip_norm) + tuple(a / examples + n for a, n in zip(finals, noises))


def solution(mesh):
    both, cut = P(("dp", "fsdp"), None), P("fsdp", "dp")
    weights = (cut, cut, cut, cut, P("dp"), P(None, "dp"))
    return jax.shard_map(shards, mesh=mesh, in_specs=(both,) + weights + (both, P(("dp", "fsdp")), P()) + weights,
        out_specs=(both, both, P(("dp", "fsdp"))) + weights, check_vma=False)
```

```python
import functools
import types
import jax
import jax.numpy as jnp
from jax import lax
from jax.experimental import pallas as pl
from jax.experimental.pallas import tpu as pltpu
from jax.sharding import PartitionSpec as P

MESH = pl.DeviceIdType.MESH
f32 = jnp.float32
bf16 = jnp.bfloat16
HD=64; T=256; QB=256
EPS=1e-05
GC=0.7978845608028654
GA=0.044715

def nn(a, b): return lax.dot_general(a, b, (((1,), (0,)), ((), ())), preferred_element_type=f32)
def nt(a, b): return lax.dot_general(a, b, (((1,), (1,)), ((), ())), preferred_element_type=f32)
def at(i, n): return pl.ds(pl.multiple_of(i * n, n), n)
def loop(n, body): lax.fori_loop(0, n, lambda i, c: (body(i), c)[1], 0)

class Block:
    def __init__(s, **refs): s.__dict__.update(refs)
    def unpack(s):
        V = s.V
        n = V.shape[0]; w = s.x.shape[1] // n; k = s.bf.shape[1] // n // 128
        s.vec[...] = jnp.concatenate([V[d][0:8, 0:w] for d in range(n)], axis=1).astype(bf16).astype(f32)
        s.bf[...] = jnp.concatenate([V[d][8 + j:9 + j, :] for d in range(n) for j in range(k)], axis=1).astype(bf16).astype(f32)
        s.clear()
    def clear(s):
        s.col[...] = jnp.zeros_like(s.col); s.ssq[...] = jnp.zeros_like(s.ssq)
        L = s.x.shape[0]
        kp = lax.broadcasted_iota(jnp.int32, (L, 128), 0)
        s.kb[...] = jnp.where(kp < s.length, 0.0, -1e30).astype(bf16)
    def row(s, i): return s.vec[i:i + 1, :]
    def ln1(s):
        def body(i):
            x = s.x[at(i, T), :].astype(f32)
            c = x - jnp.mean(x, axis=1, keepdims=True)
            v = jnp.mean(c * c, axis=1, keepdims=True)
            s.n1[at(i, T), :] = (c * lax.rsqrt(v + EPS) * s.row(0) + s.row(1)).astype(bf16)
        loop(s.x.shape[0] // T, body)
    def qkv(s):
        D = s.x.shape[1]
        for part, b in ((0, 2), (1, None), (2, 3)):
            def body(i):
                o = nt(s.n1[...], s.QT[pl.ds(pl.multiple_of(part * D + i * T, T), T), :])
                if b is not None: o = o + s.vec[b:b + 1, at(i, T)]
                s.m[:, pl.ds(pl.multiple_of(part * D + i * T, T), T)] = o.astype(bf16)
            loop(D // T, body)
    def heads(s, hp):
        D = s.x.shape[1]
        q = s.m[:, at(hp, 128)] * bf16(HD ** -0.5)
        k = s.m[:, pl.ds(pl.multiple_of(D + hp * 128, 128), 128)]
        v = s.m[:, pl.ds(pl.multiple_of(2 * D + hp * 128, 128), 128)]
        return q, k, v
    def masked(s, q, k, h):
        lane = lax.broadcasted_iota(jnp.int32, q.shape, 1)
        mine = (lane // HD) == h
        free = lane == (1 - h) * HD
        zero = jnp.zeros_like(q)
        return jnp.where(mine, q, jnp.where(free, jnp.ones_like(q), zero)), jnp.where(mine, k, jnp.where(free, s.kb[...], zero))
    def scores(s, kh, qh, b):
        qq = qh[b * QB:(b + 1) * QB]
        parts = []
        if b: parts.append(nt(kh[:b * QB], qq))
        o = nt(kh[b * QB:(b + 1) * QB], qq)
        r = lax.broadcasted_iota(jnp.int32, o.shape, 0); c = lax.broadcasted_iota(jnp.int32, o.shape, 1)
        parts.append(jnp.where(r <= c, o, -1e30))
        return parts
    def attend(s, hp):
        L = s.x.shape[0]
        q, k, v = s.heads(hp)
        vt = v.T
        outs = []
        for h in (0, 1):
            qh, kh = s.masked(q, k, h)
            for b in range(L // QB):
                parts = s.scores(kh, qh, b)
                mx = jnp.max(parts[-1], axis=0, keepdims=True)
                if b: mx = jnp.maximum(mx, jnp.max(parts[0], axis=0, keepdims=True))
                es = [jnp.exp(p - mx) for p in parts]
                l = sum(jnp.sum(e, axis=0, keepdims=True) for e in es)
                o = nn(vt[h * HD:(h + 1) * HD, b * QB:(b + 1) * QB], es[-1].astype(bf16))
                if b: o = o + nn(vt[h * HD:(h + 1) * HD, :b * QB], es[0].astype(bf16))
                s.lse[hp, h:h + 1, b * QB:(b + 1) * QB] = mx + jnp.log(l)
                s.ot[h * HD:(h + 1) * HD, b * QB:(b + 1) * QB] = o / l
        s.A[:, at(hp, 128)] = s.ot[...].T.astype(bf16)
    def out(s):
        def body(i):
            o = nt(s.A[...], s.OT[at(i, T), :])
            s.r[:, at(i, T)] = s.x[:, at(i, T)].astype(f32) + o + s.vec[4:5, at(i, T)]
        loop(s.x.shape[1] // T, body)
    def ln2(s):
        def body(i):
            x = s.r[at(i, T), :]
            c = x - jnp.mean(x, axis=1, keepdims=True)
            v = jnp.mean(c * c, axis=1, keepdims=True)
            s.n2[at(i, T), :] = (c * lax.rsqrt(v + EPS) * s.row(5) + s.row(6)).astype(bf16)
        loop(s.x.shape[0] // T, body)
    def fc(s):
        def body(i):
            f = nn(s.n2[...], s.F[:, at(i, T)]) + s.bf[:, at(i, T)]
            f2 = f * f
            t = jnp.tanh(f * (GC + GC * GA * f2))
            p = 0.5 * t + 0.5
            u = f * p
            s.u[:, at(i, T)] = u.astype(bf16)
            s.gp[:, at(i, T)] = (p + u * (1.0 - p) * (2 * GC + 6 * GC * GA * f2)).astype(bf16)
        loop(s.u.shape[1] // T, body)
    def ey_mask(s):
        def body(i):
            rp = i * T + lax.broadcasted_iota(jnp.int32, (T, s.x.shape[1]), 0)
            e = jnp.where(rp < s.length, s.ey[at(i, T), :].astype(f32), 0.0)
            s.ey[at(i, T), :] = e.astype(bf16)
            s.col[7:8, :] += jnp.sum(e, axis=0, keepdims=True)
        loop(s.x.shape[0] // T, body)
    def wgrad(s, lhs, rhs, out, nw, cols, first=0):
        W = min(cols, s.stage.shape[2]); nh = cols // W; n = out.shape[0] // T
        def cp(i, h):
            slot = (i * nh + h) % 2
            return pltpu.make_async_copy(s.stage.at[slot, :, pl.ds(0, W)], out.at[at(i, T), pl.ds(h * W, W)], s.dsem.at[slot])
        def body(i):
            s.lt[...] = lhs[:, at(i, T)].T
            for h in range(nh):
                @pl.when(i * nh + h >= 2)
                def _(): cp(i - 2 // nh, h).wait()
                def inner(j):
                    o = nn(s.lt[...], rhs[:, pl.ds(pl.multiple_of(h * W + j * nw, nw), nw)])
                    s.ssq[:, 0:nw] += jnp.sum(o * o, axis=0, keepdims=True)
                    s.stage[(i * nh + h) % 2, :, at(j, nw)] = o.astype(bf16)
                loop(W // nw, inner)
                cp(i, h).start()
        loop(n, body)
        for t in (n * nh - 2, n * nh - 1): cp(t // nh, t % nh).wait()
    def y(s):
        def body(i):
            o = nt(s.u[...], s.PT[at(i, T), :])
            s.er[:, at(i, T)] = (s.r[:, at(i, T)] + o + s.vec[7:8, at(i, T)]).astype(bf16)
        loop(s.x.shape[1] // T, body)
    def ef(s):
        def body(i):
            g = nn(s.ey[...], s.PT[:, at(i, T)]) * s.gp[:, at(i, T)].astype(f32)
            e = g.astype(bf16)
            s.gp[:, at(i, T)] = e
            s.dbf[:, at(i, T)] = jnp.sum(e.astype(f32), axis=0, keepdims=True)
        loop(s.u.shape[1] // T, body)
    def gn2(s):
        def body(i):
            s.G[:, at(i, T)] = nt(s.gp[...], s.F[at(i, T), :])
        loop(s.x.shape[1] // T, body)
    def lnb(s, x, gn, gain):
        c = x - jnp.mean(x, axis=1, keepdims=True)
        v = jnp.mean(c * c, axis=1, keepdims=True)
        rs = lax.rsqrt(v + EPS)
        h = c * rs
        a = gn * gain
        return h, rs * (a - jnp.mean(a, axis=1, keepdims=True) - h * jnp.mean(a * h, axis=1, keepdims=True))
    def ln2b(s):
        def body(i):
            gn = s.G[at(i, T), :]
            h, g = s.lnb(s.r[at(i, T), :], gn, s.row(5))
            s.col[5:6, :] += jnp.sum(gn * h, axis=0, keepdims=True)
            s.col[6:7, :] += jnp.sum(gn, axis=0, keepdims=True)
            g = g + s.ey[at(i, T), :].astype(f32)
            s.r[at(i, T), :] = g
            e = g.astype(bf16)
            s.er[at(i, T), :] = e
            s.col[4:5, :] += jnp.sum(e.astype(f32), axis=0, keepdims=True)
        loop(s.x.shape[0] // T, body)
    def eA(s):
        def body(i):
            s.n2[:, at(i, T)] = nn(s.er[...], s.OT[:, at(i, T)]).astype(bf16)
        loop(s.x.shape[1] // T, body)
    def attend_back(s, hp):
        L, D = s.x.shape
        q, k, v = s.heads(hp)
        e = s.n2[:, at(hp, 128)]
        kt = k.T
        ea = (e.astype(f32) * s.A[:, at(hp, 128)].astype(f32)).T
        lane = lax.broadcasted_iota(jnp.int32, e.shape, 1)
        s.dk[...] = jnp.zeros_like(s.dk); s.dv[...] = jnp.zeros_like(s.dv)
        for h in (0, 1):
            qh, kh = s.masked(q, k, h)
            mine = (lane // HD) == h
            eh = jnp.where(mine, e, jnp.zeros_like(e))
            qz = jnp.where(mine, q, jnp.zeros_like(q))
            delta = jnp.sum(ea[h * HD:(h + 1) * HD, :], axis=0, keepdims=True)
            for b in range(L // QB):
                cols = slice(b * QB, (b + 1) * QB)
                n = (b + 1) * QB
                parts = s.scores(kh, qh, b)
                lse = s.lse[hp, h:h + 1, cols]
                P = [jnp.exp(p - lse) for p in parts]
                dP = nt(v[:n], eh[cols])
                dl = delta[:, cols]
                dS = [(P[-1] * (dP[n - QB:] - dl)).astype(bf16)]
                if b: dS = [(P[0] * (dP[:n - QB] - dl)).astype(bf16)] + dS
                for i, (p, ds) in enumerate(zip(P, dS)):
                    rows = slice(n - QB, n) if i == len(P) - 1 else slice(0, n - QB)
                    s.dv[rows, :] += nn(p.astype(bf16), eh[cols])
                    s.dk[rows, :] += nn(ds, qz[cols])
                o = nn(kt[h * HD:(h + 1) * HD, n - QB:n], dS[-1])
                if b: o = o + nn(kt[h * HD:(h + 1) * HD, :n - QB], dS[0])
                s.ot[h * HD:(h + 1) * HD, cols] = o * (HD ** -0.5)
        s.u[:, at(hp, 128)] = s.ot[...].T.astype(bf16)
        s.u[:, pl.ds(pl.multiple_of(D + hp * 128, 128), 128)] = s.dk[...].astype(bf16)
        s.u[:, pl.ds(pl.multiple_of(2 * D + hp * 128, 128), 128)] = s.dv[...].astype(bf16)
    def bias_cols(s):
        D = s.x.shape[1]
        def body(i):
            s.col[2:3, :] += jnp.sum(s.u[at(i, T), 0:D].astype(f32), axis=0, keepdims=True)
            s.col[3:4, :] += jnp.sum(s.u[at(i, T), 2 * D:3 * D].astype(f32), axis=0, keepdims=True)
        loop(s.x.shape[0] // T, body)
    def gn1(s):
        D = s.x.shape[1]
        def body(i):
            s.G[:, at(i, T)] = nn(s.u[:, 0:3 * D], s.QT[:, at(i, T)])
        loop(D // T, body)
    def ln1b(s):
        def body(i):
            gn = s.G[at(i, T), :]
            h, g = s.lnb(s.x[at(i, T), :].astype(f32), gn, s.row(0))
            s.col[0:1, :] += jnp.sum(gn * h, axis=0, keepdims=True)
            s.col[1:2, :] += jnp.sum(gn, axis=0, keepdims=True)
            s.er[at(i, T), :] = (s.r[at(i, T), :] + g).astype(bf16)
        loop(s.x.shape[0] // T, body)
    def norm(s):
        t = jnp.sum(s.ssq[...]) + jnp.sum(s.dbf[...] * s.dbf[...]) + jnp.sum(s.col[...] * s.col[...])
        return t

def scratch(L, D, FF, rows=None):
    return dict(
        vec=pltpu.VMEM((8, D), f32), bf=pltpu.VMEM((1, FF), f32), col=pltpu.VMEM((8, D), f32), dbf=pltpu.VMEM((1, FF), f32),
        ssq=pltpu.VMEM((1, 512), f32), kb=pltpu.VMEM((L, 128), bf16),
        n1=pltpu.VMEM((L, D), bf16), m=pltpu.VMEM((L, 3 * D), bf16), A=pltpu.VMEM((L, D), bf16), r=pltpu.VMEM((L, D), f32),
        n2=pltpu.VMEM((L, D), bf16), u=pltpu.VMEM((L, FF), bf16), gp=pltpu.VMEM((L, FF), bf16), er=pltpu.VMEM((L, D), bf16),
        G=pltpu.VMEM((L, D), f32), stage=pltpu.VMEM((2, T, FF // 2), bf16), lt=pltpu.VMEM((T, L), bf16),
        lse=pltpu.VMEM((D // 128, 2, L), f32), ot=pltpu.VMEM((128, L), f32), dk=pltpu.VMEM((L, 128), f32), dv=pltpu.VMEM((L, 128), f32),
        x=pltpu.VMEM((L, D), bf16), ey=pltpu.VMEM((L, D), bf16),
        dsem=pltpu.SemaphoreType.DMA((2,)), isem=pltpu.SemaphoreType.DMA((4,)))


def place():
    d = lax.axis_index("dp"); z = lax.axis_index("fsdp")
    core = d % 2; xx = (d // 2) % 2; yy = d // 4
    return d, z, d + 1 - 2 * core, d + 2 - 4 * xx, d + 4 - 8 * yy


def greet(partners):
    bar = pltpu.get_barrier_semaphore()
    for dev in partners:
        pl.semaphore_signal(bar, inc=1, device_id=dev, device_id_type=MESH)
    pl.semaphore_wait(bar, len(partners))


def split(n):
    return n // 32 * 16 if n >= 32 else n // 2


class Comm:
    def __init__(s):
        s.d, s.z, s.sib, s.xn, s.yn = place()
        s.dg = s.xn + s.yn - s.d
        s.nz = lax.axis_size("fsdp")
        s.partners = [(s.d, (s.z + j) % s.nz) for j in range(1, s.nz)] + [((s.d + k) % 8, s.z) for k in range(1, 8)]


class Gather(Comm):
    def __init__(s, items, shards, zb, full, send, recv):
        super().__init__()
        s.items = items; s.sh = shards; s.zb = zb; s.full = full; s.send = send; s.recv = recv
    def cp(s, src, dst, i, slot, dev):
        return pltpu.make_async_remote_copy(src_ref=src, dst_ref=dst, send_sem=s.send.at[i, slot], recv_sem=s.recv.at[i, slot], device_id=dev, device_id_type=MESH)
    def block(s, i, d, half=None):
        w, r0, n = s.items[i]
        ref = s.full[w]
        a, m = (0, n) if half is None else ((0, split(n)) if half == 0 else (split(n), n - split(n)))
        if w == 4:
            return ref.at[d, pl.ds(r0 + a, m)]
        if w == 2:
            cols = ref.shape[1] // 8
            return ref.at[pl.ds(r0 + a, m), pl.ds(pl.multiple_of(d * cols, 128), cols)]
        rows = ref.shape[0] // 8
        return ref.at[pl.ds(pl.multiple_of(d * rows + (r0 + a), 16), m), :]
    def shard(s, i):
        w, r0, n = s.items[i]
        return s.sh[w] if w in (2, 4) else s.sh[w].at[pl.ds(r0, n), :]
    def zslot(s, i, z):
        w, r0, n = s.items[i]
        if w < 2:
            return s.zb[w].at[z, pl.ds(r0, n)]
        ref = s.full[w]
        if w == 2:
            r, c = ref.shape[0] // s.nz, ref.shape[1] // 8
            return ref.at[pl.ds(pl.multiple_of(z * r, 16), r), pl.ds(pl.multiple_of(s.d * c, 128), c)]
        r, c = ref.shape[0] // 8, ref.shape[1] // s.nz
        return ref.at[pl.ds(pl.multiple_of(s.d * r + r0, 16), n), pl.ds(pl.multiple_of(z * c, 128), c)]
    def zc(s, i, j, recv=False):
        other = (s.z - j + s.nz) % s.nz if recv else (s.z + j) % s.nz
        return s.cp(s.shard(i), s.zslot(i, other if recv else s.z), i, j - 1, (s.d, other))
    def start(s, i):
        if s.items[i][0] == 4:
            s.block(i, s.d)[...] = s.shard(i)[...]
            return
        for j in range(1, s.nz):
            s.zc(i, j).start()
        s.zslot(i, s.z)[...] = s.shard(i)[...]
    def sibc(s, i, k, d):
        return s.cp(s.block(i, d), s.block(i, d), i, 7 + k, (s.sib, s.z))
    def bx(s, i, b, dev, slot, half=None):
        return s.cp(s.block(i, b, half), s.block(i, b, half), i, slot, (dev, s.z))
    def e1(s, i):
        w = s.items[i][0]
        if w < 4:
            for j in range(1, s.nz):
                s.zc(i, j, True).wait_recv()
        if w < 2:
            s.block(i, s.d)[...] = jnp.concatenate([s.zslot(i, k)[...] for k in range(s.nz)], axis=1)
        s.bx(i, s.d, s.xn, 3).start()
        s.bx(i, s.d, s.yn, 4).start()
        s.sibc(i, 0, s.d).start()
    def e2(s, i):
        s.bx(i, s.xn, s.xn, 3).wait_recv()
        s.bx(i, s.xn, s.yn, 5, 0).start()
        s.sibc(i, 1, s.xn).start()
    def e3(s, i):
        s.bx(i, s.yn, s.yn, 4).wait_recv()
        s.bx(i, s.yn, s.xn, 6, 1).start()
        s.sibc(i, 2, s.yn).start()
    def e4(s, i):
        s.bx(i, s.dg, s.yn, 5, 0).wait_recv()
        s.bx(i, s.dg, s.xn, 6, 1).wait_recv()
        s.sibc(i, 3, s.dg).start()
    def e5(s, i):
        o = s.sib - s.d
        for k, b in enumerate((s.d, s.xn, s.yn, s.dg)):
            s.sibc(i, k, b + o).wait_recv()
    def finish(s, i):
        if s.items[i][0] < 4:
            for j in range(1, s.nz):
                s.zc(i, j).wait_send()
        s.bx(i, s.d, s.xn, 3).wait_send()
        s.bx(i, s.d, s.yn, 4).wait_send()
        s.bx(i, s.xn, s.yn, 5, 0).wait_send()
        s.bx(i, s.yn, s.xn, 6, 1).wait_send()
        for k, b in enumerate((s.d, s.xn, s.yn, s.dg)):
            s.sibc(i, k, b).wait_send()


class Reduce(Comm):
    def __init__(s, hbm, far, near, v, sems):
        super().__init__()
        s.hbm = hbm; s.v = v; s.near = near
        s.pP, s.pF = far
        s.sems = sems
        s.chips = (s.dg, s.xn, s.yn, s.d)
        s.ndp = 8
        s.fr = hbm[2].shape[0] // s.nz; s.fh = s.fr // 2; s.fc = hbm[2].shape[1] // 8
        s.qr = hbm[0].shape[0] // 8; s.orr = hbm[1].shape[0] // 8; s.pr = hbm[3].shape[0] // 8; s.pc = hbm[3].shape[1] // s.nz
        s.peers = [((s.d + k) % 8, s.z) for k in range(1, 8)] + [(s.d, (s.z + j) % s.nz) for j in range(1, s.nz)]
    def cp(s, src, dst, kind, i, dev):
        a, b = s.sems[kind]
        return pltpu.make_async_remote_copy(src_ref=src, dst_ref=dst, send_sem=a.at[i], recv_sem=b.at[i], device_id=dev, device_id_type=MESH)
    def rows(s, ref, d, n): return ref.at[pl.ds(pl.multiple_of(d * n, 16), n), :]
    def pp(s, k):
        d = (s.d + k) % 8
        return s.cp(s.rows(s.hbm[3], d, s.pr), s.pP.at[k - 1], "p", k - 1, (d, s.z))
    def start_p(s):
        for k in (2, 6, 4, 3, 5, 7, 1): s.pp(k).start()
    def pf(s, j):
        z = (s.z + j) % s.nz
        return s.cp(s.hbm[2].at[pl.ds(pl.multiple_of(z * s.fr, 16), s.fh), :], s.pF.at[j - 1], "f", j - 1, (s.d, z))
    def start_f(s):
        for j in range(1, s.nz): s.pf(j).start()
    def fpiece(s, d, k):
        return s.hbm[2].at[pl.ds(k * s.fr + s.fh, s.fh), pl.ds(pl.multiple_of(d * s.fc, 128), s.fc)]
    def s0(s, w, i, k=0):
        d = s.chips[i] + s.sib - s.d
        if w == 2:
            return s.cp(s.fpiece(d, k), s.near[2].at[i, pl.ds(k * s.fh, s.fh)], "s", w * 4 + i, (s.sib, s.z))
        return s.cp(s.rows(s.hbm[w], d, s.qr if w == 0 else s.orr), s.near[w].at[i], "s", w * 4 + i, (s.sib, s.z))
    def s0all(s, w, i): return s.cp(s.near[w].at[i], s.near[w].at[i], "s", w * 4 + i, (s.sib, s.z))
    def start_s(s, w):
        for i in range(4):
            for k in range(s.nz if w == 2 else 1): s.s0(w, i, k).start()
    def own(s, w, i):
        v = s.v
        if w == 0: return v.QT.at[pl.ds(i * s.qr, s.qr)]
        if w == 1: return v.OT.at[pl.ds(i * s.orr, s.orr)]
        if w == 2: return v.F.at[pl.ds(0, s.nz * s.fh), pl.ds(i * s.fc, s.fc)]
        if w == 3: return v.gp.at[pl.ds(512, s.fh), pl.ds(pl.multiple_of(s.chips[i] * s.fc, 128), s.fc)]
        return v.gv.at[s.chips[i]]
    def sb(s, w, i):
        v = s.v
        if w == 0: return v.QT.at[pl.ds((4 + i) * s.qr, s.qr)]
        if w == 1: return v.OT.at[pl.ds((4 + i) * s.orr, s.orr)]
        if w == 2: return v.F.at[pl.ds(0, s.nz * s.fh), pl.ds((4 + i) * s.fc, s.fc)]
        if w == 3: return v.gp.at[pl.ds(512 + s.fh, s.fh), pl.ds(i * s.fc, s.fc)]
        return v.vs.at[i]
    def land(s, w, what):
        v = s.v
        i = ("rx", "ry", "ra", "rb", "zs").index(what)
        if w == 2 or w == 3:
            ref, base, n = (v.F, s.nz * s.fh, s.nz * s.fh) if w == 2 else (v.gp, 512 + 2 * s.fh, s.fh)
            k = split(n)
            a, m, c = [(0, n, 0), (0, n, 1), (0, k, 2), (k, n - k, 2), (0, n, 3)][i]
            return ref.at[pl.ds(base + a, m), pl.ds(c * s.fc, s.fc)]
        if w == 4:
            return [v.vs.at[4], v.vs.at[5], v.vs.at[6, pl.ds(0, 8)], v.vs.at[6, pl.ds(8, 8)], v.vs.at[7]][i]
        ref, n = (v.n1, s.qr) if w == 0 else (v.A, s.orr)
        if what == "zs": return (v.zq, v.zo)[w]
        k = split(n)
        a, m = [(0, n), (n, n), (2 * n, k), (2 * n + k, n - k)][i]
        return ref.at[pl.ds(a, m)]
    def half(s, ref, h):
        n = ref.shape[0]; k = split(n)
        return ref.at[pl.ds(0, k)] if h == 0 else ref.at[pl.ds(k, n - k)]
    def ld(s, w, i, k=0):
        src = s.fpiece(s.chips[i], k) if w == 2 else s.rows(s.hbm[w], s.chips[i], s.qr if w == 0 else s.orr)
        dst = s.own(2, i).at[pl.ds(k * s.fh, s.fh)] if w == 2 else s.own(w, i)
        return pltpu.make_async_copy(src, dst, s.v.lsem.at[w * 8 + i])
    def lds(s, w, i): return pltpu.make_async_copy(s.near[w].at[i], s.sb(w, i), s.v.lsem.at[w * 8 + 4 + i])
    def load_own(s, w):
        for i in range(4):
            for k in range(s.nz if w == 2 else 1): s.ld(w, i, k).start()
    def load_sib(s, w):
        for i in range(4):
            s.s0all(w, i).wait_recv()
            s.lds(w, i).start()
    def lp(s, k):
        src = s.rows(s.hbm[3], s.d, s.pr) if k == 0 else s.pP.at[k - 1]
        return pltpu.make_async_copy(src, s.v.PT.at[pl.ds(k * s.pr, s.pr)], s.v.lsem.at[24 + k])
    def load_p(s):
        for k in range(8):
            if k: s.pp(k).wait_recv()
            s.lp(k).start()
    def lf(s, j):
        src = s.hbm[2].at[pl.ds(pl.multiple_of(s.z * s.fr, 16), s.fh), :] if j == 0 else s.pF.at[j - 1]
        return pltpu.make_async_copy(src, s.v.gp.at[pl.ds(j * s.fh, s.fh)], s.v.lsem.at[32 + j])
    def load_f(s):
        for j in range(s.nz):
            if j: s.pf(j).wait_recv()
            s.lf(j).start()
    def cc(s, i): return s.cp(s.v.cs.at[0], s.v.cs.at[1 + i], "c", i, s.peers[i])
    def factors(s, c):
        s.v.cs[0] = jnp.full(s.v.cs.shape[1:], c, f32)
        for i in range(len(s.peers)): s.cc(i).start()
    def wait_factors(s):
        for i in range(len(s.peers)): s.cc(i).wait_recv()
    def c(s, i): return s.v.cs[i, 0:1, 0:1]
    def sibv(s, w, i):
        src = s.v.gv.at[s.chips[i] + s.sib - s.d] if w == 4 else s.v.gp.at[pl.ds(512, s.fh), pl.ds(pl.multiple_of((s.chips[i] + s.sib - s.d) * s.fc, 128), s.fc)]
        return s.cp(src, s.sb(w, i), "n", w * 13 + i, (s.sib, s.z))
    def start_v(s, w):
        for i in range(4): s.sibv(w, i).start()
    def psum(s):
        for k in range(8): s.lp(k).wait()
        n = s.pr
        for q in range(s.nz):
            t = s.c(0) * s.v.PT[0:n, q * s.pc:(q + 1) * s.pc].astype(f32)
            for k in range(1, 8): t = t + s.c(k) * s.v.PT[k * n:(k + 1) * n, q * s.pc:(q + 1) * s.pc].astype(f32)
            s.v.gp[800:800 + n, q * s.pc:(q + 1) * s.pc] = t.astype(bf16)
        for j in range(1, s.nz): s.pz(j).start()
    def pz(s, j):
        z = (s.z + j) % s.nz
        return s.cp(s.v.gp.at[pl.ds(800, s.pr), pl.ds(pl.multiple_of(z * s.pc, 128), s.pc)],
            s.v.gp.at[pl.ds(896, s.pr), pl.ds((j - 1) * s.pc, s.pc)], "z", j - 1, (s.d, z))
    def pfin(s):
        for j in range(1, s.nz): s.pz(j).wait_recv()
        t = s.v.gp[800:800 + s.pr, pl.ds(pl.multiple_of(s.z * s.pc, 128), s.pc)].astype(f32)
        for j in range(s.nz - 1): t = t + s.v.gp[896:896 + s.pr, j * s.pc:(j + 1) * s.pc].astype(f32)
        s.v.out[3][...] = t
    def fsum(s):
        for j in range(s.nz): s.lf(j).wait()
        n = s.fh; w = 2 * s.fc
        for q in range(4):
            t = s.c(0) * s.v.gp[0:n, q * w:(q + 1) * w].astype(f32)
            for j in range(1, s.nz): t = t + s.c(7 + j) * s.v.gp[j * n:(j + 1) * n, q * w:(q + 1) * w].astype(f32)
            s.v.gp[512:512 + n, q * w:(q + 1) * w] = t.astype(bf16)
        s.start_v(3)
    def mixed(s, w, i):
        if w < 3:
            pltpu.make_async_copy(s.own(w, i), s.own(w, i), s.v.lsem.at[w * 8 + i]).wait()
            s.lds(w, i).wait()
        else:
            s.sibv(w, i).wait_recv()
        if w == 3:
            return s.own(w, i)[...].astype(f32) + s.sb(w, i)[...].astype(f32)
        ks = (s.d - s.sib + 8) % 8
        return s.c(0) * s.own(w, i)[...].astype(f32) + s.v.cs[ks, 0:1, 0:1] * s.sb(w, i)[...].astype(f32)
    def nc(s, src, dst, w, slot, dev): return s.cp(src, dst, "n", w * 13 + slot, (dev, s.z))
    def ca(s, w): return s.nc(s.half(s.sb(w, 0), 0), s.land(w, "ra"), w, 4, s.xn)
    def cb(s, w): return s.nc(s.half(s.sb(w, 0), 1), s.land(w, "rb"), w, 5, s.yn)
    def cx(s, w, h): return s.nc(s.half(s.sb(w, 1), h), s.half(s.land(w, "rx"), h), w, 6 + h, s.xn)
    def cy(s, w, h): return s.nc(s.half(s.sb(w, 2), h), s.half(s.land(w, "ry"), h), w, 8 + h, s.yn)
    def a(s, w):
        def put(i):
            ref = s.sb(w, i)
            ref[...] = s.mixed(w, i).astype(ref.dtype)
        put(0); s.ca(w).start(); s.cb(w).start()
        put(1); s.cx(w, 0).start()
        put(2); s.cy(w, 1).start()
    def r(s, w):
        s.ca(w).wait_recv()
        t = s.half(s.sb(w, 2), 0)
        t[...] = (t[...].astype(f32) + s.land(w, "ra")[...].astype(f32)).astype(t.dtype)
        s.cy(w, 0).start()
        s.cb(w).wait_recv()
        t = s.half(s.sb(w, 1), 1)
        t[...] = (t[...].astype(f32) + s.land(w, "rb")[...].astype(f32)).astype(t.dtype)
        s.cx(w, 1).start()
    def zpiece(s, w, k):
        ref = s.land(w, "zs")
        if w < 2: return ref.at[k]
        if w == 4: return ref
        return ref.at[pl.ds(pl.multiple_of(k * s.fh, 16), s.fh)]
    def zland(s, w, j):
        if w < 2: return (s.v.zrq, s.v.zro)[w].at[j]
        if w == 4: return s.v.vs.at[8 + j]
        return s.v.F.at[pl.ds(s.nz * s.fh + j * s.fh, s.fh), pl.ds(4 * s.fc, s.fc)]
    def zc(s, w, j):
        to = (s.z + j) % s.nz
        return s.cp(s.zpiece(w, to), s.zland(w, j - 1), "n", w * 13 + 9 + j, (s.d, to))
    def f(s, w):
        t = s.mixed(w, 3)
        for h in (0, 1):
            s.cx(w, h).wait_recv(); s.cy(w, h).wait_recv()
        t = t + s.land(w, "rx")[...].astype(f32) + s.land(w, "ry")[...].astype(f32)
        if w == 3:
            s.v.out[2][0:s.fh, :] = t
            return
        ref = s.land(w, "zs")
        if w < 2:
            c = t.shape[1] // s.nz
            for k in range(s.nz): ref[k] = t[:, k * c:(k + 1) * c].astype(bf16)
        else:
            ref[...] = t.astype(ref.dtype)
        for j in range(1, s.nz): s.zc(w, j).start()
    def zf(s, w):
        for j in range(1, s.nz): s.zc(w, j).wait_recv()
        t = s.zpiece(w, s.z)[...].astype(f32)
        for j in range(s.nz - 1): t = t + s.zland(w, j)[...].astype(f32)
        if w == 2: s.v.out[2][s.fh:, :] = t
        else: s.v.out[w][...] = t
    def finish(s):
        for k in range(1, 8): s.pp(k).wait_send()
        for j in range(1, s.nz): s.pf(j).wait_send(); s.pz(j).wait_send()
        for w in range(3):
            for i in range(4): s.s0all(w, i).wait_send()
        for i in range(len(s.peers)): s.cc(i).wait_send()
        for w in range(5):
            if w > 2:
                for i in range(4): s.sibv(w, i).wait_send()
            s.ca(w).wait_send(); s.cb(w).wait_send()
            for h in (0, 1): s.cx(w, h).wait_send(); s.cy(w, h).wait_send()
            if w != 3:
                for j in range(1, s.nz): s.zc(w, j).wait_send()


def block_kernel(names, remote, length, tok, cot, *refs):
    refs = list(refs)
    take = lambda n: [refs.pop(0) for _ in range(n)]
    if remote:
        clip, *raw = take(6)
        y, gx, ss, *outs = take(8)
        gq, go, gf, gp, sQ, sO, sF, pP, pF = take(9)
        QT, OT, F, PT, V, sq, so, sf, sp, zq, zo, send, recv = take(13)
        gv, vs, cs, zrq, zro, lsem, *rsem = take(18)
    else:
        QT, OT, F, PT, vec, bf = take(6)
        y, gx, gq, go, gf, gp, col, dbf, ss = take(9)
        V = None
    s = Block(length=length[0], QT=QT, OT=OT, F=F, PT=PT, V=V, **dict(zip(names, refs)))
    D = s.x.shape[1]; FF = s.u.shape[1]
    cx = pltpu.make_async_copy(tok, s.x, s.isem.at[0]); cx.start()
    ce = pltpu.make_async_copy(cot, s.ey, s.isem.at[1]); ce.start()
    if remote:
        rows = sq.shape[0]
        items = [(4, 0, 16), (0, 0, rows // 2), (0, rows // 2, rows - rows // 2), (1, 0, so.shape[0]), (2, 0, F.shape[0]), (3, 0, sp.shape[0])]
        g = Gather(items, (sq, so, sf, sp, raw[4]), (zq, zo), (QT, OT, F, PT, V), send, recv)
        place_of = types.SimpleNamespace(QT=QT, OT=OT, F=F, PT=PT, gp=s.gp, n1=s.n1, A=s.A, gv=gv, vs=vs, cs=cs, zq=zq, zo=zo, zrq=zrq, zro=zro, lsem=lsem, out=outs)
        red = Reduce((gq, go, gf, gp), (pP, pF), (sQ, sO, sF), place_of, {k: (rsem[2 * i], rsem[2 * i + 1]) for i, k in enumerate("pfsczn")})
        sq[...] = raw[0][...].astype(bf16).T
        so[...] = raw[1][...].astype(bf16).T
        sf[...] = raw[2][...].astype(bf16)
        sp[...] = raw[3][...].astype(bf16).T
        greet(g.partners)
        v, q1, q2, o, f, p = range(6)
        for i in range(6): g.start(i)
        g.e1(v); g.e2(v); g.e3(v); g.e4(v)
        g.e1(q1); g.e5(v); s.unpack(); cx.wait(); s.ln1()
        g.e1(q2); g.e2(q1); g.e3(q1); g.e1(o); g.e2(q2); g.e3(q2); g.e4(q1); g.e1(f); g.e2(o); g.e3(o); g.e4(q2)
        g.e5(q1); g.e5(q2)
        s.qkv()
        def pair(hp):
            @pl.when(hp == 0)
            def _(): g.e4(o); g.e1(p)
            @pl.when(hp == 3)
            def _(): g.e2(f); g.e3(f)
            s.attend(hp)
        loop(D // 128, pair)
        g.e4(f); g.e5(o)
        s.out(); s.ln2(); g.e2(p); g.e3(p); g.e5(f); s.fc()
    else:
        s.vec[...] = vec[...]; s.bf[...] = bf[...]
        s.clear(); cx.wait()
        s.ln1(); s.qkv()
        loop(D // 128, s.attend)
        s.out(); s.ln2(); s.fc()
    ce.wait(); s.ey_mask()
    if remote: g.e4(p)
    s.wgrad(s.ey, s.u, gp, 512, FF)
    if remote: red.start_p(); g.e5(p)
    s.y()
    cy = pltpu.make_async_copy(s.er, y, s.isem.at[2]); cy.start()
    s.ef(); s.wgrad(s.n2, s.gp, gf, 512, FF)
    if remote: red.start_f(); red.start_s(2)
    s.gn2()
    cy.wait()
    s.ln2b(); s.wgrad(s.er, s.A, go, 256, D)
    if remote: red.start_s(1)
    s.eA()
    loop(D // 128, s.attend_back)
    s.wgrad(s.u, s.n1, gq, 256, D)
    if remote:
        for i in range(6): g.finish(i)
        red.start_s(0); red.load_own(1); red.load_own(2)
    s.bias_cols(); s.gn1()
    if remote: red.load_own(0)
    s.ln1b()
    cg = pltpu.make_async_copy(s.er, gx, s.isem.at[3]); cg.start()
    norm2 = s.norm()
    if not remote:
        ss[0] = norm2
        cg.wait()
        col[...] = s.col[...]; dbf[...] = s.dbf[...]
        return
    norm = jnp.sqrt(jnp.full((8, 128), norm2, f32))
    ss[...] = norm
    w = D // 8; nb = FF // 8 // 128
    for d in range(8):
        gv[d, 0:8, 0:w] = s.col[:, d * w:(d + 1) * w]
        gv[d, 0:8, w:128] = jnp.zeros((8, 128 - w), f32)
        for j in range(8):
            k = d * nb + j
            gv[d, 8 + j:9 + j, :] = s.dbf[:, k * 128:(k + 1) * 128] if j < nb else jnp.zeros((1, 128), f32)
    red.factors(jnp.minimum(1.0, clip[0] / norm))
    q, o, f, h, v = range(5)
    red.load_sib(o); red.load_sib(q); red.load_sib(f); red.load_p(); red.load_f()
    red.wait_factors()
    red.start_v(v)
    red.a(o); red.a(q); red.a(v); red.r(o); red.psum(); red.a(f); red.r(q); red.r(v); red.fsum(); red.f(o); red.f(v); red.r(f); red.a(h); red.f(q)
    red.r(h); red.zf(o); red.zf(v); red.pfin(); red.f(f); red.f(h); red.zf(q); red.zf(f)
    red.finish()
    cg.wait()


def run_block(remote, length, tok, cot, *ws):
    L, D = tok.shape
    sd = jax.ShapeDtypeStruct
    dma = pltpu.SemaphoreType.DMA
    vm = pl.BlockSpec(memory_space=pltpu.VMEM); an = pl.BlockSpec(memory_space=pl.ANY); sm = pl.BlockSpec(memory_space=pltpu.SMEM)
    extra = []
    if remote:
        nz = lax.axis_size("fsdp")
        clip, q, o, f, p, v = ws
        FF = f.shape[1] * 8
        qt, ot, pt = q.shape[::-1], o.shape[::-1], p.shape[::-1]
        fh = D // nz // 2; fc = FF // 8
        extra = [pltpu.VMEM((3 * D, D), bf16), pltpu.VMEM((D, D), bf16), pltpu.VMEM((D, FF), bf16), pltpu.VMEM((D, FF), bf16), pltpu.VMEM((8,) + v.shape, f32),
            pltpu.VMEM(qt, bf16), pltpu.VMEM(ot, bf16), pltpu.VMEM(f.shape, bf16), pltpu.VMEM(pt, bf16),
            pltpu.VMEM((nz,) + qt, bf16), pltpu.VMEM((nz,) + ot, bf16), dma((6, 11)), dma((6, 11)),
            pltpu.VMEM((8, 16, 128), f32), pltpu.VMEM((12, 16, 128), f32), pltpu.VMEM((8 + nz - 1, 8, 128), f32),
            pltpu.VMEM((nz - 1,) + qt, bf16), pltpu.VMEM((nz - 1,) + ot, bf16), dma((36,))]
        for n in (7, 3, 12, 10, 3, 65): extra += [dma((n,)), dma((n,))]
        outs = [sd((8, 128), f32), sd(qt, f32), sd(ot, f32), sd(f.shape, f32), sd(pt, f32), sd((16, 128), f32)]
        hbm = [sd((4, 3 * D // 8, D), bf16), sd((4, D // 8, D), bf16), sd((4, nz * fh, fc), bf16), sd((7, D // 8, FF), bf16), sd((nz - 1, fh, FF), bf16)]
        ins = [sm] + [vm] * 5
    else:
        FF = ws[2].shape[1]
        outs, hbm = [], []
        ins = [vm] * len(ws)
    acts = [sd((L, D), bf16), sd((L, D), bf16)]
    grads = [sd((3 * D, D), bf16), sd((D, D), bf16), sd((D, FF), bf16), sd((D, FF), bf16)]
    scr = scratch(L, D, FF)
    params = dict(collective_id=0, has_side_effects=True) if remote else {}
    if remote:
        shapes = acts + outs + grads + hbm
        specs = [an] * 2 + [vm] * 6 + [an] * 9
    else:
        shapes = acts + grads + [sd((8, D), f32), sd((1, FF), f32), sd((1,), f32)]
        specs = [an] * 6 + [vm, vm, sm]
    return pl.pallas_call(functools.partial(block_kernel, list(scr), remote), out_shape=shapes,
        in_specs=[sm, an, an] + ins, out_specs=specs, scratch_shapes=extra + list(scr.values()),
        compiler_params=pltpu.CompilerParams(vmem_limit_bytes=VLIM, **params))(length, tok, cot, *ws)


VLIM = (63 << 20) + (768 << 10)


def shards(tokens, qkv_weight, out_weight, fc_weight, proj_weight, fc_bias, vectors, cotangent, lengths, clip_norm,
           noise_qkv, noise_out, noise_fc, noise_proj, noise_fc_bias, noise_vectors):
    ndp, nz = lax.axis_size("dp"), lax.axis_size("fsdp")
    if ndp == 8:
        nb = fc_bias.shape[0] // 128
        small = jnp.concatenate([jnp.pad(vectors, ((0, 0), (0, 128 - vectors.shape[1]))), jnp.pad(fc_bias.reshape(nb, 128), ((0, 8 - nb), (0, 0)))], axis=0)
        y, gx, norm, sq, so, sf, sp, sv, *_ = run_block(True, lengths, tokens, cotangent, clip_norm.reshape(1), qkv_weight, out_weight, fc_weight, proj_weight, small)
        norm = norm[0, :1]
        finals = (sq.T, so.T, sf, sp.T, sv[8:8 + nb].reshape(-1), sv[:8, :vectors.shape[1]])
    else:
        g = lambda a: lax.all_gather(lax.all_gather(a.astype(bf16), "dp", axis=1, tiled=True), "fsdp", axis=0, tiled=True)
        vec = lax.all_gather(vectors.astype(bf16), "dp", axis=1, tiled=True).astype(f32)
        bf = lax.all_gather(fc_bias.astype(bf16), "dp", axis=0, tiled=True).astype(f32).reshape(1, -1)
        y, gx, gq, go, gf, gp, col, dbf, ss = run_block(False, lengths, tokens, cotangent, g(qkv_weight).T, g(out_weight).T, g(fc_weight), g(proj_weight).T, vec, bf)
        norm = jnp.sqrt(ss)
        factor = jnp.minimum(1.0, clip_norm / norm)
        ps = lambda a, dim: lax.psum_scatter(factor * a.astype(f32), "dp", scatter_dimension=dim, tiled=True)
        pz = lambda a: lax.psum_scatter(a.astype(bf16), "fsdp", scatter_dimension=0, tiled=True).astype(f32)
        finals = tuple(pz(ps(a, 1)) for a in (gq.T, go.T, gf, gp.T)) + lax.psum((ps(dbf[0], 0), ps(col, 1)), "fsdp")
    examples = ndp * nz
    noises = (noise_qkv, noise_out, noise_fc, noise_proj, noise_fc_bias, noise_vectors)
    return (y, gx, norm / clip_norm) + tuple(a / examples + n for a, n in zip(finals, noises))


def solution(mesh):
    both, cut = P(("dp", "fsdp"), None), P("fsdp", "dp")
    weights = (cut, cut, cut, cut, P("dp"), P(None, "dp"))
    return jax.shard_map(shards, mesh=mesh, in_specs=(both,) + weights + (both, P(("dp", "fsdp")), P()) + weights,
        out_specs=(both, both, P(("dp", "fsdp"))) + weights, check_vma=False)
```

```python
import functools
import types
import jax
import jax.numpy as jnp
from jax import lax
from jax.experimental import pallas as pl
from jax.experimental.pallas import tpu as pltpu
from jax.sharding import PartitionSpec as P

MESH = pl.DeviceIdType.MESH
f32 = jnp.float32
bf16 = jnp.bfloat16
HD=64; T=256; QB=256; C=768
EPS=1e-05
GC=0.7978845608028654
GA=0.044715

def nn(a, b): return lax.dot_general(a, b, (((1,), (0,)), ((), ())), preferred_element_type=f32)
def nt(a, b): return lax.dot_general(a, b, (((1,), (1,)), ((), ())), preferred_element_type=f32)
def at(i, n): return pl.ds(pl.multiple_of(i * n, n), n)
def loop(n, body, hooks={}):
    def step(i, c):
        for k, fn in hooks.items():
            @pl.when(i == k)
            def _(): fn()
        body(i)
        return c
    lax.fori_loop(0, n, step, 0)

class Block:
    def __init__(s, **refs):
        s.__dict__.update(refs)
        s.x = s.er
    def unpack(s):
        V = s.V
        n = V.shape[0]; w = s.x.shape[1] // n; k = s.bf.shape[1] // n // 128
        s.vec[...] = jnp.concatenate([V[d][0:8, 0:w] for d in range(n)], axis=1).astype(bf16).astype(f32)
        s.bf[...] = jnp.concatenate([V[d][8 + j:9 + j, :] for d in range(n) for j in range(k)], axis=1).astype(bf16).astype(f32)
        s.clear()
    def clear(s):
        s.col[...] = jnp.zeros_like(s.col); s.ssq[...] = jnp.zeros_like(s.ssq)
    def row(s, i): return s.vec[i:i + 1, :]
    def ln1(s):
        def body(i):
            x = s.x[at(i, T), :].astype(f32)
            c = x - jnp.mean(x, axis=1, keepdims=True)
            v = jnp.mean(c * c, axis=1, keepdims=True)
            s.n1[at(i, T), :] = (c * lax.rsqrt(v + EPS) * s.row(0) + s.row(1)).astype(bf16)
        loop(s.x.shape[0] // T, body)
    def qkv(s):
        D = s.x.shape[1]
        for part, b in ((0, 2), (1, None), (2, 3)):
            o = nt(s.n1[...], s.QT[part * D:(part + 1) * D, :])
            if b is not None: o = o + s.row(b)
            s.m[:, part * D:(part + 1) * D] = o.astype(bf16)
    def heads(s, hp):
        D = s.x.shape[1]
        q = s.m[:, at(hp, 128)] * bf16(HD ** -0.5)
        k = s.m[:, pl.ds(pl.multiple_of(D + hp * 128, 128), 128)]
        v = s.m[:, pl.ds(pl.multiple_of(2 * D + hp * 128, 128), 128)]
        return q, k, v
    def masked(s, q, k, h):
        lane = lax.broadcasted_iota(jnp.int32, q.shape, 1)
        mine = (lane // HD) == h
        free = lane == (1 - h) * HD
        zero = jnp.zeros_like(q)
        bias = jnp.where(lax.broadcasted_iota(jnp.int32, q.shape, 0) < s.length, 0.0, -1e30).astype(bf16)
        return jnp.where(mine, q, jnp.where(free, jnp.ones_like(q), zero)), jnp.where(mine, k, jnp.where(free, bias, zero))
    def scores(s, kh, qh, b):
        n = (b + 1) * QB
        o = nt(kh[:n], qh[n - QB:n])
        r = lax.broadcasted_iota(jnp.int32, (QB, QB), 0); c = lax.broadcasted_iota(jnp.int32, (QB, QB), 1)
        d = jnp.where(r <= c, o[n - QB:], -1e30)
        return jnp.concatenate([o[:n - QB], d], axis=0) if b else d
    def attend(s, hp):
        L = s.x.shape[0]; nb = L // QB
        q, k, v = s.heads(hp)
        vt = v.T
        ones = jnp.ones((16, L), bf16)
        qk = [s.masked(q, k, h) for h in (0, 1)]
        ve = [jnp.concatenate([vt[h * HD:(h + 1) * HD], ones], axis=0) for h in (0, 1)]
        units = [(h, b) for h in (0, 1) for b in range(nb)]
        S = {}
        def first(u):
            h, b = units[u]
            o = s.scores(qk[h][1], qk[h][0], b)
            S[u] = o, jnp.max(o, axis=0, keepdims=True)
        first(0)
        for u, (h, b) in enumerate(units):
            if u + 1 < len(units): first(u + 1)
            p, mx = S.pop(u)
            o = nn(ve[h][:, :(b + 1) * QB], jnp.exp(p - mx).astype(bf16))
            l = o[HD:HD + 1]
            s.lse[hp, h:h + 1, b * QB:(b + 1) * QB] = mx + jnp.log(l)
            s.ot[h * HD:(h + 1) * HD, b * QB:(b + 1) * QB] = o[:HD] / l
        s.A[:, at(hp, 128)] = s.ot[...].T.astype(bf16)
    def out(s):
        s.r[...] = s.x[...].astype(f32) + nt(s.A[...], s.OT[...]) + s.row(4)
    def ln2(s):
        def body(i):
            x = s.r[at(i, T), :]
            c = x - jnp.mean(x, axis=1, keepdims=True)
            v = jnp.mean(c * c, axis=1, keepdims=True)
            s.n2[at(i, T), :] = (c * lax.rsqrt(v + EPS) * s.row(5) + s.row(6)).astype(bf16)
        loop(s.x.shape[0] // T, body)
    def fc(s, hooks={}):
        def body(i):
            f = nn(s.n2[...], s.F[:, at(i, 512)]) + s.bf[:, at(i, 512)]
            f2 = f * f
            t = jnp.tanh(f * (GC + GC * GA * f2))
            p = 0.5 * t + 0.5
            u = f * p
            s.u[:, at(i, 512)] = u.astype(bf16)
            s.gp[:, at(i, 512)] = (p + u * (1.0 - p) * (2 * GC + 6 * GC * GA * f2)).astype(bf16)
        loop(s.u.shape[1] // 512, body, hooks)
    def ey_mask(s):
        def body(i):
            rp = i * T + lax.broadcasted_iota(jnp.int32, (T, s.x.shape[1]), 0)
            e = jnp.where(rp < s.length, s.ey[at(i, T), :].astype(f32), 0.0)
            s.ey[at(i, T), :] = e.astype(bf16)
            s.col[7:8, :] += jnp.sum(e, axis=0, keepdims=True)
        loop(s.x.shape[0] // T, body)
    def wgrad(s, lhs, rhs, out, cols, nw, hooks={}):
        n = cols // nw; R = s.lt.shape[0]; m = out.shape[0] // R
        def cp(t):
            slot = t % 2
            return pltpu.make_async_copy(s.stage.at[slot, :, pl.ds(0, nw)], out.at[at(t // n, R), at(t % n, nw)], s.dsem.at[slot])
        for c in range(m):
            def tr(i): s.lt[at(i, T), :] = lhs[:, pl.ds(pl.multiple_of(c * R + i * T, T), T)].T
            loop(R // T, tr)
            def inner(j):
                t = c * n + j
                o = nn(s.lt[...], rhs[:, at(j, nw)])
                @pl.when(t >= 2)
                def _(): cp(t - 2).wait()
                s.ssq[:, 0:nw] += jnp.sum(o * o, axis=0, keepdims=True)
                s.stage[t % 2, :, 0:nw] = o.astype(bf16)
                cp(t).start()
            loop(n, inner, hooks)
        cp(m * n - 2).wait(); cp(m * n - 1).wait()
    def y(s):
        s.er[...] = (s.r[...] + nt(s.u[...], s.PT[...]) + s.row(7)).astype(bf16)
    def ef(s):
        def body(i):
            e = (nn(s.ey[...], s.PT[:, at(i, C)]) * s.gp[:, at(i, C)].astype(f32)).astype(bf16)
            s.gp[:, at(i, C)] = e
            s.dbf[:, at(i, C)] = jnp.sum(e.astype(f32), axis=0, keepdims=True)
        loop(s.u.shape[1] // C, body)
    def ef_y(s):
        s.ef(); s.y()
    def gn2(s):
        s.G[...] = nt(s.gp[...], s.F[...])
    def lnb(s, x, gn, gain):
        c = x - jnp.mean(x, axis=1, keepdims=True)
        v = jnp.mean(c * c, axis=1, keepdims=True)
        rs = lax.rsqrt(v + EPS)
        h = c * rs
        a = gn * gain
        return h, rs * (a - jnp.mean(a, axis=1, keepdims=True) - h * jnp.mean(a * h, axis=1, keepdims=True))
    def ln2b(s):
        def body(i):
            gn = s.G[at(i, T), :]
            h, g = s.lnb(s.r[at(i, T), :], gn, s.row(5))
            s.col[5:6, :] += jnp.sum(gn * h, axis=0, keepdims=True)
            s.col[6:7, :] += jnp.sum(gn, axis=0, keepdims=True)
            g = g + s.ey[at(i, T), :].astype(f32)
            s.r[at(i, T), :] = g
            e = g.astype(bf16)
            s.er[at(i, T), :] = e
            s.col[4:5, :] += jnp.sum(e.astype(f32), axis=0, keepdims=True)
        loop(s.x.shape[0] // T, body)
    def eA(s):
        s.n2[...] = nn(s.er[...], s.OT[...]).astype(bf16)
    def attend_back(s, hp):
        L, D = s.x.shape; nb = L // QB
        q, k, v = s.heads(hp)
        e = s.n2[:, at(hp, 128)]
        kt = k.T
        ea = (e.astype(f32) * s.A[:, at(hp, 128)].astype(f32)).T
        lane = lax.broadcasted_iota(jnp.int32, e.shape, 1)
        s.dk[...] = jnp.zeros_like(s.dk); s.dv[...] = jnp.zeros_like(s.dv)
        heads = []
        for h in (0, 1):
            mine = (lane // HD) == h
            zero = jnp.zeros_like(e)
            heads.append((*s.masked(q, k, h), jnp.where(mine, e, zero), jnp.where(mine, q, zero), jnp.sum(ea[h * HD:(h + 1) * HD, :], axis=0, keepdims=True)))
        units = [(h, b) for h in (0, 1) for b in range(nb)]
        st = {}
        def one(u):
            h, b = units[u]; qh, kh, eh, qz, delta = heads[h]
            st[u] = s.scores(kh, qh, b), nt(v[:(b + 1) * QB], eh[b * QB:(b + 1) * QB])
        def two(u):
            h, b = units[u]; S, dP = st[u]
            cols = slice(b * QB, (b + 1) * QB)
            p = jnp.exp(S - s.lse[hp, h:h + 1, cols])
            st[u] = p.astype(bf16), (p * (dP - heads[h][4][:, cols])).astype(bf16)
        def three(u):
            h, b = units[u]; qh, kh, eh, qz, delta = heads[h]; p, ds = st.pop(u)
            rows = slice(0, (b + 1) * QB); cols = slice(b * QB, (b + 1) * QB)
            s.dv[rows] += nn(p, eh[cols]); s.dk[rows] += nn(ds, qz[cols])
            s.ot[h * HD:(h + 1) * HD, cols] = nn(kt[h * HD:(h + 1) * HD, rows], ds) * (HD ** -0.5)
        n = len(units)
        for u in range(-1, n + 1):
            if u + 1 < n: one(u + 1)
            if 0 <= u < n: two(u)
            if u >= 1: three(u - 1)
        s.u[:, at(hp, 128)] = s.ot[...].T.astype(bf16)
        s.u[:, pl.ds(pl.multiple_of(D + hp * 128, 128), 128)] = s.dk[...].astype(bf16)
        s.u[:, pl.ds(pl.multiple_of(2 * D + hp * 128, 128), 128)] = s.dv[...].astype(bf16)
    def bias_cols(s):
        D = s.x.shape[1]
        def body(i):
            s.col[2:3, :] += jnp.sum(s.u[at(i, T), 0:D].astype(f32), axis=0, keepdims=True)
            s.col[3:4, :] += jnp.sum(s.u[at(i, T), 2 * D:3 * D].astype(f32), axis=0, keepdims=True)
        loop(s.x.shape[0] // T, body)
    def gn1(s):
        s.G[...] = nn(s.u[:, 0:s.QT.shape[0]], s.QT[...])
    def ln1b(s):
        def body(i):
            gn = s.G[at(i, T), :]
            h, g = s.lnb(s.A[at(i, T), :].astype(f32), gn, s.row(0))
            s.col[0:1, :] += jnp.sum(gn * h, axis=0, keepdims=True)
            s.col[1:2, :] += jnp.sum(gn, axis=0, keepdims=True)
            s.er[at(i, T), :] = (s.r[at(i, T), :] + g).astype(bf16)
        loop(s.x.shape[0] // T, body)
    def norm(s):
        t = jnp.sum(s.ssq[...]) + jnp.sum(s.dbf[...] * s.dbf[...]) + jnp.sum(s.col[...] * s.col[...])
        return t

def scratch(L, D, FF, rows=None):
    return dict(
        vec=pltpu.VMEM((8, D), f32), bf=pltpu.VMEM((1, FF), f32), col=pltpu.VMEM((8, D), f32), dbf=pltpu.VMEM((1, FF), f32),
        ssq=pltpu.VMEM((1, 512), f32),
        n1=pltpu.VMEM((L, D), bf16), m=pltpu.VMEM((L, 3 * D), bf16), A=pltpu.VMEM((L, D), bf16), r=pltpu.VMEM((L, D), f32),
        n2=pltpu.VMEM((L, D), bf16), u=pltpu.VMEM((L, FF), bf16), gp=pltpu.VMEM((L, FF), bf16), er=pltpu.VMEM((L, D), bf16),
        G=pltpu.VMEM((L, D), f32), stage=pltpu.VMEM((2, D, 512), bf16), lt=pltpu.VMEM((D, L), bf16),
        lse=pltpu.VMEM((D // 128, 2, L), f32), ot=pltpu.VMEM((128, L), f32), dk=pltpu.VMEM((L, 128), f32), dv=pltpu.VMEM((L, 128), f32),
        ey=pltpu.VMEM((L, D), bf16),
        dsem=pltpu.SemaphoreType.DMA((2,)), isem=pltpu.SemaphoreType.DMA((4,)))


def place():
    d = lax.axis_index("dp"); z = lax.axis_index("fsdp")
    core = d % 2; xx = (d // 2) % 2; yy = d // 4
    return d, z, d + 1 - 2 * core, d + 2 - 4 * xx, d + 4 - 8 * yy


def greet(partners):
    for dev in partners:
        pl.semaphore_signal(pltpu.get_barrier_semaphore(), inc=1, device_id=dev, device_id_type=MESH)


def split(n):
    return n // 32 * 16 if n >= 32 else n // 2


def pack(x):
    n = x.shape[0]
    return jnp.concatenate([x[:, :128], jnp.concatenate([x[:n // 2, 128:], x[n // 2:, 128:]], axis=1)], axis=0)


def unpack(x):
    n = x.shape[0] * 2 // 3
    return jnp.concatenate([x[:n], jnp.concatenate([x[n:, :64], x[n:, 64:]], axis=0)], axis=1)


class Comm:
    def __init__(s):
        s.d, s.z, s.sib, s.xn, s.yn = place()
        s.dg = s.xn + s.yn - s.d
        s.nz = lax.axis_size("fsdp")
        s.peers = [((s.d + k) % 8, s.z) for k in range(1, 8)] + [(s.d, (s.z + j) % s.nz) for j in range(1, s.nz)]


class Gather(Comm):
    def __init__(s, items, shards, zb, full, send, recv):
        super().__init__()
        s.items = items; s.sh = shards; s.zb = zb; s.full = full; s.send = send; s.recv = recv
        s.chips = (s.d, s.xn, s.yn, s.dg)
    def cp(s, src, dst, i, slot, dev):
        return pltpu.make_async_remote_copy(src_ref=src, dst_ref=dst, send_sem=s.send.at[i, slot], recv_sem=s.recv.at[i, slot], device_id=dev, device_id_type=MESH)
    def part(s, i, d, z=None):
        w, r0, n, _ = s.items[i]
        ref = s.full[w]
        if w == 4:
            return ref.at[d, pl.ds(r0, n)]
        if w == 2:
            rows = pl.ds(0, ref.shape[0]) if z is None else pl.ds(pl.multiple_of(z * (ref.shape[0] // s.nz), 16), ref.shape[0] // s.nz)
            return ref.at[rows, pl.ds(pl.multiple_of(d * (ref.shape[1] // 8) + r0, 128), n)]
        rows = pl.ds(pl.multiple_of(d * (ref.shape[0] // 8) + r0, 16), n)
        if z is None:
            return ref.at[rows, :]
        return ref.at[rows, pl.ds(pl.multiple_of(z * (ref.shape[1] // s.nz), 128), ref.shape[1] // s.nz)]
    def block(s, i, d, half=None):
        ref = s.part(i, d, s.z if s.items[i][3] else None)
        if half is None: return ref
        n = ref.shape[0]; k = split(n)
        return ref.at[pl.ds(0, k)] if half == 0 else ref.at[pl.ds(k, n - k)]
    def rows(s, w, r0, n): return pl.ds(r0 * 3 // 2, n * 3 // 2) if w < 2 else pl.ds(r0, n)
    def shard(s, i):
        w, r0, n, _ = s.items[i]
        if w == 4: return s.sh[w]
        return s.sh[w].at[:, pl.ds(r0, n)] if w == 2 else s.sh[w].at[s.rows(w, r0, n)]
    def zslot(s, i, z):
        w, r0, n, _ = s.items[i]
        return s.zb[w].at[z, s.rows(w, r0, n)] if w < 2 else s.part(i, s.d, z)
    def zc(s, i, j, recv=False):
        other = (s.z - j + s.nz) % s.nz if recv else (s.z + j) % s.nz
        return s.cp(s.shard(i), s.zslot(i, other if recv else s.z), i, j - 1, (s.d, other))
    def start(s, i):
        if s.items[i][0] == 4:
            s.block(i, s.d)[...] = s.shard(i)[...]
            return
        s.zslot(i, s.z)[...] = s.shard(i)[...]
        if s.items[i][3]:
            s.bx(i, s.d, s.xn, 3).start()
            s.bx(i, s.d, s.yn, 4).start()
            return
        for j in range(1, s.nz):
            s.zc(i, j).start()
    def sibc(s, i, k, d):
        return s.cp(s.part(i, d), s.part(i, d), i, 7 + k, (s.sib, s.z))
    def bx(s, i, b, dev, slot, half=None):
        return s.cp(s.block(i, b, half), s.block(i, b, half), i, slot, (dev, s.z))
    def e1(s, i):
        w = s.items[i][0]
        if w < 4:
            for j in range(1, s.nz):
                s.zc(i, j, True).wait_recv()
        if w < 2:
            s.block(i, s.d)[...] = jnp.concatenate([unpack(s.zslot(i, k)[...]) for k in range(s.nz)], axis=1)
        s.bx(i, s.d, s.xn, 3).start()
        s.bx(i, s.d, s.yn, 4).start()
        s.sibc(i, 0, s.d).start()
    def e2(s, i):
        s.bx(i, s.xn, s.xn, 3).wait_recv()
        s.bx(i, s.xn, s.yn, 5, 0).start()
        if not s.items[i][3]: s.sibc(i, 1, s.xn).start()
    def e3(s, i):
        s.bx(i, s.yn, s.yn, 4).wait_recv()
        s.bx(i, s.yn, s.xn, 6, 1).start()
        if not s.items[i][3]: s.sibc(i, 2, s.yn).start()
    def e4(s, i):
        s.bx(i, s.dg, s.yn, 5, 0).wait_recv()
        s.bx(i, s.dg, s.xn, 6, 1).wait_recv()
        if not s.items[i][3]: s.sibc(i, 3, s.dg).start()
    def z1(s, i):
        for j in range(1, s.nz):
            for d in s.chips:
                s.cp(s.part(i, d, s.z), s.part(i, d, s.z), i, j - 1, (s.d, (s.z + j) % s.nz)).start()
    def zall(s, i, j):
        w, r0, n, _ = s.items[i]
        ref = s.full[w]
        ref = ref.at[pl.ds(0, ref.shape[0] // s.nz), pl.ds(0, 4 * n)] if w == 2 else ref.at[pl.ds(0, 4 * n), pl.ds(0, ref.shape[1] // s.nz)]
        return s.cp(ref, ref, i, j - 1, (s.d, (s.z + j) % s.nz))
    def z2(s, i):
        for j in range(1, s.nz): s.zall(i, j).wait_recv()
        for k, d in enumerate(s.chips): s.sibc(i, k, d).start()
    def e5(s, i):
        o = s.sib - s.d
        for k, b in enumerate(s.chips):
            s.sibc(i, k, b + o).wait_recv()
    def finish(s, i):
        if s.items[i][0] < 4:
            for j in range(1, s.nz):
                (s.zall(i, j) if s.items[i][3] else s.zc(i, j)).wait_send()
        s.bx(i, s.d, s.xn, 3).wait_send()
        s.bx(i, s.d, s.yn, 4).wait_send()
        s.bx(i, s.xn, s.yn, 5, 0).wait_send()
        s.bx(i, s.yn, s.xn, 6, 1).wait_send()
        for k, b in enumerate(s.chips):
            s.sibc(i, k, b).wait_send()


class Reduce(Comm):
    def __init__(s, hbm, far, near, v, sems):
        super().__init__()
        s.hbm = hbm; s.v = v; s.near = near
        s.pP, s.pF, s.pZ = far
        s.sems = sems
        s.chips = (s.dg, s.xn, s.yn, s.d)
        s.fr = hbm[2].shape[0] // s.nz; s.fc = hbm[2].shape[1] // 8
        s.f1 = s.pF.shape[1] // s.nz; s.f2 = s.fr - s.f1
        s.qr = hbm[0].shape[0] // 8; s.orr = hbm[1].shape[0] // 8
        s.pr = hbm[3].shape[0] // 8; s.pc = hbm[3].shape[1] // s.nz
        s.p1 = s.pZ.shape[1] // 8; s.p2 = s.pr - s.p1
        q1 = s.qr // 32 * 16 // 32 * 32
        s.qi = ((0, q1), (q1, s.qr - q1))
    def cp(s, src, dst, kind, i, dev):
        a, b = s.sems[kind]
        return pltpu.make_async_remote_copy(src_ref=src, dst_ref=dst, send_sem=a.at[i], recv_sem=b.at[i], device_id=dev, device_id_type=MESH)
    def rows(s, ref, d, n, a=0, m=None): return ref.at[pl.ds(pl.multiple_of(d * n + a, 16), n if m is None else m), :]
    def pp(s, k):
        dev = s.peers[k - 1]
        return s.cp(s.rows(s.hbm[3], dev[0], s.pr, s.p1, s.p2), s.pP.at[k - 1], "p", k - 1, dev)
    def zpart(s, z, d): return s.hbm[3].at[pl.ds(d * s.pr, s.p1), pl.ds(pl.multiple_of(z * s.pc, 128), s.pc)]
    def pz(s, j, d):
        dev = s.peers[6 + j]
        return s.cp(s.zpart(dev[1], d), s.pZ.at[j - 1, pl.ds(d * s.p1, s.p1)], "y", j - 1, dev)
    def pz_all(s, j): return s.cp(s.pZ.at[j - 1], s.pZ.at[j - 1], "y", j - 1, s.peers[6 + j])
    def start_p(s):
        for j in range(1, s.nz):
            for d in range(8): s.pz(j, d).start()
        for k in range(1, 8): s.pp(k).start()
    def fpart(s, d, z, a, n): return s.hbm[2].at[pl.ds(z * s.fr + a, n), pl.ds(pl.multiple_of(d * s.fc, 128), s.fc)]
    def pf_all(s, k): return s.cp(s.pF.at[k - 1], s.pF.at[k - 1], "f", k - 1, s.peers[k - 1])
    def start_f(s):
        for k in range(1, 8):
            dev = s.peers[k - 1]
            for z in range(s.nz):
                s.cp(s.fpart(dev[0], z, 0, s.f1), s.pF.at[k - 1, pl.ds(z * s.f1, s.f1)], "f", k - 1, dev).start()
    def s0all(s, w, i): return s.cp(s.near[w].at[i], s.near[w].at[i], "s", w * 4 + i, (s.sib, s.z))
    def start_s(s, w):
        for i in range(4):
            d = s.chips[i] + s.sib - s.d
            if w == 2:
                for z in range(s.nz):
                    s.cp(s.fpart(d, z, s.f1, s.f2), s.near[2].at[i, pl.ds(z * s.f2, s.f2)], "s", w * 4 + i, (s.sib, s.z)).start()
            else:
                s.cp(s.rows(s.hbm[w], d, s.qr if w == 0 else s.orr), s.near[w].at[i], "s", w * 4 + i, (s.sib, s.z)).start()
    def own(s, t, i):
        v = s.v
        if t < 2: return v.QT.at[pl.ds(i * s.qr + s.qi[t][0], s.qi[t][1])]
        if t == 2: return v.OT.at[pl.ds(i * s.orr, s.orr)]
        if t == 3: return v.F.at[pl.ds(s.nz * s.f1, s.nz * s.f2), pl.ds(i * s.fc, s.fc)]
        if t == 4: return v.m.at[pl.ds(pl.multiple_of(8 * s.p1 + s.chips[i] * s.p1, 16), s.p1), pl.ds(s.pc, s.pc)]
        return v.gv.at[s.chips[i]]
    def sb(s, t, i):
        v = s.v
        if t < 2: return v.QT.at[pl.ds((4 + i) * s.qr + s.qi[t][0], s.qi[t][1])]
        if t == 2: return v.OT.at[pl.ds((4 + i) * s.orr, s.orr)]
        if t == 3: return v.F.at[pl.ds(s.nz * s.f1, s.nz * s.f2), pl.ds((4 + i) * s.fc, s.fc)]
        if t == 4: return v.m.at[pl.ds((8 + i) * s.p1, s.p1), pl.ds(2 * s.pc, s.pc)]
        return v.vs.at[i]
    def land(s, t, what):
        v = s.v
        i = ("rx", "ry", "ra", "rb", "zs").index(what)
        if t == 3:
            n = s.nz * s.f2; base = s.nz * s.f1 + s.f1; k = split(n)
            a, m, c = [(0, n, 0), (0, n, 1), (0, k, 2), (k, n - k, 2), (0, n, 3)][i]
            return v.gp.at[pl.ds(base + a, m), pl.ds(c * s.fc, s.fc)]
        if t == 5:
            return [v.vs.at[4], v.vs.at[5], v.vs.at[6, pl.ds(0, 8)], v.vs.at[6, pl.ds(8, 8)], v.vs.at[7]][i]
        if t == 4: ref, base, n = v.m, 12 * s.p1, s.p1
        elif t == 2: ref, base, n = v.A, 0, s.orr
        else: ref, base, n = v.n1, t * 3 * s.qi[0][1], s.qi[t][1]
        k = split(n)
        a, m = [(0, n), (n, n), (2 * n, k), (2 * n + k, n - k)][i]
        return ref.at[pl.ds(base + a, m), pl.ds(2 * s.pc, s.pc)] if t == 4 else ref.at[pl.ds(base + a, m)]
    def half(s, ref, h):
        n = ref.shape[0]; k = split(n)
        return ref.at[pl.ds(0, k)] if h == 0 else ref.at[pl.ds(k, n - k)]
    def load_own(s, t):
        for i in range(4):
            sem = s.v.lsem.at[t * 8 + i]
            if t == 3:
                for z in range(s.nz):
                    pltpu.make_async_copy(s.fpart(s.chips[i], z, s.f1, s.f2), s.own(3, i).at[pl.ds(z * s.f2, s.f2)], sem).start()
            elif t == 2:
                pltpu.make_async_copy(s.rows(s.hbm[1], s.chips[i], s.orr), s.own(2, i), sem).start()
            else:
                pltpu.make_async_copy(s.rows(s.hbm[0], s.chips[i], s.qr, *s.qi[t]), s.own(t, i), sem).start()
    def near_of(s, t, i):
        if t < 2: return s.near[0].at[i, pl.ds(*s.qi[t])]
        return s.near[t - 1].at[i]
    def load_sib(s, t):
        for i in range(4):
            if t != 1: s.s0all(max(t - 1, 0), i).wait_recv()
            pltpu.make_async_copy(s.near_of(t, i), s.sb(t, i), s.v.lsem.at[t * 8 + 4 + i]).start()
    def slot_p(s, k): return s.v.PT.at[pl.ds(k * s.p2, s.p2)]
    def slot_f(s, k): return s.v.F.at[pl.ds(0, s.nz * s.f1), pl.ds(k * s.fc, s.fc)]
    def slot_z(s, j): return s.v.m.at[pl.ds(j // 3 * 8 * s.p1, 8 * s.p1), pl.ds(j % 3 * s.pc, s.pc)]
    def load_p(s):
        pltpu.make_async_copy(s.rows(s.hbm[3], s.d, s.pr, s.p1, s.p2), s.slot_p(0), s.v.lsem.at[32]).start()
        for k in range(1, 8):
            s.pp(k).wait_recv()
            pltpu.make_async_copy(s.pP.at[k - 1], s.slot_p(k), s.v.lsem.at[32 + k]).start()
    def load_f(s):
        for z in range(s.nz):
            pltpu.make_async_copy(s.fpart(s.d, z, 0, s.f1), s.slot_f(0).at[pl.ds(z * s.f1, s.f1)], s.v.lsem.at[40]).start()
        for k in range(1, 8):
            s.pf_all(k).wait_recv()
            pltpu.make_async_copy(s.pF.at[k - 1], s.slot_f(k), s.v.lsem.at[40 + k]).start()
    def load_z(s):
        for d in range(8):
            pltpu.make_async_copy(s.zpart(s.z, d), s.slot_z(0).at[pl.ds(d * s.p1, s.p1)], s.v.lsem.at[48]).start()
        for j in range(1, s.nz):
            s.pz_all(j).wait_recv()
            pltpu.make_async_copy(s.pZ.at[j - 1], s.slot_z(j), s.v.lsem.at[48 + j]).start()
    def loaded(s, ref, sem): pltpu.make_async_copy(ref, ref, s.v.lsem.at[sem]).wait()
    def cc(s, i): return s.cp(s.v.cs.at[0], s.v.cs.at[1 + i], "c", i, s.peers[i])
    def factors(s, c):
        s.v.cs[0] = jnp.full(s.v.cs.shape[1:], c, f32)
        for i in range(len(s.peers)): s.cc(i).start()
    def wait_factors(s):
        for i in range(len(s.peers)): s.cc(i).wait_recv()
    def c(s, i): return s.v.cs[i, 0:1, 0:1]
    def sibv(s, t, i):
        d = s.chips[i] + s.sib - s.d
        src = s.v.gv.at[d] if t == 5 else s.v.m.at[pl.ds(pl.multiple_of(8 * s.p1 + d * s.p1, 16), s.p1), pl.ds(s.pc, s.pc)]
        return s.cp(src, s.sb(t, i), "n", t * 13 + i, (s.sib, s.z))
    def start_v(s, t):
        for i in range(4): s.sibv(t, i).start()
    def sum_p(s):
        for k in range(8): s.loaded(s.slot_p(k), 32 + k)
        for q in range(s.nz):
            cols = slice(q * s.pc, (q + 1) * s.pc)
            t = sum(s.c(k) * s.v.PT[k * s.p2:(k + 1) * s.p2, cols].astype(f32) for k in range(8))
            s.v.PT[8 * s.p2:9 * s.p2, cols] = t.astype(bf16)
        for j in range(1, s.nz): s.zp(j).start()
    def zp(s, j):
        dev = s.peers[6 + j]
        return s.cp(s.v.PT.at[pl.ds(8 * s.p2, s.p2), pl.ds(pl.multiple_of(dev[1] * s.pc, 128), s.pc)],
            s.v.PT.at[pl.ds(9 * s.p2, s.p2), pl.ds((j - 1) * s.pc, s.pc)], "z", j - 1, dev)
    def fin_p(s):
        for j in range(1, s.nz): s.zp(j).wait_recv()
        t = s.v.PT[8 * s.p2:9 * s.p2, pl.ds(pl.multiple_of(s.z * s.pc, 128), s.pc)].astype(f32)
        s.v.out[3][s.p1:, :] = t + sum(s.v.PT[9 * s.p2:10 * s.p2, j * s.pc:(j + 1) * s.pc].astype(f32) for j in range(s.nz - 1))
    def sum_f(s):
        for k in range(8): s.loaded(s.slot_f(k), 40 + k)
        for q in range(s.nz):
            rows = slice(q * s.f1, (q + 1) * s.f1)
            t = sum(s.c(k) * s.v.F[rows, k * s.fc:(k + 1) * s.fc].astype(f32) for k in range(8))
            s.v.gp[rows, 0:s.fc] = t.astype(bf16)
        for j in range(1, s.nz): s.zf(j).start()
    def zf(s, j):
        dev = s.peers[6 + j]
        return s.cp(s.v.gp.at[pl.ds(pl.multiple_of(dev[1] * s.f1, 16), s.f1), pl.ds(0, s.fc)],
            s.v.gp.at[pl.ds(s.nz * s.f1, s.f1), pl.ds((j - 1) * s.fc, s.fc)], "z", 2 + j, dev)
    def fin_f(s):
        for j in range(1, s.nz): s.zf(j).wait_recv()
        t = s.v.gp[pl.ds(pl.multiple_of(s.z * s.f1, 16), s.f1), 0:s.fc].astype(f32)
        b = s.nz * s.f1
        s.v.out[2][0:s.f1, :] = t + sum(s.v.gp[b:b + s.f1, j * s.fc:(j + 1) * s.fc].astype(f32) for j in range(s.nz - 1))
    def sum_z(s):
        for j in range(s.nz): s.loaded(s.slot_z(j), 48 + j)
        n = s.p1
        for d in range(8):
            t = s.c(0) * s.v.m[d * n:(d + 1) * n, 0:s.pc].astype(f32)
            for j in range(1, s.nz):
                a = j // 3 * 8 * n + d * n; b = j % 3 * s.pc
                t = t + s.c(7 + j) * s.v.m[a:a + n, b:b + s.pc].astype(f32)
            s.v.m[(8 + d) * n:(9 + d) * n, s.pc:2 * s.pc] = t.astype(bf16)
        s.start_v(4)
    def mixed(s, t, i):
        if t < 4:
            s.loaded(s.own(t, i), t * 8 + i); s.loaded(s.sb(t, i), t * 8 + 4 + i)
        else:
            s.sibv(t, i).wait_recv()
        a, b = s.own(t, i)[...].astype(f32), s.sb(t, i)[...].astype(f32)
        if t == 4: return a + b
        return s.c(0) * a + s.v.cs[(s.d - s.sib + 8) % 8, 0:1, 0:1] * b
    def nc(s, src, dst, t, slot, dev): return s.cp(src, dst, "n", t * 13 + slot, (dev, s.z))
    def ca(s, t): return s.nc(s.half(s.sb(t, 0), 0), s.land(t, "ra"), t, 4, s.xn)
    def cb(s, t): return s.nc(s.half(s.sb(t, 0), 1), s.land(t, "rb"), t, 5, s.yn)
    def cx(s, t, h): return s.nc(s.half(s.sb(t, 1), h), s.half(s.land(t, "rx"), h), t, 6 + h, s.xn)
    def cy(s, t, h): return s.nc(s.half(s.sb(t, 2), h), s.half(s.land(t, "ry"), h), t, 8 + h, s.yn)
    def a(s, t):
        def put(i):
            ref = s.sb(t, i)
            ref[...] = s.mixed(t, i).astype(ref.dtype)
        put(0); s.ca(t).start(); s.cb(t).start()
        put(1); s.cx(t, 0).start()
        put(2); s.cy(t, 1).start()
    def r(s, t):
        s.ca(t).wait_recv()
        x = s.half(s.sb(t, 2), 0)
        x[...] = (x[...].astype(f32) + s.land(t, "ra")[...].astype(f32)).astype(x.dtype)
        s.cy(t, 0).start()
        s.cb(t).wait_recv()
        x = s.half(s.sb(t, 1), 1)
        x[...] = (x[...].astype(f32) + s.land(t, "rb")[...].astype(f32)).astype(x.dtype)
        s.cx(t, 1).start()
    def packed(s, t):
        r0, n = s.qi[t] if t < 2 else (0, s.orr)
        return pl.ds(r0 * 3 // 2, n * 3 // 2)
    def zpiece(s, t, k):
        if t < 3: return (s.v.zq, s.v.zq, s.v.zo)[t].at[k, s.packed(t)]
        ref = s.land(t, "zs")
        return ref if t == 5 else ref.at[pl.ds(pl.multiple_of(k * s.f2, 16), s.f2)]
    def zland(s, t, j):
        if t < 3: return (s.v.zrq, s.v.zrq, s.v.zro)[t].at[j, s.packed(t)]
        if t == 5: return s.v.vs.at[8 + j]
        return s.v.gp.at[pl.ds(s.nz * s.f1 + s.f1 + j * s.f2, s.f2), pl.ds(4 * s.fc, s.fc)]
    def zc(s, t, j):
        dev = s.peers[6 + j]
        return s.cp(s.zpiece(t, dev[1]), s.zland(t, j - 1), "n", t * 13 + 9 + j, dev)
    def f(s, t):
        x = s.mixed(t, 3)
        for h in (0, 1):
            s.cx(t, h).wait_recv(); s.cy(t, h).wait_recv()
        x = x + s.land(t, "rx")[...].astype(f32) + s.land(t, "ry")[...].astype(f32)
        if t == 4:
            s.v.out[3][0:s.p1, :] = x
            return
        if t < 3:
            c = x.shape[1] // s.nz
            for k in range(s.nz): s.zpiece(t, k)[...] = pack(x[:, k * c:(k + 1) * c].astype(bf16))
        else:
            ref = s.land(t, "zs")
            ref[...] = x.astype(ref.dtype)
        for j in range(1, s.nz): s.zc(t, j).start()
    def fin(s, t):
        for j in range(1, s.nz): s.zc(t, j).wait_recv()
        x = s.zpiece(t, s.z)[...].astype(f32)
        for j in range(s.nz - 1): x = x + s.zland(t, j)[...].astype(f32)
        if t == 3: s.v.out[2][s.f1:, :] = x
        elif t == 5: s.v.out[4][...] = x
        elif t == 2: s.v.out[1][...] = unpack(x)
        else: s.v.out[0][s.qi[t][0]:s.qi[t][0] + s.qi[t][1], :] = unpack(x)
    def finish(s):
        for k in range(1, 8): s.pp(k).wait_send(); s.pf_all(k).wait_send()
        for j in range(1, s.nz): s.pz_all(j).wait_send(); s.zp(j).wait_send(); s.zf(j).wait_send()
        for w in range(3):
            for i in range(4): s.s0all(w, i).wait_send()
        for i in range(len(s.peers)): s.cc(i).wait_send()
        for t in range(6):
            if t > 3:
                for i in range(4): s.sibv(t, i).wait_send()
            s.ca(t).wait_send(); s.cb(t).wait_send()
            for h in (0, 1): s.cx(t, h).wait_send(); s.cy(t, h).wait_send()
            if t != 4:
                for j in range(1, s.nz): s.zc(t, j).wait_send()


def block_kernel(names, remote, length, tok, cot, *refs):
    refs = list(refs)
    take = lambda n: [refs.pop(0) for _ in range(n)]
    if remote:
        clip, *raw = take(7)
        y, gx, ratio, *outs = take(8)
        gq, go, gf, gp, sQ, sO, sF, pP, pF, pZ = take(10)
        QT, OT, F, PT, V, sq, so, sf, sp, sv, zq, zo, send, recv = take(14)
        gv, vs, cs, zrq, zro, lsem, *rsem = take(20)
    else:
        QT, OT, F, PT, vec, bf = take(6)
        y, gx, gq, go, gf, gp, col, dbf, ss = take(9)
        V = None
    s = Block(length=length[0], QT=QT, OT=OT, F=F, PT=PT, V=V, **dict(zip(names, refs)))
    D = s.x.shape[1]; FF = s.u.shape[1]
    cx = pltpu.make_async_copy(tok, s.x, s.isem.at[0]); cx.start()
    ce = pltpu.make_async_copy(cot, s.ey, s.isem.at[1]); ce.start()
    if remote:
        places = types.SimpleNamespace(QT=QT, OT=OT, F=F, PT=PT, m=s.m, gp=s.gp, n1=s.n1, A=s.A, gv=gv, vs=vs, cs=cs, zq=zq, zo=zo, zrq=zrq, zro=zro, lsem=lsem, out=outs)
        red = Reduce((gq, go, gf, gp), (pP, pF, pZ), (sQ, sO, sF), places, {k: (rsem[2 * i], rsem[2 * i + 1]) for i, k in enumerate("pfysczn")})
        greet(g_peers := Comm().peers)
        qn = raw[0].shape[1]
        cuts = [0, 64, 128, 192, qn]
        fc = F.shape[1] // 8; pr = sp.shape[0]
        items = [(4, 0, 16, False)] + [(0, a, b - a, False) for a, b in zip(cuts, cuts[1:])] + [(1, 0, raw[1].shape[1], False),
            (2, 0, fc - 128, False), (3, 0, pr - 16, False), (2, fc - 128, 128, True), (3, pr - 16, 16, True)]
        g = Gather(items, (sq, so, sf, sp, sv), (zq, zo), (QT, OT, F, PT, V), send, recv)
        q = raw[0][...].astype(bf16).T
        for a, b in zip(cuts, cuts[1:]): sq[a * 3 // 2:b * 3 // 2, :] = pack(q[a:b])
        so[...] = pack(raw[1][...].astype(bf16).T)
        sf[...] = raw[2][...].astype(bf16)
        sp[...] = raw[3][...].astype(bf16)
        sv[...] = jnp.zeros_like(sv)
        sv[0:8, 0:raw[5].shape[1]] = raw[5][...]
        nb = raw[4].shape[1] // 128
        for j in range(nb): sv[8 + j:9 + j, :] = raw[4][:, j * 128:(j + 1) * 128]
        pl.semaphore_wait(pltpu.get_barrier_semaphore(), len(g_peers))
        v, q1, q2, q3, q4, o, f, p, f2, p2 = range(10)
        qs = (q1, q2, q3, q4)
        for i in qs + (o, v, f2, p2): g.start(i)
        g.e1(v); g.e2(v); g.e3(v); g.e2(f2); g.e3(f2); g.e2(p2); g.e3(p2); g.e4(v); g.e1(q1); g.e5(v); s.unpack(); cx.wait(); s.ln1()
        g.e1(q2); g.start(f); g.e2(q1); g.e3(q1); g.e1(q3); g.e2(q2); g.e3(q2); g.e4(q1); g.e1(q4); g.e4(f2); g.e2(q3); g.e3(q3); g.e4(q2)
        g.e1(o); g.z1(f2); g.e2(q4); g.e3(q4); g.e4(q3); g.start(p); g.e4(q4)
        for i in qs: g.e5(i)
        s.qkv()
        g.e1(f); g.e2(o); g.e3(o)
        loop(D // 128, s.attend, {2: lambda: (g.e4(o), g.e4(p2), g.z1(p2)), 5: lambda: g.e1(p)})
        g.e5(o)
        s.out(); g.e2(f); g.e3(f); s.ln2(); g.z2(f2); g.e4(f); g.e5(f); g.e5(f2)
        s.fc({3: lambda: (g.e2(p), g.e3(p))})
    else:
        s.vec[...] = vec[...]; s.bf[...] = bf[...]
        s.clear(); cx.wait()
        s.ln1(); s.qkv()
        loop(D // 128, s.attend)
        s.out(); s.ln2(); s.fc()
    ce.wait(); s.ey_mask()
    s.wgrad(s.ey, s.u, gp, FF, 512, {4: lambda: (g.e4(p), g.z2(p2))} if remote else {})
    if remote: red.start_p(); g.e5(p); g.e5(p2)
    s.ef_y(); s.wgrad(s.n2, s.gp, gf, FF, 512)
    cy = pltpu.make_async_copy(s.er, y, s.isem.at[2]); cy.start()
    if remote: red.start_f(); red.start_s(2)
    s.gn2()
    cy.wait()
    s.ln2b(); s.wgrad(s.er, s.A, go, D, 384)
    if remote: red.start_s(1)
    s.eA()
    loop(D // 128, s.attend_back)
    cx = pltpu.make_async_copy(tok, s.A, s.isem.at[0]); cx.start()
    s.wgrad(s.u, s.n1, gq, D, 384)
    if remote:
        for i in range(len(items)): g.finish(i)
        red.start_s(0); red.load_own(2); red.load_own(3)
    s.bias_cols(); s.gn1()
    if remote: red.load_own(0); red.load_own(1)
    cx.wait(); s.ln1b()
    cg = pltpu.make_async_copy(s.er, gx, s.isem.at[3]); cg.start()
    norm2 = s.norm()
    if not remote:
        ss[0] = norm2
        cg.wait()
        col[...] = s.col[...]; dbf[...] = s.dbf[...]
        return
    norm = jnp.sqrt(jnp.full((8, 128), norm2, f32))
    ratio[...] = norm / clip[0]
    red.factors(jnp.minimum(1.0, clip[0] / norm))
    w = D // 8
    for d in range(8):
        gv[d, 0:8, 0:w] = s.col[:, d * w:(d + 1) * w]
        gv[d, 0:8, w:128] = jnp.zeros((8, 128 - w), f32)
        for j in range(8):
            k = d * nb + j
            gv[d, 8 + j:9 + j, :] = s.dbf[:, k * 128:(k + 1) * 128] if j < nb else jnp.zeros((1, 128), f32)
    q1, q2, o, f, h, v = range(6)
    for t in (q1, q2, o, f): red.load_sib(t)
    red.load_f(); red.load_p(); red.load_z()
    red.wait_factors()
    red.start_v(v)
    red.a(q1); red.sum_f(); red.a(q2); red.sum_p(); red.r(q1); red.a(o); red.a(v); red.sum_z(); red.r(q2); red.a(f); red.f(q1); red.r(o); red.r(v); red.a(h)
    red.f(q2); red.r(f); red.r(h); red.f(o); red.f(v); red.f(f); red.f(h)
    red.fin_f(); red.fin_p(); red.fin(q1); red.fin(q2); red.fin(o); red.fin(v); red.fin(f)
    red.finish()
    cg.wait()


def run_block(remote, length, tok, cot, *ws):
    L, D = tok.shape
    sd = jax.ShapeDtypeStruct
    dma = pltpu.SemaphoreType.DMA
    V = pltpu.VMEM
    vm = pl.BlockSpec(memory_space=pltpu.VMEM); an = pl.BlockSpec(memory_space=pl.ANY); sm = pl.BlockSpec(memory_space=pltpu.SMEM)
    extra = []
    if remote:
        nz = lax.axis_size("fsdp")
        clip, q, o, f, p, b, v = ws
        FF = f.shape[1] * 8
        qt, ot, pt = q.shape[::-1], o.shape[::-1], p.shape
        qp, op = (qt[0] * 3 // 2, 128), (ot[0] * 3 // 2, 128)
        fr = D // nz; f1 = fr // 32 * 16; fc = FF // 8; pr = D // 8; p1 = pr // 32 * 16; pc = FF // nz
        extra = [V((3 * D, D), bf16), V((D, D), bf16), V((D, FF), bf16), V((D, FF), bf16), V((8, 16, 128), f32),
            V(qp, bf16), V(op, bf16), V(f.shape, bf16), V(pt, bf16), V((16, 128), f32),
            V((nz,) + qp, bf16), V((nz,) + op, bf16), dma((10, 11)), dma((10, 11)),
            V((8, 16, 128), f32), V((12, 16, 128), f32), V((8 + nz - 1, 8, 128), f32), V((nz - 1,) + qp, bf16), V((nz - 1,) + op, bf16), dma((52,))]
        for n in (7, 7, 3, 12, 10, 6, 78): extra += [dma((n,)), dma((n,))]
        outs = [sd((8, 128), f32), sd(qt, f32), sd(ot, f32), sd(f.shape, f32), sd(pt, f32), sd((16, 128), f32)]
        hbm = [sd((4, 3 * D // 8, D), bf16), sd((4, pr, D), bf16), sd((4, nz * (fr - f1), fc), bf16),
            sd((7, pr - p1, FF), bf16), sd((7, nz * f1, fc), bf16), sd((nz - 1, 8 * p1, pc), bf16)]
        ins = [sm] + [vm] * 6
    else:
        FF = ws[2].shape[1]
        ins = [vm] * len(ws)
    acts = [sd((L, D), bf16), sd((L, D), bf16)]
    grads = [sd((3 * D, D), bf16), sd((D, D), bf16), sd((D, FF), bf16), sd((D, FF), bf16)]
    scr = scratch(L, D, FF)
    params = dict(collective_id=0, has_side_effects=True) if remote else {}
    if remote:
        shapes = acts + outs + grads + hbm
        specs = [an] * 2 + [vm] * 6 + [an] * 10
    else:
        shapes = acts + grads + [sd((8, D), f32), sd((1, FF), f32), sd((1,), f32)]
        specs = [an] * 6 + [vm, vm, sm]
    return pl.pallas_call(functools.partial(block_kernel, list(scr), remote), out_shape=shapes,
        in_specs=[sm, an, an] + ins, out_specs=specs, scratch_shapes=extra + list(scr.values()),
        compiler_params=pltpu.CompilerParams(vmem_limit_bytes=VLIM, **params))(length, tok, cot, *ws)


VLIM = (63 << 20) + (900 << 10)


def last_kernel(examples, ratio, sq, so, sf, sp, sv, nq, no, nf, np_, nb, nv, oratio, oq, oo, of, op, ob, ov):
    oratio[0] = jnp.sum(ratio[0:1, 0:1])
    e = 1.0 / examples
    oq[...] = sq[...].T * e + nq[...]
    oo[...] = so[...].T * e + no[...]
    of[...] = sf[...] * e + nf[...]
    op[...] = sp[...] * e + np_[...]
    for j in range(ob.shape[1] // 128):
        ob[:, j * 128:(j + 1) * 128] = sv[8 + j:9 + j, :] * e + nb[:, j * 128:(j + 1) * 128]
    ov[...] = sv[0:8, 0:ov.shape[1]] * e + nv[...]


def shards(tokens, qkv_weight, out_weight, fc_weight, proj_weight, fc_bias, vectors, cotangent, lengths, clip_norm,
           noise_qkv, noise_out, noise_fc, noise_proj, noise_fc_bias, noise_vectors):
    ndp, nz = lax.axis_size("dp"), lax.axis_size("fsdp")
    examples = ndp * nz
    noises = (noise_qkv, noise_out, noise_fc, noise_proj, noise_fc_bias, noise_vectors)
    if ndp == 8:
        y, gx, ratio, sq, so, sf, sp, sv, *_ = run_block(True, lengths, tokens, cotangent, clip_norm.reshape(1), qkv_weight, out_weight, fc_weight, proj_weight.T, fc_bias.reshape(1, -1), vectors)
        sd = jax.ShapeDtypeStruct
        vm = pl.BlockSpec(memory_space=pltpu.VMEM); sm = pl.BlockSpec(memory_space=pltpu.SMEM)
        pt = proj_weight.shape[::-1]
        ratio, gq, go, gf, gp, gb, gv = pl.pallas_call(functools.partial(last_kernel, examples),
            out_shape=[sd((1,), f32), sd(qkv_weight.shape, f32), sd(out_weight.shape, f32), sd(fc_weight.shape, f32), sd(pt, f32), sd((1, fc_bias.shape[0]), f32), sd(vectors.shape, f32)],
            in_specs=[vm] * 12, out_specs=[sm] + [vm] * 6)(
            ratio, sq, so, sf, sp, sv, noise_qkv, noise_out, noise_fc, noise_proj.T, noise_fc_bias.reshape(1, -1), noise_vectors)
        return y, gx, ratio, gq, go, gf, gp.T, gb.reshape(-1), gv
    g = lambda a: lax.all_gather(lax.all_gather(a.astype(bf16), "dp", axis=1, tiled=True), "fsdp", axis=0, tiled=True)
    vec = lax.all_gather(vectors.astype(bf16), "dp", axis=1, tiled=True).astype(f32)
    bf = lax.all_gather(fc_bias.astype(bf16), "dp", axis=0, tiled=True).astype(f32).reshape(1, -1)
    y, gx, gq, go, gf, gp, col, dbf, ss = run_block(False, lengths, tokens, cotangent, g(qkv_weight).T, g(out_weight).T, g(fc_weight), g(proj_weight).T, vec, bf)
    norm = jnp.sqrt(ss)
    factor = jnp.minimum(1.0, clip_norm / norm)
    ps = lambda a, dim: lax.psum_scatter(factor * a.astype(f32), "dp", scatter_dimension=dim, tiled=True)
    pz = lambda a: lax.psum_scatter(a.astype(bf16), "fsdp", scatter_dimension=0, tiled=True).astype(f32)
    finals = tuple(pz(ps(a, 1)) for a in (gq.T, go.T, gf, gp.T)) + lax.psum((ps(dbf[0], 0), ps(col, 1)), "fsdp")
    return (y, gx, norm / clip_norm) + tuple(a / examples + n for a, n in zip(finals, noises))


def solution(mesh):
    both, cut = P(("dp", "fsdp"), None), P("fsdp", "dp")
    weights = (cut, cut, cut, cut, P("dp"), P(None, "dp"))
    return jax.shard_map(shards, mesh=mesh, in_specs=(both,) + weights + (both, P(("dp", "fsdp")), P()) + weights,
        out_specs=(both, both, P(("dp", "fsdp"))) + weights, check_vma=False)
```

```python
import functools
import types
import jax
import jax.numpy as jnp
from jax import lax
from jax.experimental import pallas as pl
from jax.experimental.pallas import tpu as pltpu
from jax.sharding import PartitionSpec as P

MESH = pl.DeviceIdType.MESH
f32 = jnp.float32
bf16 = jnp.bfloat16
HD=64; T=256; QB=256; C=768
EPS=1e-05
GC=0.7978845608028654
GA=0.044715

def nn(a, b): return lax.dot_general(a, b, (((1,), (0,)), ((), ())), preferred_element_type=f32)
def nt(a, b): return lax.dot_general(a, b, (((1,), (1,)), ((), ())), preferred_element_type=f32)
def at(i, n): return pl.ds(pl.multiple_of(i * n, n), n)
def loop(n, body, hooks={}):
    def step(i, c):
        for k, fn in hooks.items():
            @pl.when(i == k)
            def _(): fn()
        body(i)
        return c
    lax.fori_loop(0, n, step, 0)

class Block:
    def __init__(s, **refs):
        s.__dict__.update(refs)
        s.x = s.er
    def unpack(s):
        V = s.V
        n = V.shape[0]; w = s.x.shape[1] // n; k = s.bf.shape[1] // n // 128
        s.vec[...] = jnp.concatenate([V[d][0:8, 0:w] for d in range(n)], axis=1).astype(bf16).astype(f32)
        s.bf[...] = jnp.concatenate([V[d][8 + j:9 + j, :] for d in range(n) for j in range(k)], axis=1).astype(bf16).astype(f32)
        s.clear()
    def clear(s):
        s.col[...] = jnp.zeros_like(s.col); s.ssq[...] = jnp.zeros_like(s.ssq)
    def row(s, i): return s.vec[i:i + 1, :]
    def ln1(s):
        def body(i):
            x = s.x[at(i, T), :].astype(f32)
            c = x - jnp.mean(x, axis=1, keepdims=True)
            v = jnp.mean(c * c, axis=1, keepdims=True)
            s.n1[at(i, T), :] = (c * lax.rsqrt(v + EPS) * s.row(0) + s.row(1)).astype(bf16)
        loop(s.x.shape[0] // T, body)
    def qkv(s, hooks={}):
        D = s.n1.shape[1]
        for part, b in ((0, 2), (1, None), (2, 3)):
            if part in hooks: hooks[part]()
            o = nt(s.n1[...], s.QT[part * D:(part + 1) * D, :])
            if b is not None: o = o + s.row(b)
            s.m[:, part * D:(part + 1) * D] = o.astype(bf16)
    def heads(s, hp):
        D = s.x.shape[1]
        q = s.m[:, at(hp, 128)] * bf16(HD ** -0.5)
        k = s.m[:, pl.ds(pl.multiple_of(D + hp * 128, 128), 128)]
        v = s.m[:, pl.ds(pl.multiple_of(2 * D + hp * 128, 128), 128)]
        return q, k, v
    def masked(s, q, k, h):
        lane = lax.broadcasted_iota(jnp.int32, q.shape, 1)
        mine = (lane // HD) == h
        free = lane == (1 - h) * HD
        zero = jnp.zeros_like(q)
        bias = jnp.where(lax.broadcasted_iota(jnp.int32, q.shape, 0) < s.length, 0.0, -1e30).astype(bf16)
        return jnp.where(mine, q, jnp.where(free, jnp.ones_like(q), zero)), jnp.where(mine, k, jnp.where(free, bias, zero))
    def scores(s, kh, qh, b):
        n = (b + 1) * QB
        o = nt(kh[:n], qh[n - QB:n])
        r = lax.broadcasted_iota(jnp.int32, (QB, QB), 0); c = lax.broadcasted_iota(jnp.int32, (QB, QB), 1)
        d = jnp.where(r <= c, o[n - QB:], -1e30)
        return jnp.concatenate([o[:n - QB], d], axis=0) if b else d
    def attend(s, hp):
        L = s.x.shape[0]; nb = L // QB
        q, k, v = s.heads(hp)
        vt = v.T
        ones = jnp.ones((16, L), bf16)
        qk = [s.masked(q, k, h) for h in (0, 1)]
        ve = [jnp.concatenate([vt[h * HD:(h + 1) * HD], ones], axis=0) for h in (0, 1)]
        units = [(h, b) for h in (0, 1) for b in range(nb)]
        S = {}
        def first(u):
            h, b = units[u]
            o = s.scores(qk[h][1], qk[h][0], b)
            S[u] = o, jnp.max(o, axis=0, keepdims=True)
        first(0)
        for u, (h, b) in enumerate(units):
            if u + 1 < len(units): first(u + 1)
            p, mx = S.pop(u)
            o = nn(ve[h][:, :(b + 1) * QB], jnp.exp(p - mx).astype(bf16))
            l = o[HD:HD + 1]
            s.lse[hp, h:h + 1, b * QB:(b + 1) * QB] = mx + jnp.log(l)
            s.ot[h * HD:(h + 1) * HD, b * QB:(b + 1) * QB] = o[:HD] / l
        s.A[:, at(hp, 128)] = s.ot[...].T.astype(bf16)
    def out(s):
        s.r[...] = s.x[...].astype(f32) + nt(s.A[...], s.OT[...]) + s.row(4)
    def ln2(s):
        def body(i):
            x = s.r[at(i, T), :]
            c = x - jnp.mean(x, axis=1, keepdims=True)
            v = jnp.mean(c * c, axis=1, keepdims=True)
            s.n2[at(i, T), :] = (c * lax.rsqrt(v + EPS) * s.row(5) + s.row(6)).astype(bf16)
        loop(s.x.shape[0] // T, body)
    def fc(s, hooks={}, order=lambda i: i):
        n = s.u.shape[1] // 8
        def body(i):
            c = at(order(i), n)
            f = nn(s.n2[...], s.F[:, c]) + s.bf[:, c]
            f2 = f * f
            t = jnp.tanh(f * (GC + GC * GA * f2))
            p = 0.5 * t + 0.5
            u = f * p
            s.u[:, c] = u.astype(bf16)
            s.gp[:, c] = (p + u * (1.0 - p) * (2 * GC + 6 * GC * GA * f2)).astype(bf16)
        loop(8, body, hooks)
    def ey_mask(s):
        def body(i):
            rp = i * T + lax.broadcasted_iota(jnp.int32, (T, s.x.shape[1]), 0)
            e = jnp.where(rp < s.length, s.ey[at(i, T), :].astype(f32), 0.0)
            s.ey[at(i, T), :] = e.astype(bf16)
            s.col[7:8, :] += jnp.sum(e, axis=0, keepdims=True)
        loop(s.x.shape[0] // T, body)
    def wgrad(s, lhs, rhs, out, cols, nw, hooks={}):
        n = cols // nw; R = s.lt.shape[0]; m = out.shape[0] // R
        def cp(t):
            slot = t % 2
            return pltpu.make_async_copy(s.stage.at[slot, :, pl.ds(0, nw)], out.at[at(t // n, R), at(t % n, nw)], s.dsem.at[slot])
        for c in range(m):
            def tr(i): s.lt[at(i, T), :] = lhs[:, pl.ds(pl.multiple_of(c * R + i * T, T), T)].T
            loop(R // T, tr)
            def inner(j):
                t = c * n + j
                o = nn(s.lt[...], rhs[:, at(j, nw)])
                @pl.when(t >= 2)
                def _(): cp(t - 2).wait()
                s.ssq[:, 0:nw] += jnp.sum(o * o, axis=0, keepdims=True)
                s.stage[t % 2, :, 0:nw] = o.astype(bf16)
                cp(t).start()
            loop(n, inner, hooks)
        cp(m * n - 2).wait(); cp(m * n - 1).wait()
    def y(s):
        s.er[...] = (s.r[...] + nt(s.u[...], s.PT[...]) + s.row(7)).astype(bf16)
    def ef(s):
        def body(i):
            e = (nn(s.ey[...], s.PT[:, at(i, C)]) * s.gp[:, at(i, C)].astype(f32)).astype(bf16)
            s.gp[:, at(i, C)] = e
            s.dbf[:, at(i, C)] = jnp.sum(e.astype(f32), axis=0, keepdims=True)
        loop(s.u.shape[1] // C, body)
    def ef_y(s):
        s.ef(); s.y()
    def gn2(s):
        s.G[...] = nt(s.gp[...], s.F[...])
    def lnb(s, x, gn, gain):
        c = x - jnp.mean(x, axis=1, keepdims=True)
        v = jnp.mean(c * c, axis=1, keepdims=True)
        rs = lax.rsqrt(v + EPS)
        h = c * rs
        a = gn * gain
        return h, rs * (a - jnp.mean(a, axis=1, keepdims=True) - h * jnp.mean(a * h, axis=1, keepdims=True))
    def ln2b(s):
        def body(i):
            gn = s.G[at(i, T), :]
            h, g = s.lnb(s.r[at(i, T), :], gn, s.row(5))
            s.col[5:6, :] += jnp.sum(gn * h, axis=0, keepdims=True)
            s.col[6:7, :] += jnp.sum(gn, axis=0, keepdims=True)
            g = g + s.ey[at(i, T), :].astype(f32)
            s.r[at(i, T), :] = g
            e = g.astype(bf16)
            s.er[at(i, T), :] = e
            s.col[4:5, :] += jnp.sum(e.astype(f32), axis=0, keepdims=True)
        loop(s.x.shape[0] // T, body)
    def eA(s):
        s.n2[...] = nn(s.er[...], s.OT[...]).astype(bf16)
    def attend_back(s, hp):
        L, D = s.x.shape; nb = L // QB
        q, k, v = s.heads(hp)
        e = s.n2[:, at(hp, 128)]
        kt = k.T
        ea = (e.astype(f32) * s.A[:, at(hp, 128)].astype(f32)).T
        lane = lax.broadcasted_iota(jnp.int32, e.shape, 1)
        s.dk[...] = jnp.zeros_like(s.dk); s.dv[...] = jnp.zeros_like(s.dv)
        heads = []
        for h in (0, 1):
            mine = (lane // HD) == h
            zero = jnp.zeros_like(e)
            heads.append((*s.masked(q, k, h), jnp.where(mine, e, zero), jnp.where(mine, q, zero), jnp.sum(ea[h * HD:(h + 1) * HD, :], axis=0, keepdims=True)))
        units = [(h, b) for h in (0, 1) for b in range(nb)]
        st = {}
        def one(u):
            h, b = units[u]; qh, kh, eh, qz, delta = heads[h]
            st[u] = s.scores(kh, qh, b), nt(v[:(b + 1) * QB], eh[b * QB:(b + 1) * QB])
        def two(u):
            h, b = units[u]; S, dP = st[u]
            cols = slice(b * QB, (b + 1) * QB)
            p = jnp.exp(S - s.lse[hp, h:h + 1, cols])
            st[u] = p.astype(bf16), (p * (dP - heads[h][4][:, cols])).astype(bf16)
        def three(u):
            h, b = units[u]; qh, kh, eh, qz, delta = heads[h]; p, ds = st.pop(u)
            rows = slice(0, (b + 1) * QB); cols = slice(b * QB, (b + 1) * QB)
            s.dv[rows] += nn(p, eh[cols]); s.dk[rows] += nn(ds, qz[cols])
            s.ot[h * HD:(h + 1) * HD, cols] = nn(kt[h * HD:(h + 1) * HD, rows], ds) * (HD ** -0.5)
        n = len(units)
        for u in range(-1, n + 1):
            if u + 1 < n: one(u + 1)
            if 0 <= u < n: two(u)
            if u >= 1: three(u - 1)
        s.u[:, at(hp, 128)] = s.ot[...].T.astype(bf16)
        s.u[:, pl.ds(pl.multiple_of(D + hp * 128, 128), 128)] = s.dk[...].astype(bf16)
        s.u[:, pl.ds(pl.multiple_of(2 * D + hp * 128, 128), 128)] = s.dv[...].astype(bf16)
    def bias_cols(s):
        D = s.x.shape[1]
        def body(i):
            s.col[2:3, :] += jnp.sum(s.u[at(i, T), 0:D].astype(f32), axis=0, keepdims=True)
            s.col[3:4, :] += jnp.sum(s.u[at(i, T), 2 * D:3 * D].astype(f32), axis=0, keepdims=True)
        loop(s.x.shape[0] // T, body)
    def gn1(s):
        s.G[...] = nn(s.u[:, 0:s.QT.shape[0]], s.QT[...])
    def ln1b(s):
        def body(i):
            gn = s.G[at(i, T), :]
            h, g = s.lnb(s.A[at(i, T), :].astype(f32), gn, s.row(0))
            s.col[0:1, :] += jnp.sum(gn * h, axis=0, keepdims=True)
            s.col[1:2, :] += jnp.sum(gn, axis=0, keepdims=True)
            s.er[at(i, T), :] = (s.r[at(i, T), :] + g).astype(bf16)
        loop(s.x.shape[0] // T, body)
    def norm(s):
        t = jnp.sum(s.ssq[...]) + jnp.sum(s.dbf[...] * s.dbf[...]) + jnp.sum(s.col[...] * s.col[...])
        return t

def scratch(L, D, FF, rows=None):
    return dict(
        vec=pltpu.VMEM((8, D), f32), bf=pltpu.VMEM((1, FF), f32), col=pltpu.VMEM((8, D), f32), dbf=pltpu.VMEM((1, FF), f32),
        ssq=pltpu.VMEM((1, 512), f32),
        n1=pltpu.VMEM((L, D), bf16), m=pltpu.VMEM((L, 3 * D), bf16), A=pltpu.VMEM((L, D), bf16), r=pltpu.VMEM((L, D), f32),
        n2=pltpu.VMEM((L, D), bf16), u=pltpu.VMEM((L, FF), bf16), gp=pltpu.VMEM((L, FF), bf16), er=pltpu.VMEM((L, D), bf16),
        G=pltpu.VMEM((L, D), f32), stage=pltpu.VMEM((2, D, 512), bf16), lt=pltpu.VMEM((D, L), bf16),
        lse=pltpu.VMEM((D // 128, 2, L), f32), ot=pltpu.VMEM((128, L), f32), dk=pltpu.VMEM((L, 128), f32), dv=pltpu.VMEM((L, 128), f32),
        ey=pltpu.VMEM((L, D), bf16),
        dsem=pltpu.SemaphoreType.DMA((2,)), isem=pltpu.SemaphoreType.DMA((4,)))


def place():
    d = lax.axis_index("dp"); z = lax.axis_index("fsdp")
    core = d % 2; xx = (d // 2) % 2; yy = d // 4
    return d, z, d + 1 - 2 * core, d + 2 - 4 * xx, d + 4 - 8 * yy


def greet(partners):
    for dev in partners:
        pl.semaphore_signal(pltpu.get_barrier_semaphore(), inc=1, device_id=dev, device_id_type=MESH)


def split(n):
    return n // 32 * 16 if n >= 32 else n // 2


def pack(x):
    n = x.shape[0]
    return jnp.concatenate([x[:, :128], jnp.concatenate([x[:n // 2, 128:], x[n // 2:, 128:]], axis=1)], axis=0)


def unpack(x):
    n = x.shape[0] * 2 // 3
    return jnp.concatenate([x[:n], jnp.concatenate([x[n:, :64], x[n:, 64:]], axis=0)], axis=1)


class Comm:
    def __init__(s):
        s.d, s.z, s.sib, s.xn, s.yn = place()
        s.dg = s.xn + s.yn - s.d
        s.nz = lax.axis_size("fsdp")
        s.peers = [((s.d + k) % 8, s.z) for k in range(1, 8)] + [(s.d, (s.z + j) % s.nz) for j in range(1, s.nz)]


class Gather(Comm):
    def __init__(s, items, shards, zb, full, send, recv):
        super().__init__()
        s.items = items; s.sh = shards; s.zb = zb; s.full = full; s.send = send; s.recv = recv
        s.chips = (s.d, s.xn, s.yn, s.dg)
    def cp(s, src, dst, i, slot, dev):
        return pltpu.make_async_remote_copy(src_ref=src, dst_ref=dst, send_sem=s.send.at[i, slot], recv_sem=s.recv.at[i, slot], device_id=dev, device_id_type=MESH)
    def part(s, i, d, z=None):
        w, r0, n, _ = s.items[i]
        ref = s.full[w]
        if w == 4:
            return ref.at[d, pl.ds(r0, n)]
        if w == 2:
            rows = pl.ds(0, ref.shape[0]) if z is None else pl.ds(pl.multiple_of(z * (ref.shape[0] // s.nz), 16), ref.shape[0] // s.nz)
            return ref.at[rows, pl.ds(pl.multiple_of(d * (ref.shape[1] // 8) + r0, 128), n)]
        rows = pl.ds(pl.multiple_of(d * (ref.shape[0] // 8) + r0, 16), n)
        if z is None:
            return ref.at[rows, :]
        return ref.at[rows, pl.ds(pl.multiple_of(z * (ref.shape[1] // s.nz), 128), ref.shape[1] // s.nz)]
    def block(s, i, d, half=None):
        ref = s.part(i, d, s.z if s.items[i][3] else None)
        if half is None: return ref
        n = ref.shape[0]; k = split(n)
        return ref.at[pl.ds(0, k)] if half == 0 else ref.at[pl.ds(k, n - k)]
    def rows(s, w, r0, n): return pl.ds(r0 * 3 // 2, n * 3 // 2) if w < 2 else pl.ds(r0, n)
    def shard(s, i):
        w, r0, n, _ = s.items[i]
        if w == 4: return s.sh[w]
        return s.sh[w].at[:, pl.ds(r0, n)] if w == 2 else s.sh[w].at[s.rows(w, r0, n)]
    def zslot(s, i, z):
        w, r0, n, _ = s.items[i]
        return s.zb[w].at[z, s.rows(w, r0, n)] if w < 2 else s.part(i, s.d, z)
    def zc(s, i, j, recv=False):
        other = (s.z - j + s.nz) % s.nz if recv else (s.z + j) % s.nz
        return s.cp(s.shard(i), s.zslot(i, other if recv else s.z), i, j - 1, (s.d, other))
    def start(s, i):
        if s.items[i][0] == 4:
            s.block(i, s.d)[...] = s.shard(i)[...]
            return
        s.zslot(i, s.z)[...] = s.shard(i)[...]
        if s.items[i][3]:
            s.bx(i, s.d, s.xn, 3).start()
            s.bx(i, s.d, s.yn, 4).start()
            return
        for j in range(1, s.nz):
            s.zc(i, j).start()
    def sibc(s, i, k, d):
        return s.cp(s.part(i, d), s.part(i, d), i, 7 + k, (s.sib, s.z))
    def bx(s, i, b, dev, slot, half=None):
        return s.cp(s.block(i, b, half), s.block(i, b, half), i, slot, (dev, s.z))
    def e1(s, i):
        w = s.items[i][0]
        if w < 4:
            for j in range(1, s.nz):
                s.zc(i, j, True).wait_recv()
        if w < 2:
            s.block(i, s.d)[...] = jnp.concatenate([unpack(s.zslot(i, k)[...]) for k in range(s.nz)], axis=1)
        s.bx(i, s.d, s.xn, 3).start()
        s.bx(i, s.d, s.yn, 4).start()
        s.sibc(i, 0, s.d).start()
    def e2(s, i):
        s.bx(i, s.xn, s.xn, 3).wait_recv()
        s.bx(i, s.xn, s.yn, 5, 0).start()
        if not s.items[i][3]: s.sibc(i, 1, s.xn).start()
    def e3(s, i):
        s.bx(i, s.yn, s.yn, 4).wait_recv()
        s.bx(i, s.yn, s.xn, 6, 1).start()
        if not s.items[i][3]: s.sibc(i, 2, s.yn).start()
    def e4(s, i):
        s.bx(i, s.dg, s.yn, 5, 0).wait_recv()
        s.bx(i, s.dg, s.xn, 6, 1).wait_recv()
        if not s.items[i][3]: s.sibc(i, 3, s.dg).start()
    def z1(s, i):
        for j in range(1, s.nz):
            for d in s.chips:
                s.cp(s.part(i, d, s.z), s.part(i, d, s.z), i, j - 1, (s.d, (s.z + j) % s.nz)).start()
    def zall(s, i, j):
        w, r0, n, _ = s.items[i]
        ref = s.full[w]
        ref = ref.at[pl.ds(0, ref.shape[0] // s.nz), pl.ds(0, 4 * n)] if w == 2 else ref.at[pl.ds(0, 4 * n), pl.ds(0, ref.shape[1] // s.nz)]
        return s.cp(ref, ref, i, j - 1, (s.d, (s.z + j) % s.nz))
    def z2(s, i):
        for j in range(1, s.nz): s.zall(i, j).wait_recv()
        for k, d in enumerate(s.chips): s.sibc(i, k, d).start()
    def e5(s, i, ks=(0, 1, 2, 3)):
        for k in ks:
            s.sibc(i, k, s.chips[k] + s.sib - s.d).wait_recv()
    def order(s, i):
        x, y = i // 2 % 2, i // 4
        mine = s.d % 2, s.d // 2 % 2, s.d // 4
        return ((y + mine[2]) % 2 * 2 + (x + mine[1]) % 2) * 2 + (i + mine[0]) % 2
    def finish(s, i):
        if s.items[i][0] < 4:
            for j in range(1, s.nz):
                (s.zall(i, j) if s.items[i][3] else s.zc(i, j)).wait_send()
        s.bx(i, s.d, s.xn, 3).wait_send()
        s.bx(i, s.d, s.yn, 4).wait_send()
        s.bx(i, s.xn, s.yn, 5, 0).wait_send()
        s.bx(i, s.yn, s.xn, 6, 1).wait_send()
        for k, b in enumerate(s.chips):
            s.sibc(i, k, b).wait_send()


class Reduce(Comm):
    def __init__(s, hbm, far, near, v, sems):
        super().__init__()
        s.hbm = hbm; s.v = v; s.near = near
        s.pP, s.pF, s.pZ = far
        s.sems = sems
        s.chips = (s.dg, s.xn, s.yn, s.d)
        s.fr = hbm[2].shape[0] // s.nz; s.fc = hbm[2].shape[1] // 8
        s.f1 = s.pF.shape[1] // s.nz; s.f2 = s.fr - s.f1
        s.qr = hbm[0].shape[0] // 8; s.orr = hbm[1].shape[0] // 8
        s.pr = hbm[3].shape[0] // 8; s.pc = hbm[3].shape[1] // s.nz
        s.p1 = s.pZ.shape[1] // 8; s.p2 = s.pr - s.p1
        q1 = s.qr // 32 * 16 // 32 * 32
        s.qi = ((0, q1), (q1, s.qr - q1))
    def cp(s, src, dst, kind, i, dev):
        a, b = s.sems[kind]
        return pltpu.make_async_remote_copy(src_ref=src, dst_ref=dst, send_sem=a.at[i], recv_sem=b.at[i], device_id=dev, device_id_type=MESH)
    def rows(s, ref, d, n, a=0, m=None): return ref.at[pl.ds(pl.multiple_of(d * n + a, 16), n if m is None else m), :]
    def pp(s, k):
        dev = s.peers[k - 1]
        return s.cp(s.rows(s.hbm[3], dev[0], s.pr, s.p1, s.p2), s.pP.at[k - 1], "p", k - 1, dev)
    def zpart(s, z, d): return s.hbm[3].at[pl.ds(d * s.pr, s.p1), pl.ds(pl.multiple_of(z * s.pc, 128), s.pc)]
    def pz(s, j, d):
        dev = s.peers[6 + j]
        return s.cp(s.zpart(dev[1], d), s.pZ.at[j - 1, pl.ds(d * s.p1, s.p1)], "y", j - 1, dev)
    def pz_all(s, j): return s.cp(s.pZ.at[j - 1], s.pZ.at[j - 1], "y", j - 1, s.peers[6 + j])
    def start_p(s):
        for j in range(1, s.nz):
            for d in range(8): s.pz(j, d).start()
        for k in range(1, 8): s.pp(k).start()
    def fpart(s, d, z, a, n): return s.hbm[2].at[pl.ds(z * s.fr + a, n), pl.ds(pl.multiple_of(d * s.fc, 128), s.fc)]
    def pf_all(s, k): return s.cp(s.pF.at[k - 1], s.pF.at[k - 1], "f", k - 1, s.peers[k - 1])
    def start_f(s):
        for k in range(1, 8):
            dev = s.peers[k - 1]
            for z in range(s.nz):
                s.cp(s.fpart(dev[0], z, 0, s.f1), s.pF.at[k - 1, pl.ds(z * s.f1, s.f1)], "f", k - 1, dev).start()
    def s0all(s, w, i): return s.cp(s.near[w].at[i], s.near[w].at[i], "s", w * 4 + i, (s.sib, s.z))
    def start_s(s, w):
        for i in range(4):
            d = s.chips[i] + s.sib - s.d
            if w == 2:
                for z in range(s.nz):
                    s.cp(s.fpart(d, z, s.f1, s.f2), s.near[2].at[i, pl.ds(z * s.f2, s.f2)], "s", w * 4 + i, (s.sib, s.z)).start()
            else:
                s.cp(s.rows(s.hbm[w], d, s.qr if w == 0 else s.orr), s.near[w].at[i], "s", w * 4 + i, (s.sib, s.z)).start()
    def own(s, t, i):
        v = s.v
        if t < 2: return v.QT.at[pl.ds(i * s.qr + s.qi[t][0], s.qi[t][1])]
        if t == 2: return v.OT.at[pl.ds(i * s.orr, s.orr)]
        if t == 3: return v.F.at[pl.ds(s.nz * s.f1, s.nz * s.f2), pl.ds(i * s.fc, s.fc)]
        if t == 4: return v.m.at[pl.ds(pl.multiple_of(8 * s.p1 + s.chips[i] * s.p1, 16), s.p1), pl.ds(s.pc, s.pc)]
        return v.gv.at[s.chips[i]]
    def sb(s, t, i):
        v = s.v
        if t < 2: return v.QT.at[pl.ds((4 + i) * s.qr + s.qi[t][0], s.qi[t][1])]
        if t == 2: return v.OT.at[pl.ds((4 + i) * s.orr, s.orr)]
        if t == 3: return v.F.at[pl.ds(s.nz * s.f1, s.nz * s.f2), pl.ds((4 + i) * s.fc, s.fc)]
        if t == 4: return v.m.at[pl.ds((8 + i) * s.p1, s.p1), pl.ds(2 * s.pc, s.pc)]
        return v.vs.at[i]
    def land(s, t, what):
        v = s.v
        i = ("rx", "ry", "ra", "rb", "zs").index(what)
        if t == 3:
            n = s.nz * s.f2; base = s.nz * s.f1 + s.f1; k = split(n)
            a, m, c = [(0, n, 0), (0, n, 1), (0, k, 2), (k, n - k, 2), (0, n, 3)][i]
            return v.gp.at[pl.ds(base + a, m), pl.ds(c * s.fc, s.fc)]
        if t == 5:
            return [v.vs.at[4], v.vs.at[5], v.vs.at[6, pl.ds(0, 8)], v.vs.at[6, pl.ds(8, 8)], v.vs.at[7]][i]
        if t == 4: ref, base, n = v.m, 12 * s.p1, s.p1
        elif t == 2: ref, base, n = v.A, 0, s.orr
        else: ref, base, n = v.n1, t * 3 * s.qi[0][1], s.qi[t][1]
        k = split(n)
        a, m = [(0, n), (n, n), (2 * n, k), (2 * n + k, n - k)][i]
        return ref.at[pl.ds(base + a, m), pl.ds(2 * s.pc, s.pc)] if t == 4 else ref.at[pl.ds(base + a, m)]
    def half(s, ref, h):
        n = ref.shape[0]; k = split(n)
        return ref.at[pl.ds(0, k)] if h == 0 else ref.at[pl.ds(k, n - k)]
    def load_own(s, t):
        for i in range(4):
            sem = s.v.lsem.at[t * 8 + i]
            if t == 3:
                for z in range(s.nz):
                    pltpu.make_async_copy(s.fpart(s.chips[i], z, s.f1, s.f2), s.own(3, i).at[pl.ds(z * s.f2, s.f2)], sem).start()
            elif t == 2:
                pltpu.make_async_copy(s.rows(s.hbm[1], s.chips[i], s.orr), s.own(2, i), sem).start()
            else:
                pltpu.make_async_copy(s.rows(s.hbm[0], s.chips[i], s.qr, *s.qi[t]), s.own(t, i), sem).start()
    def near_of(s, t, i):
        if t < 2: return s.near[0].at[i, pl.ds(*s.qi[t])]
        return s.near[t - 1].at[i]
    def load_sib(s, t):
        for i in range(4):
            if t != 1: s.s0all(max(t - 1, 0), i).wait_recv()
            pltpu.make_async_copy(s.near_of(t, i), s.sb(t, i), s.v.lsem.at[t * 8 + 4 + i]).start()
    def slot_p(s, k): return s.v.PT.at[pl.ds(k * s.p2, s.p2)]
    def slot_f(s, k): return s.v.F.at[pl.ds(0, s.nz * s.f1), pl.ds(k * s.fc, s.fc)]
    def slot_z(s, j): return s.v.m.at[pl.ds(j // 3 * 8 * s.p1, 8 * s.p1), pl.ds(j % 3 * s.pc, s.pc)]
    def load_p(s):
        pltpu.make_async_copy(s.rows(s.hbm[3], s.d, s.pr, s.p1, s.p2), s.slot_p(0), s.v.lsem.at[32]).start()
        for k in range(1, 8):
            s.pp(k).wait_recv()
            pltpu.make_async_copy(s.pP.at[k - 1], s.slot_p(k), s.v.lsem.at[32 + k]).start()
    def load_f(s):
        for z in range(s.nz):
            pltpu.make_async_copy(s.fpart(s.d, z, 0, s.f1), s.slot_f(0).at[pl.ds(z * s.f1, s.f1)], s.v.lsem.at[40]).start()
        for k in range(1, 8):
            s.pf_all(k).wait_recv()
            pltpu.make_async_copy(s.pF.at[k - 1], s.slot_f(k), s.v.lsem.at[40 + k]).start()
    def load_z(s):
        for d in range(8):
            pltpu.make_async_copy(s.zpart(s.z, d), s.slot_z(0).at[pl.ds(d * s.p1, s.p1)], s.v.lsem.at[48]).start()
        for j in range(1, s.nz):
            s.pz_all(j).wait_recv()
            pltpu.make_async_copy(s.pZ.at[j - 1], s.slot_z(j), s.v.lsem.at[48 + j]).start()
    def loaded(s, ref, sem): pltpu.make_async_copy(ref, ref, s.v.lsem.at[sem]).wait()
    def cc(s, i): return s.cp(s.v.cs.at[0], s.v.cs.at[1 + i], "c", i, s.peers[i])
    def factors(s, c):
        s.v.cs[0] = jnp.full(s.v.cs.shape[1:], c, f32)
        for i in range(len(s.peers)): s.cc(i).start()
    def wait_factors(s):
        for i in range(len(s.peers)): s.cc(i).wait_recv()
    def c(s, i): return s.v.cs[i, 0:1, 0:1]
    def sibv(s, t, i):
        d = s.chips[i] + s.sib - s.d
        src = s.v.gv.at[d] if t == 5 else s.v.m.at[pl.ds(pl.multiple_of(8 * s.p1 + d * s.p1, 16), s.p1), pl.ds(s.pc, s.pc)]
        return s.cp(src, s.sb(t, i), "n", t * 13 + i, (s.sib, s.z))
    def start_v(s, t):
        for i in range(4): s.sibv(t, i).start()
    def sum_p(s):
        for k in range(8): s.loaded(s.slot_p(k), 32 + k)
        for q in range(s.nz):
            cols = slice(q * s.pc, (q + 1) * s.pc)
            t = sum(s.c(k) * s.v.PT[k * s.p2:(k + 1) * s.p2, cols].astype(f32) for k in range(8))
            s.v.PT[8 * s.p2:9 * s.p2, cols] = t.astype(bf16)
        s.zfirst("p")
    def zpart_of(s, t, k):
        if t == "p": return s.v.PT.at[pl.ds(8 * s.p2, s.p2), pl.ds(pl.multiple_of(k * s.pc, 128), s.pc)]
        if t == "f": return s.v.n2.at[pl.ds(pl.multiple_of(k * s.f1, 16), s.f1), pl.ds(0, s.fc)]
        return s.zpiece(t, k)
    def zland_of(s, t, j):
        if t == "p": return s.v.PT.at[pl.ds(9 * s.p2, s.p2), pl.ds(j * s.pc, s.pc)]
        if t == "f": return s.v.n2.at[pl.ds((s.nz + j // 2) * s.f1, s.f1), pl.ds(j % 2 * s.fc, s.fc)]
        return s.zland(t, j)
    def zcp(s, t, j):
        a, b = s.z + 1 - 2 * (s.z % 2), (s.z + 2) % 4
        k, to = ((a, a), (3 - s.z, a), (b, b))[j]
        kind, i = ("z", "pf".index(t) * 3 + j) if t in ("p", "f") else ("n", t * 13 + 10 + j)
        return s.cp(s.zpart_of(t, k), s.zland_of(t, j), kind, i, (s.d, to))
    def zfirst(s, t):
        s.zcp(t, 1).start(); s.zcp(t, 0).start()
    def zsecond(s, t):
        s.zcp(t, 1).wait_recv()
        ref = s.zpart_of(t, (s.z + 2) % 4)
        ref[...] = (ref[...].astype(f32) + s.zland_of(t, 1)[...].astype(f32)).astype(bf16)
        s.zcp(t, 2).start()
    def zsum(s, t):
        s.zcp(t, 0).wait_recv(); s.zcp(t, 2).wait_recv()
        return s.zpart_of(t, s.z)[...].astype(f32) + s.zland_of(t, 0)[...].astype(f32) + s.zland_of(t, 2)[...].astype(f32)
    def zsent(s, t):
        for j in range(3): s.zcp(t, j).wait_send()
    def fin_p(s): s.v.out[3][s.p1:, :] = s.zsum("p")
    def sum_f(s):
        for k in range(8): s.loaded(s.slot_f(k), 40 + k)
        for q in range(s.nz):
            rows = slice(q * s.f1, (q + 1) * s.f1)
            t = sum(s.c(k) * s.v.F[rows, k * s.fc:(k + 1) * s.fc].astype(f32) for k in range(8))
            s.v.n2[rows, 0:s.fc] = t.astype(bf16)
        s.zfirst("f")
    def fin_f(s): s.v.out[2][0:s.f1, :] = s.zsum("f")
    def sum_z(s):
        for j in range(s.nz): s.loaded(s.slot_z(j), 48 + j)
        n = s.p1
        for d in range(8):
            t = s.c(0) * s.v.m[d * n:(d + 1) * n, 0:s.pc].astype(f32)
            for j in range(1, s.nz):
                a = j // 3 * 8 * n + d * n; b = j % 3 * s.pc
                t = t + s.c(7 + j) * s.v.m[a:a + n, b:b + s.pc].astype(f32)
            s.v.m[(8 + d) * n:(9 + d) * n, s.pc:2 * s.pc] = t.astype(bf16)
        s.start_v(4)
    def mixed(s, t, i):
        if t < 4:
            s.loaded(s.own(t, i), t * 8 + i); s.loaded(s.sb(t, i), t * 8 + 4 + i)
        else:
            s.sibv(t, i).wait_recv()
        a, b = s.own(t, i)[...].astype(f32), s.sb(t, i)[...].astype(f32)
        if t == 4: return a + b
        return s.c(0) * a + s.v.cs[(s.d - s.sib + 8) % 8, 0:1, 0:1] * b
    def nc(s, src, dst, t, slot, dev): return s.cp(src, dst, "n", t * 13 + slot, (dev, s.z))
    def ca(s, t): return s.nc(s.half(s.sb(t, 0), 0), s.land(t, "ra"), t, 4, s.xn)
    def cb(s, t): return s.nc(s.half(s.sb(t, 0), 1), s.land(t, "rb"), t, 5, s.yn)
    def cx(s, t, h): return s.nc(s.half(s.sb(t, 1), h), s.half(s.land(t, "rx"), h), t, 6 + h, s.xn)
    def cy(s, t, h): return s.nc(s.half(s.sb(t, 2), h), s.half(s.land(t, "ry"), h), t, 8 + h, s.yn)
    def a(s, t):
        def put(i):
            ref = s.sb(t, i)
            ref[...] = s.mixed(t, i).astype(ref.dtype)
        put(0); s.ca(t).start(); s.cb(t).start()
        put(1); s.cx(t, 0).start()
        put(2); s.cy(t, 1).start()
    def r(s, t):
        s.ca(t).wait_recv()
        x = s.half(s.sb(t, 2), 0)
        x[...] = (x[...].astype(f32) + s.land(t, "ra")[...].astype(f32)).astype(x.dtype)
        s.cy(t, 0).start()
        s.cb(t).wait_recv()
        x = s.half(s.sb(t, 1), 1)
        x[...] = (x[...].astype(f32) + s.land(t, "rb")[...].astype(f32)).astype(x.dtype)
        s.cx(t, 1).start()
    def packed(s, t):
        r0, n = s.qi[t] if t < 2 else (0, s.orr)
        return pl.ds(r0 * 3 // 2, n * 3 // 2)
    def zpiece(s, t, k):
        if t < 3: return (s.v.zq, s.v.zq, s.v.zo)[t].at[k, s.packed(t)]
        ref = s.land(t, "zs")
        return ref if t == 5 else ref.at[pl.ds(pl.multiple_of(k * s.f2, 16), s.f2)]
    def zland(s, t, j):
        if t < 3: return (s.v.zrq, s.v.zrq, s.v.zro)[t].at[j, s.packed(t)]
        if t == 5: return s.v.vs.at[8 + j]
        return s.v.gp.at[pl.ds(s.nz * s.f1 + s.f1 + j * s.f2, s.f2), pl.ds(4 * s.fc, s.fc)]
    def zc(s, t, j):
        dev = s.peers[6 + j]
        return s.cp(s.zpiece(t, dev[1]), s.zland(t, j - 1), "n", t * 13 + 9 + j, dev)
    def f(s, t):
        x = s.mixed(t, 3)
        for h in (0, 1):
            s.cx(t, h).wait_recv(); s.cy(t, h).wait_recv()
        x = x + s.land(t, "rx")[...].astype(f32) + s.land(t, "ry")[...].astype(f32)
        if t == 4:
            s.v.out[3][0:s.p1, :] = x
            return
        if t < 3:
            c = x.shape[1] // s.nz
            for k in range(s.nz): s.zpiece(t, k)[...] = pack(x[:, k * c:(k + 1) * c].astype(bf16))
        else:
            ref = s.land(t, "zs")
            ref[...] = x.astype(ref.dtype)
        if t == 5:
            for j in range(1, s.nz): s.zc(t, j).start()
        else:
            s.zfirst(t)
    def fin(s, t):
        if t == 5:
            for j in range(1, s.nz): s.zc(t, j).wait_recv()
            x = s.zpiece(t, s.z)[...]
            for j in range(s.nz - 1): x = x + s.zland(t, j)[...]
            s.v.out[4][...] = x
            return
        x = s.zsum(t)
        if t == 3: s.v.out[2][s.f1:, :] = x
        elif t == 2: s.v.out[1][...] = unpack(x)
        else: s.v.out[0][s.qi[t][0]:s.qi[t][0] + s.qi[t][1], :] = unpack(x)
    def finish(s):
        for k in range(1, 8): s.pp(k).wait_send(); s.pf_all(k).wait_send()
        for j in range(1, s.nz): s.pz_all(j).wait_send()
        for w in range(3):
            for i in range(4): s.s0all(w, i).wait_send()
        for i in range(len(s.peers)): s.cc(i).wait_send()
        for t in range(6):
            if t > 3:
                for i in range(4): s.sibv(t, i).wait_send()
            s.ca(t).wait_send(); s.cb(t).wait_send()
            for h in (0, 1): s.cx(t, h).wait_send(); s.cy(t, h).wait_send()
            if t == 5:
                for j in range(1, s.nz): s.zc(t, j).wait_send()
            elif t != 4: s.zsent(t)
        s.zsent("p"); s.zsent("f")


def block_kernel(names, remote, length, tok, cot, *refs):
    refs = list(refs)
    take = lambda n: [refs.pop(0) for _ in range(n)]
    if remote:
        clip, *raw = take(7)
        y, gx, ratio, *outs = take(8)
        gq, go, gf, gp, sQ, sO, sF, pP, pF, pZ = take(10)
        QT, OT, F, PT, V, sq, so, sf, sp, sv, zq, zo, send, recv = take(14)
        gv, vs, cs, zrq, zro, lsem, *rsem = take(20)
    else:
        QT, OT, F, PT, vec, bf = take(6)
        y, gx, gq, go, gf, gp, col, dbf, ss = take(9)
        V = None
    s = Block(length=length[0], QT=QT, OT=OT, F=F, PT=PT, V=V, **dict(zip(names, refs)))
    D = s.x.shape[1]; FF = s.u.shape[1]
    cx = pltpu.make_async_copy(tok, s.x, s.isem.at[0]); cx.start()
    ce = pltpu.make_async_copy(cot, s.ey, s.isem.at[1]); ce.start()
    if remote:
        places = types.SimpleNamespace(QT=QT, OT=OT, F=F, PT=PT, m=s.m, gp=s.gp, n1=s.n1, n2=s.n2, A=s.A, gv=gv, vs=vs, cs=cs, zq=zq, zo=zo, zrq=zrq, zro=zro, lsem=lsem, out=outs)
        red = Reduce((gq, go, gf, gp), (pP, pF, pZ), (sQ, sO, sF), places, {k: (rsem[2 * i], rsem[2 * i + 1]) for i, k in enumerate("pfysczn")})
        greet(g_peers := Comm().peers)
        qn = raw[0].shape[1]
        cuts = [0, 64, 128, 192, qn]
        fc = F.shape[1] // 8; pr = sp.shape[0]
        p0 = pr // 48 * 32
        items = [(4, 0, 16, False)] + [(0, a, b - a, False) for a, b in zip(cuts, cuts[1:])] + [(1, 0, raw[1].shape[1], False),
            (2, 0, fc, False), (3, 0, p0, False), (3, p0, pr - p0, True)]
        g = Gather(items, (sq, so, sf, sp, sv), (zq, zo), (QT, OT, F, PT, V), send, recv)
        q = raw[0][...].astype(bf16).T
        for a, b in zip(cuts, cuts[1:]): sq[a * 3 // 2:b * 3 // 2, :] = pack(q[a:b])
        so[...] = pack(raw[1][...].astype(bf16).T)
        sf[...] = raw[2][...].astype(bf16)
        sp[...] = raw[3][...].astype(bf16)
        sv[...] = jnp.zeros_like(sv)
        sv[0:8, 0:raw[5].shape[1]] = raw[5][...]
        nb = raw[4].shape[0] // 128
        for j in range(nb): sv[8 + j:9 + j, :] = raw[4][j * 128:(j + 1) * 128].reshape(1, 128)
        pl.semaphore_wait(pltpu.get_barrier_semaphore(), len(g_peers))
        v, q1, q2, q3, q4, o, f, p, p2 = range(9)
        qs = (q1, q2, q3, q4)
        for i in qs + (o, v, p2): g.start(i)
        g.e1(v); g.e2(v); g.e3(v); g.e2(p2); g.e3(p2); g.e4(v); g.e1(q1); g.e5(v); s.unpack(); cx.wait(); s.ln1(); ce.wait(); s.ey_mask()
        g.e1(q2); g.start(f); g.e2(q1); g.e3(q1); g.e1(q3); g.e2(q2); g.e3(q2); g.e4(q1); g.e1(q4); g.e2(q3); g.e3(q3); g.e4(q2)
        g.e1(o); g.start(p); g.e2(q4); g.e3(q4); g.e4(q3); g.e4(p2); g.z1(p2); g.e4(q4)
        for i in qs: g.e5(i)
        s.qkv({2: lambda: (g.e2(o), g.e3(o))})
        g.e1(f)
        loop(D // 128, s.attend, {1: lambda: g.e4(o), 3: lambda: g.e1(p)})
        g.e5(o); g.e2(f); g.e3(f)
        s.out(); s.ln2(); g.e5(f, (0, 1, 2))
        s.fc({4: lambda: (g.e2(p), g.e3(p)), 6: lambda: (g.e4(f), g.e5(f, (3,)))}, g.order)
    else:
        s.vec[...] = vec[...]; s.bf[...] = bf[...]
        s.clear(); cx.wait()
        s.ln1(); ce.wait(); s.ey_mask(); s.qkv()
        loop(D // 128, s.attend)
        s.out(); s.ln2(); s.fc()
    s.wgrad(s.ey, s.u, gp, FF, 512, {3: lambda: g.e4(p), 5: lambda: g.z2(p2)} if remote else {})
    if remote: red.start_p(); g.e5(p); g.e5(p2)
    s.ef_y(); s.wgrad(s.n2, s.gp, gf, FF, 512)
    cy = pltpu.make_async_copy(s.er, y, s.isem.at[2]); cy.start()
    if remote: red.start_f(); red.start_s(2)
    s.gn2()
    cy.wait()
    s.ln2b(); s.wgrad(s.er, s.A, go, D, 384)
    if remote: red.start_s(1)
    s.eA()
    loop(D // 128, s.attend_back)
    cx = pltpu.make_async_copy(tok, s.A, s.isem.at[0]); cx.start()
    s.wgrad(s.u, s.n1, gq, D, 384)
    if remote:
        for i in range(len(items)): g.finish(i)
        red.start_s(0); red.load_own(2); red.load_own(3); red.load_p()
    s.bias_cols(); s.gn1()
    if remote: red.load_own(0); red.load_own(1); red.load_z()
    cx.wait(); s.ln1b()
    cg = pltpu.make_async_copy(s.er, gx, s.isem.at[3]); cg.start()
    norm2 = s.norm()
    if not remote:
        ss[0] = norm2
        cg.wait()
        col[...] = s.col[...]; dbf[...] = s.dbf[...]
        return
    norm = jnp.sqrt(jnp.full((8, 128), norm2, f32))
    ratio[...] = norm / clip[0]
    red.factors(jnp.minimum(1.0, clip[0] / norm))
    w = D // 8
    for d in range(8):
        gv[d, 0:8, 0:w] = s.col[:, d * w:(d + 1) * w]
        gv[d, 0:8, w:128] = jnp.zeros((8, 128 - w), f32)
        for j in range(8):
            k = d * nb + j
            gv[d, 8 + j:9 + j, :] = s.dbf[:, k * 128:(k + 1) * 128] if j < nb else jnp.zeros((1, 128), f32)
    q1, q2, o, f, h, v = range(6)
    for t in (q1, q2, o, f): red.load_sib(t)
    red.load_f()
    red.wait_factors()
    red.start_v(v)
    red.a(q1); red.a(q2); red.sum_p(); red.r(q1); red.a(f); red.sum_f(); red.a(v); red.r(q2); red.f(q1); red.zsecond("p"); red.sum_z(); red.a(o); red.r(v)
    red.r(f); red.zsecond("f"); red.f(q2); red.zsecond(q1); red.a(h); red.r(o); red.f(v); red.f(f); red.zsecond(q2); red.r(h); red.fin_p(); red.fin_f()
    red.f(o); red.zsecond(f); red.fin(q1); red.f(h); red.zsecond(o); red.fin(q2); red.fin(v); red.fin(f); red.fin(o)
    red.finish()
    cg.wait()


def run_block(remote, length, tok, cot, *ws):
    L, D = tok.shape
    sd = jax.ShapeDtypeStruct
    dma = pltpu.SemaphoreType.DMA
    V = pltpu.VMEM
    vm = pl.BlockSpec(memory_space=pltpu.VMEM); an = pl.BlockSpec(memory_space=pl.ANY); sm = pl.BlockSpec(memory_space=pltpu.SMEM)
    extra = []
    if remote:
        nz = lax.axis_size("fsdp")
        clip, q, o, f, p, b, v = ws
        FF = f.shape[1] * 8
        qt, ot, pt = q.shape[::-1], o.shape[::-1], p.shape
        qp, op = (qt[0] * 3 // 2, 128), (ot[0] * 3 // 2, 128)
        fr = D // nz; f1 = fr // 96 * 80; fc = FF // 8; pr = D // 8; p1 = pr // 32 * 16; pc = FF // nz
        extra = [V((3 * D, D), bf16), V((D, D), bf16), V((D, FF), bf16), V((D, FF), bf16), V((8, 16, 128), f32),
            V(qp, bf16), V(op, bf16), V(f.shape, bf16), V(pt, bf16), V((16, 128), f32),
            V((nz,) + qp, bf16), V((nz,) + op, bf16), dma((9, 11)), dma((9, 11)),
            V((8, 16, 128), f32), V((12, 16, 128), f32), V((8 + nz - 1, 8, 128), f32), V((nz - 1,) + qp, bf16), V((nz - 1,) + op, bf16), dma((52,))]
        for n in (7, 7, 3, 12, 10, 6, 78): extra += [dma((n,)), dma((n,))]
        outs = [sd((8, 128), f32), sd(qt, f32), sd(ot, f32), sd(f.shape, f32), sd(pt, f32), sd((16, 128), f32)]
        hbm = [sd((4, 3 * D // 8, D), bf16), sd((4, pr, D), bf16), sd((4, nz * (fr - f1), fc), bf16),
            sd((7, pr - p1, FF), bf16), sd((7, nz * f1, fc), bf16), sd((nz - 1, 8 * p1, pc), bf16)]
        ins = [sm] + [vm] * 6
    else:
        FF = ws[2].shape[1]
        ins = [vm] * len(ws)
    acts = [sd((L, D), bf16), sd((L, D), bf16)]
    grads = [sd((3 * D, D), bf16), sd((D, D), bf16), sd((D, FF), bf16), sd((D, FF), bf16)]
    scr = scratch(L, D, FF)
    params = dict(collective_id=0, has_side_effects=True) if remote else {}
    if remote:
        shapes = acts + outs + grads + hbm
        specs = [an] * 2 + [vm] * 6 + [an] * 10
    else:
        shapes = acts + grads + [sd((8, D), f32), sd((1, FF), f32), sd((1,), f32)]
        specs = [an] * 6 + [vm, vm, sm]
    return pl.pallas_call(functools.partial(block_kernel, list(scr), remote), out_shape=shapes,
        in_specs=[sm, an, an] + ins, out_specs=specs, scratch_shapes=extra + list(scr.values()),
        compiler_params=pltpu.CompilerParams(vmem_limit_bytes=VLIM, **params))(length, tok, cot, *ws)


VLIM = (63 << 20) + (900 << 10)


def last_kernel(examples, ratio, sq, so, sf, sp, sv, nq, no, nf, np_, nb, nv, oratio, oq, oo, of, op, ob, ov):
    oratio[0] = jnp.sum(ratio[0:1, 0:1])
    e = 1.0 / examples
    oq[...] = sq[...].T * e + nq[...]
    oo[...] = so[...].T * e + no[...]
    of[...] = sf[...] * e + nf[...]
    op[...] = sp[...] * e + np_[...]
    for j in range(ob.shape[0] // 128):
        ob[j * 128:(j + 1) * 128] = sv[8 + j:9 + j, :].reshape(128) * e + nb[j * 128:(j + 1) * 128]
    ov[...] = sv[0:8, 0:ov.shape[1]] * e + nv[...]


def shards(tokens, qkv_weight, out_weight, fc_weight, proj_weight, fc_bias, vectors, cotangent, lengths, clip_norm,
           noise_qkv, noise_out, noise_fc, noise_proj, noise_fc_bias, noise_vectors):
    ndp, nz = lax.axis_size("dp"), lax.axis_size("fsdp")
    examples = ndp * nz
    noises = (noise_qkv, noise_out, noise_fc, noise_proj, noise_fc_bias, noise_vectors)
    if ndp == 8:
        y, gx, ratio, sq, so, sf, sp, sv, *_ = run_block(True, lengths, tokens, cotangent, clip_norm.reshape(1), qkv_weight, out_weight, fc_weight, proj_weight.T, fc_bias, vectors)
        sd = jax.ShapeDtypeStruct
        vm = pl.BlockSpec(memory_space=pltpu.VMEM); sm = pl.BlockSpec(memory_space=pltpu.SMEM)
        pt = proj_weight.shape[::-1]
        ratio, gq, go, gf, gp, gb, gv = pl.pallas_call(functools.partial(last_kernel, examples),
            out_shape=[sd((1,), f32), sd(qkv_weight.shape, f32), sd(out_weight.shape, f32), sd(fc_weight.shape, f32), sd(pt, f32), sd(fc_bias.shape, f32), sd(vectors.shape, f32)],
            in_specs=[vm] * 12, out_specs=[sm] + [vm] * 6)(
            ratio, sq, so, sf, sp, sv, noise_qkv, noise_out, noise_fc, noise_proj.T, noise_fc_bias, noise_vectors)
        return y, gx, ratio, gq, go, gf, gp.T, gb, gv
    g = lambda a: lax.all_gather(lax.all_gather(a.astype(bf16), "dp", axis=1, tiled=True), "fsdp", axis=0, tiled=True)
    vec = lax.all_gather(vectors.astype(bf16), "dp", axis=1, tiled=True).astype(f32)
    bf = lax.all_gather(fc_bias.astype(bf16), "dp", axis=0, tiled=True).astype(f32).reshape(1, -1)
    y, gx, gq, go, gf, gp, col, dbf, ss = run_block(False, lengths, tokens, cotangent, g(qkv_weight).T, g(out_weight).T, g(fc_weight), g(proj_weight).T, vec, bf)
    norm = jnp.sqrt(ss)
    factor = jnp.minimum(1.0, clip_norm / norm)
    ps = lambda a, dim: lax.psum_scatter(factor * a.astype(f32), "dp", scatter_dimension=dim, tiled=True)
    pz = lambda a: lax.psum_scatter(a.astype(bf16), "fsdp", scatter_dimension=0, tiled=True).astype(f32)
    finals = tuple(pz(ps(a, 1)) for a in (gq.T, go.T, gf, gp.T)) + lax.psum((ps(dbf[0], 0), ps(col, 1)), "fsdp")
    return (y, gx, norm / clip_norm) + tuple(a / examples + n for a, n in zip(finals, noises))


def solution(mesh):
    both, cut = P(("dp", "fsdp"), None), P("fsdp", "dp")
    weights = (cut, cut, cut, cut, P("dp"), P(None, "dp"))
    return jax.shard_map(shards, mesh=mesh, in_specs=(both,) + weights + (both, P(("dp", "fsdp")), P()) + weights,
        out_specs=(both, both, P(("dp", "fsdp"))) + weights, check_vma=False)
```

```python
import functools
import types
import jax
import jax.numpy as jnp
from jax import lax
from jax.experimental import pallas as pl
from jax.experimental.pallas import tpu as pltpu
from jax.sharding import PartitionSpec as P

MESH = pl.DeviceIdType.MESH
f32 = jnp.float32
bf16 = jnp.bfloat16
HD=64; T=256; QB=256; C=768
EPS=1e-05
GC=0.7978845608028654
GA=0.044715

def nn(a, b): return lax.dot_general(a, b, (((1,), (0,)), ((), ())), preferred_element_type=f32)
def nt(a, b): return lax.dot_general(a, b, (((1,), (1,)), ((), ())), preferred_element_type=f32)
def at(i, n): return pl.ds(pl.multiple_of(i * n, n), n)
def loop(n, body, hooks={}):
    def step(i, c):
        for k, fn in hooks.items():
            @pl.when(i == k)
            def _(): fn()
        body(i)
        return c
    lax.fori_loop(0, n, step, 0)

class Block:
    def __init__(s, **refs):
        s.__dict__.update(refs)
        s.x = s.er
    def unpack(s):
        V = s.V
        n = V.shape[0]; w = s.x.shape[1] // n; k = s.bf.shape[1] // n // 128
        s.vec[...] = jnp.concatenate([V[d][0:8, 0:w] for d in range(n)], axis=1).astype(bf16).astype(f32)
        s.bf[...] = jnp.concatenate([V[d][8 + j:9 + j, :] for d in range(n) for j in range(k)], axis=1).astype(bf16).astype(f32)
        s.clear()
    def clear(s):
        s.col[...] = jnp.zeros_like(s.col); s.ssq[...] = jnp.zeros_like(s.ssq)
    def row(s, i): return s.vec[i:i + 1, :]
    def ln1(s):
        def body(i):
            x = s.x[at(i, T), :].astype(f32)
            c = x - jnp.mean(x, axis=1, keepdims=True)
            v = jnp.mean(c * c, axis=1, keepdims=True)
            s.n1[at(i, T), :] = (c * lax.rsqrt(v + EPS) * s.row(0) + s.row(1)).astype(bf16)
        loop(s.x.shape[0] // T, body)
    def qkv(s, hooks={}):
        D = s.n1.shape[1]
        for part, b in ((0, 2), (1, None), (2, 3)):
            if part in hooks: hooks[part]()
            o = nt(s.n1[...], s.QT[part * D:(part + 1) * D, :])
            if b is not None: o = o + s.row(b)
            s.m[:, part * D:(part + 1) * D] = o.astype(bf16)
    def heads(s, hp):
        D = s.x.shape[1]
        q = s.m[:, at(hp, 128)] * bf16(HD ** -0.5)
        k = s.m[:, pl.ds(pl.multiple_of(D + hp * 128, 128), 128)]
        v = s.m[:, pl.ds(pl.multiple_of(2 * D + hp * 128, 128), 128)]
        return q, k, v
    def masked(s, q, k, h):
        lane = lax.broadcasted_iota(jnp.int32, q.shape, 1)
        mine = (lane // HD) == h
        free = lane == (1 - h) * HD
        zero = jnp.zeros_like(q)
        bias = jnp.where(lax.broadcasted_iota(jnp.int32, q.shape, 0) < s.length, 0.0, -1e30).astype(bf16)
        return jnp.where(mine, q, jnp.where(free, jnp.ones_like(q), zero)), jnp.where(mine, k, jnp.where(free, bias, zero))
    def scores(s, kh, qh, b):
        n = (b + 1) * QB
        o = nt(kh[:n], qh[n - QB:n])
        r = lax.broadcasted_iota(jnp.int32, (QB, QB), 0); c = lax.broadcasted_iota(jnp.int32, (QB, QB), 1)
        d = jnp.where(r <= c, o[n - QB:], -1e30)
        return jnp.concatenate([o[:n - QB], d], axis=0) if b else d
    def attend(s, hp):
        L = s.x.shape[0]; nb = L // QB
        q, k, v = s.heads(hp)
        vt = v.T
        ones = jnp.ones((16, L), bf16)
        qk = [s.masked(q, k, h) for h in (0, 1)]
        ve = [jnp.concatenate([vt[h * HD:(h + 1) * HD], ones], axis=0) for h in (0, 1)]
        units = [(h, b) for h in (0, 1) for b in range(nb)]
        S = {}
        def first(u):
            h, b = units[u]
            o = s.scores(qk[h][1], qk[h][0], b)
            S[u] = o, jnp.max(o, axis=0, keepdims=True)
        first(0)
        for u, (h, b) in enumerate(units):
            if u + 1 < len(units): first(u + 1)
            p, mx = S.pop(u)
            o = nn(ve[h][:, :(b + 1) * QB], jnp.exp(p - mx).astype(bf16))
            l = o[HD:HD + 1]
            s.lse[hp, h:h + 1, b * QB:(b + 1) * QB] = mx + jnp.log(l)
            s.ot[h * HD:(h + 1) * HD, b * QB:(b + 1) * QB] = o[:HD] / l
        s.A[:, at(hp, 128)] = s.ot[...].T.astype(bf16)
    def out(s):
        s.r[...] = s.x[...].astype(f32) + nt(s.A[...], s.OT[...]) + s.row(4)
    def ln2(s):
        def body(i):
            x = s.r[at(i, T), :]
            c = x - jnp.mean(x, axis=1, keepdims=True)
            v = jnp.mean(c * c, axis=1, keepdims=True)
            s.n2[at(i, T), :] = (c * lax.rsqrt(v + EPS) * s.row(5) + s.row(6)).astype(bf16)
        loop(s.x.shape[0] // T, body)
    def fc(s, hooks={}, order=lambda i: i):
        n = s.u.shape[1] // 4 // T
        def body(i):
            c = at(order(i // n) * n + i % n, T)
            f = nn(s.n2[...], s.F[:, c]) + s.bf[:, c]
            f2 = f * f
            t = jnp.tanh(f * (GC + GC * GA * f2))
            p = 0.5 * t + 0.5
            u = f * p
            s.u[:, c] = u.astype(bf16)
            s.gp[:, c] = (p + u * (1.0 - p) * (2 * GC + 6 * GC * GA * f2)).astype(bf16)
        loop(4 * n, body, hooks)
    def ey_mask(s):
        def body(i):
            rp = i * T + lax.broadcasted_iota(jnp.int32, (T, s.x.shape[1]), 0)
            e = jnp.where(rp < s.length, s.ey[at(i, T), :].astype(f32), 0.0)
            s.ey[at(i, T), :] = e.astype(bf16)
            s.col[7:8, :] += jnp.sum(e, axis=0, keepdims=True)
        loop(s.x.shape[0] // T, body)
    def turn(s, lhs, c):
        R = s.lt.shape[0]
        def tr(i): s.lt[at(i, T), :] = lhs[:, pl.ds(pl.multiple_of(c * R + i * T, T), T)].T
        loop(R // T, tr)
    def wgrad(s, lhs, rhs, out, cols, nw, hooks={}, turned=False):
        n = cols // nw; R = s.lt.shape[0]; m = out.shape[0] // R
        def cp(t):
            slot = t % 2
            return pltpu.make_async_copy(s.stage.at[slot, :, pl.ds(0, nw)], out.at[at(t // n, R), at(t % n, nw)], s.dsem.at[slot])
        for c in range(m):
            if not turned: s.turn(lhs, c)
            def inner(j):
                t = c * n + j
                o = nn(s.lt[...], rhs[:, at(j, nw)])
                @pl.when(t >= 2)
                def _(): cp(t - 2).wait()
                s.ssq[:, 0:nw] += jnp.sum(o * o, axis=0, keepdims=True)
                s.stage[t % 2, :, 0:nw] = o.astype(bf16)
                cp(t).start()
            loop(n, inner, hooks)
        cp(m * n - 2).wait(); cp(m * n - 1).wait()
    def y(s):
        s.er[...] = (s.r[...] + nt(s.u[...], s.PT[...]) + s.row(7)).astype(bf16)
    def ef(s):
        def body(i):
            e = (nn(s.ey[...], s.PT[:, at(i, C)]) * s.gp[:, at(i, C)].astype(f32)).astype(bf16)
            s.gp[:, at(i, C)] = e
            s.dbf[:, at(i, C)] = jnp.sum(e.astype(f32), axis=0, keepdims=True)
        loop(s.u.shape[1] // C, body)
    def ef_y(s):
        s.ef(); s.y()
    def gn2(s):
        s.G[...] = nt(s.gp[...], s.F[...])
    def lnb(s, x, gn, gain):
        c = x - jnp.mean(x, axis=1, keepdims=True)
        v = jnp.mean(c * c, axis=1, keepdims=True)
        rs = lax.rsqrt(v + EPS)
        h = c * rs
        a = gn * gain
        return h, rs * (a - jnp.mean(a, axis=1, keepdims=True) - h * jnp.mean(a * h, axis=1, keepdims=True))
    def ln2b(s):
        def body(i):
            gn = s.G[at(i, T), :]
            h, g = s.lnb(s.r[at(i, T), :], gn, s.row(5))
            s.col[5:6, :] += jnp.sum(gn * h, axis=0, keepdims=True)
            s.col[6:7, :] += jnp.sum(gn, axis=0, keepdims=True)
            g = g + s.ey[at(i, T), :].astype(f32)
            s.r[at(i, T), :] = g
            e = g.astype(bf16)
            s.er[at(i, T), :] = e
            s.col[4:5, :] += jnp.sum(e.astype(f32), axis=0, keepdims=True)
        loop(s.x.shape[0] // T, body)
    def eA(s):
        s.n2[...] = nn(s.er[...], s.OT[...]).astype(bf16)
    def attend_back(s, hp):
        L, D = s.x.shape; nb = L // QB
        q, k, v = s.heads(hp)
        e = s.n2[:, at(hp, 128)]
        kt = k.T
        ea = (e.astype(f32) * s.A[:, at(hp, 128)].astype(f32)).T
        lane = lax.broadcasted_iota(jnp.int32, e.shape, 1)
        s.dk[...] = jnp.zeros_like(s.dk); s.dv[...] = jnp.zeros_like(s.dv)
        heads = []
        for h in (0, 1):
            mine = (lane // HD) == h
            zero = jnp.zeros_like(e)
            heads.append((*s.masked(q, k, h), jnp.where(mine, e, zero), jnp.where(mine, q, zero), jnp.sum(ea[h * HD:(h + 1) * HD, :], axis=0, keepdims=True)))
        units = [(h, b) for h in (0, 1) for b in range(nb)]
        st = {}
        def one(u):
            h, b = units[u]; qh, kh, eh, qz, delta = heads[h]
            st[u] = s.scores(kh, qh, b), nt(v[:(b + 1) * QB], eh[b * QB:(b + 1) * QB])
        def two(u):
            h, b = units[u]; S, dP = st[u]
            cols = slice(b * QB, (b + 1) * QB)
            p = jnp.exp(S - s.lse[hp, h:h + 1, cols])
            st[u] = p.astype(bf16), (p * (dP - heads[h][4][:, cols])).astype(bf16)
        def three(u):
            h, b = units[u]; qh, kh, eh, qz, delta = heads[h]; p, ds = st.pop(u)
            rows = slice(0, (b + 1) * QB); cols = slice(b * QB, (b + 1) * QB)
            s.dv[rows] += nn(p, eh[cols]); s.dk[rows] += nn(ds, qz[cols])
            s.ot[h * HD:(h + 1) * HD, cols] = nn(kt[h * HD:(h + 1) * HD, rows], ds) * (HD ** -0.5)
        n = len(units)
        for u in range(-1, n + 1):
            if u + 1 < n: one(u + 1)
            if 0 <= u < n: two(u)
            if u >= 1: three(u - 1)
        s.u[:, at(hp, 128)] = s.ot[...].T.astype(bf16)
        s.u[:, pl.ds(pl.multiple_of(D + hp * 128, 128), 128)] = s.dk[...].astype(bf16)
        s.u[:, pl.ds(pl.multiple_of(2 * D + hp * 128, 128), 128)] = s.dv[...].astype(bf16)
    def bias_cols(s):
        D = s.x.shape[1]
        def body(i):
            s.col[2:3, :] += jnp.sum(s.u[at(i, T), 0:D].astype(f32), axis=0, keepdims=True)
            s.col[3:4, :] += jnp.sum(s.u[at(i, T), 2 * D:3 * D].astype(f32), axis=0, keepdims=True)
        loop(s.x.shape[0] // T, body)
    def gn1(s):
        s.G[...] = nn(s.u[:, 0:s.QT.shape[0]], s.QT[...])
    def ln1b(s):
        def body(i):
            gn = s.G[at(i, T), :]
            h, g = s.lnb(s.A[at(i, T), :].astype(f32), gn, s.row(0))
            s.col[0:1, :] += jnp.sum(gn * h, axis=0, keepdims=True)
            s.col[1:2, :] += jnp.sum(gn, axis=0, keepdims=True)
            s.er[at(i, T), :] = (s.r[at(i, T), :] + g).astype(bf16)
        loop(s.x.shape[0] // T, body)
    def norm(s):
        t = jnp.sum(s.ssq[...]) + jnp.sum(s.dbf[...] * s.dbf[...]) + jnp.sum(s.col[...] * s.col[...])
        return t

def scratch(L, D, FF, rows=None):
    return dict(
        vec=pltpu.VMEM((8, D), f32), bf=pltpu.VMEM((1, FF), f32), col=pltpu.VMEM((8, D), f32), dbf=pltpu.VMEM((1, FF), f32),
        ssq=pltpu.VMEM((1, 512), f32),
        n1=pltpu.VMEM((L, D), bf16), m=pltpu.VMEM((L, 3 * D), bf16), A=pltpu.VMEM((L, D), bf16), r=pltpu.VMEM((L, D), f32),
        n2=pltpu.VMEM((L, D), bf16), u=pltpu.VMEM((L, FF), bf16), gp=pltpu.VMEM((L, FF), bf16), er=pltpu.VMEM((L, D), bf16),
        G=pltpu.VMEM((L, D), f32), stage=pltpu.VMEM((2, D, 512), bf16), lt=pltpu.VMEM((D, L), bf16),
        lse=pltpu.VMEM((D // 128, 2, L), f32), ot=pltpu.VMEM((128, L), f32), dk=pltpu.VMEM((L, 128), f32), dv=pltpu.VMEM((L, 128), f32),
        ey=pltpu.VMEM((L, D), bf16),
        dsem=pltpu.SemaphoreType.DMA((2,)), isem=pltpu.SemaphoreType.DMA((4,)))


def place():
    d = lax.axis_index("dp"); z = lax.axis_index("fsdp")
    core = d % 2; xx = (d // 2) % 2; yy = d // 4
    return d, z, d + 1 - 2 * core, d + 2 - 4 * xx, d + 4 - 8 * yy


def greet(partners):
    for dev in partners:
        pl.semaphore_signal(pltpu.get_barrier_semaphore(), inc=1, device_id=dev, device_id_type=MESH)


def split(n):
    return n // 32 * 16 if n >= 32 else n // 2


def pack(x):
    n = x.shape[0]
    return jnp.concatenate([x[:, :128], jnp.concatenate([x[:n // 2, 128:], x[n // 2:, 128:]], axis=1)], axis=0)


def unpack(x):
    n = x.shape[0] * 2 // 3
    return jnp.concatenate([x[:n], jnp.concatenate([x[n:, :64], x[n:, 64:]], axis=0)], axis=1)


class Comm:
    def __init__(s):
        s.d, s.z, s.sib, s.xn, s.yn = place()
        s.dg = s.xn + s.yn - s.d
        s.nz = lax.axis_size("fsdp")
        s.peers = [((s.d + k) % 8, s.z) for k in range(1, 8)] + [(s.d, (s.z + j) % s.nz) for j in range(1, s.nz)]


class Gather(Comm):
    def __init__(s, items, shards, zb, full, send, recv):
        super().__init__()
        s.items = items; s.sh = shards; s.zb = zb; s.full = full; s.send = send; s.recv = recv
        s.chips = (s.d, s.xn, s.yn, s.dg)
    def cp(s, src, dst, i, slot, dev):
        return pltpu.make_async_remote_copy(src_ref=src, dst_ref=dst, send_sem=s.send.at[i, slot], recv_sem=s.recv.at[i, slot], device_id=dev, device_id_type=MESH)
    def part(s, i, d, z=None):
        w, r0, n, _ = s.items[i]
        ref = s.full[w]
        if w == 4:
            return ref.at[d, pl.ds(r0, n)]
        if w == 2:
            rows = pl.ds(0, ref.shape[0]) if z is None else pl.ds(pl.multiple_of(z * (ref.shape[0] // s.nz), 16), ref.shape[0] // s.nz)
            return ref.at[rows, pl.ds(pl.multiple_of(d * (ref.shape[1] // 8) + r0, 128), n)]
        rows = pl.ds(pl.multiple_of(d * (ref.shape[0] // 8) + r0, 16), n)
        if z is None:
            return ref.at[rows, :]
        return ref.at[rows, pl.ds(pl.multiple_of(z * (ref.shape[1] // s.nz), 128), ref.shape[1] // s.nz)]
    def block(s, i, d, half=None):
        ref = s.part(i, d, s.z if s.items[i][3] else None)
        if half is None: return ref
        n = ref.shape[0]; k = split(n)
        return ref.at[pl.ds(0, k)] if half == 0 else ref.at[pl.ds(k, n - k)]
    def rows(s, w, r0, n): return pl.ds(r0 * 3 // 2, n * 3 // 2) if w < 2 else pl.ds(r0, n)
    def shard(s, i):
        w, r0, n, _ = s.items[i]
        if w == 4: return s.sh[w]
        return s.sh[w].at[:, pl.ds(r0, n)] if w == 2 else s.sh[w].at[s.rows(w, r0, n)]
    def zslot(s, i, z):
        w, r0, n, _ = s.items[i]
        return s.zb[w].at[z, s.rows(w, r0, n)] if w < 2 else s.part(i, s.d, z)
    def zc(s, i, j, recv=False):
        other = (s.z - j + s.nz) % s.nz if recv else (s.z + j) % s.nz
        return s.cp(s.shard(i), s.zslot(i, other if recv else s.z), i, j - 1, (s.d, other))
    def start(s, i):
        if s.items[i][0] == 4:
            s.block(i, s.d)[...] = s.shard(i)[...]
            return
        s.zslot(i, s.z)[...] = s.shard(i)[...]
        if s.items[i][3]:
            s.bx(i, s.d, s.xn, 3).start()
            s.bx(i, s.d, s.yn, 4).start()
            return
        for j in range(1, s.nz):
            s.zc(i, j).start()
    def sibc(s, i, k, d):
        return s.cp(s.part(i, d), s.part(i, d), i, 7 + k, (s.sib, s.z))
    def bx(s, i, b, dev, slot, half=None):
        return s.cp(s.block(i, b, half), s.block(i, b, half), i, slot, (dev, s.z))
    def e1(s, i):
        w = s.items[i][0]
        if w < 4:
            for j in range(1, s.nz):
                s.zc(i, j, True).wait_recv()
        if w < 2:
            s.block(i, s.d)[...] = jnp.concatenate([unpack(s.zslot(i, k)[...]) for k in range(s.nz)], axis=1)
        s.bx(i, s.d, s.xn, 3).start()
        s.bx(i, s.d, s.yn, 4).start()
        s.sibc(i, 0, s.d).start()
    def e2(s, i):
        s.bx(i, s.xn, s.xn, 3).wait_recv()
        s.bx(i, s.xn, s.yn, 5, 0).start()
        if not s.items[i][3]: s.sibc(i, 1, s.xn).start()
    def e3(s, i):
        s.bx(i, s.yn, s.yn, 4).wait_recv()
        s.bx(i, s.yn, s.xn, 6, 1).start()
        if not s.items[i][3]: s.sibc(i, 2, s.yn).start()
    def e4(s, i):
        s.bx(i, s.dg, s.yn, 5, 0).wait_recv()
        s.bx(i, s.dg, s.xn, 6, 1).wait_recv()
        if not s.items[i][3]: s.sibc(i, 3, s.dg).start()
    def z1(s, i):
        for j in range(1, s.nz):
            for d in s.chips:
                s.cp(s.part(i, d, s.z), s.part(i, d, s.z), i, j - 1, (s.d, (s.z + j) % s.nz)).start()
    def zall(s, i, j):
        w, r0, n, _ = s.items[i]
        ref = s.full[w]
        ref = ref.at[pl.ds(0, ref.shape[0] // s.nz), pl.ds(0, 4 * n)] if w == 2 else ref.at[pl.ds(0, 4 * n), pl.ds(0, ref.shape[1] // s.nz)]
        return s.cp(ref, ref, i, j - 1, (s.d, (s.z + j) % s.nz))
    def z2(s, i):
        for j in range(1, s.nz): s.zall(i, j).wait_recv()
        for k, d in enumerate(s.chips): s.sibc(i, k, d).start()
    def e5(s, i, ks=(0, 1, 2, 3)):
        for k in ks:
            s.sibc(i, k, s.chips[k] + s.sib - s.d).wait_recv()
    def order(s, i):
        return (i // 2 + s.d // 4) % 2 * 2 + (i + s.d // 2) % 2
    def finish(s, i):
        if s.items[i][0] < 4:
            for j in range(1, s.nz):
                (s.zall(i, j) if s.items[i][3] else s.zc(i, j)).wait_send()
        s.bx(i, s.d, s.xn, 3).wait_send()
        s.bx(i, s.d, s.yn, 4).wait_send()
        s.bx(i, s.xn, s.yn, 5, 0).wait_send()
        s.bx(i, s.yn, s.xn, 6, 1).wait_send()
        for k, b in enumerate(s.chips):
            s.sibc(i, k, b).wait_send()


class Reduce(Comm):
    def __init__(s, hbm, far, near, v, sems):
        super().__init__()
        s.hbm = hbm; s.v = v; s.near = near
        s.pP, s.pF, s.pZ = far
        s.sems = sems
        s.chips = (s.dg, s.xn, s.yn, s.d)
        s.fr = hbm[2].shape[0] // s.nz; s.fc = hbm[2].shape[1] // 8
        s.f1 = s.pF.shape[1] // s.nz; s.f2 = s.fr - s.f1
        s.qr = hbm[0].shape[0] // 8; s.orr = hbm[1].shape[0] // 8
        s.pr = hbm[3].shape[0] // 8; s.pc = hbm[3].shape[1] // s.nz
        s.p1 = s.pZ.shape[1] // 8; s.p2 = s.pr - s.p1
        q1 = s.qr // 32 * 16 // 32 * 32
        s.qi = ((0, q1), (q1, s.qr - q1))
    def cp(s, src, dst, kind, i, dev):
        a, b = s.sems[kind]
        return pltpu.make_async_remote_copy(src_ref=src, dst_ref=dst, send_sem=a.at[i], recv_sem=b.at[i], device_id=dev, device_id_type=MESH)
    def rows(s, ref, d, n, a=0, m=None): return ref.at[pl.ds(pl.multiple_of(d * n + a, 16), n if m is None else m), :]
    def pp(s, k):
        dev = s.peers[k - 1]
        return s.cp(s.rows(s.hbm[3], dev[0], s.pr, s.p1, s.p2), s.pP.at[k - 1], "p", k - 1, dev)
    def zpart(s, z, d): return s.hbm[3].at[pl.ds(d * s.pr, s.p1), pl.ds(pl.multiple_of(z * s.pc, 128), s.pc)]
    def pz(s, j, d):
        dev = s.peers[6 + j]
        return s.cp(s.zpart(dev[1], d), s.pZ.at[j - 1, pl.ds(d * s.p1, s.p1)], "y", j - 1, dev)
    def pz_all(s, j): return s.cp(s.pZ.at[j - 1], s.pZ.at[j - 1], "y", j - 1, s.peers[6 + j])
    def start_p(s):
        for j in range(1, s.nz):
            for d in range(8): s.pz(j, d).start()
        for k in range(1, 8): s.pp(k).start()
    def fpart(s, d, z, a, n): return s.hbm[2].at[pl.ds(z * s.fr + a, n), pl.ds(pl.multiple_of(d * s.fc, 128), s.fc)]
    def pf_all(s, k): return s.cp(s.pF.at[k - 1], s.pF.at[k - 1], "f", k - 1, s.peers[k - 1])
    def start_f(s):
        for k in range(1, 8):
            dev = s.peers[k - 1]
            for z in range(s.nz):
                s.cp(s.fpart(dev[0], z, 0, s.f1), s.pF.at[k - 1, pl.ds(z * s.f1, s.f1)], "f", k - 1, dev).start()
    def s0all(s, w, i): return s.cp(s.near[w].at[i], s.near[w].at[i], "s", w * 4 + i, (s.sib, s.z))
    def start_s(s, w):
        for i in range(4):
            d = s.chips[i] + s.sib - s.d
            if w == 2:
                for z in range(s.nz):
                    s.cp(s.fpart(d, z, s.f1, s.f2), s.near[2].at[i, pl.ds(z * s.f2, s.f2)], "s", w * 4 + i, (s.sib, s.z)).start()
            else:
                s.cp(s.rows(s.hbm[w], d, s.qr if w == 0 else s.orr), s.near[w].at[i], "s", w * 4 + i, (s.sib, s.z)).start()
    def own(s, t, i):
        v = s.v
        if t < 2: return v.QT.at[pl.ds(i * s.qr + s.qi[t][0], s.qi[t][1])]
        if t == 2: return v.OT.at[pl.ds(i * s.orr, s.orr)]
        if t == 3: return v.F.at[pl.ds(s.nz * s.f1, s.nz * s.f2), pl.ds(i * s.fc, s.fc)]
        if t == 4: return v.m.at[pl.ds(pl.multiple_of(8 * s.p1 + s.chips[i] * s.p1, 16), s.p1), pl.ds(s.pc, s.pc)]
        return v.gv.at[s.chips[i]]
    def sb(s, t, i):
        v = s.v
        if t < 2: return v.QT.at[pl.ds((4 + i) * s.qr + s.qi[t][0], s.qi[t][1])]
        if t == 2: return v.OT.at[pl.ds((4 + i) * s.orr, s.orr)]
        if t == 3: return v.F.at[pl.ds(s.nz * s.f1, s.nz * s.f2), pl.ds((4 + i) * s.fc, s.fc)]
        if t == 4: return v.m.at[pl.ds((8 + i) * s.p1, s.p1), pl.ds(2 * s.pc, s.pc)]
        return v.vs.at[i]
    def land(s, t, what):
        v = s.v
        i = ("rx", "ry", "ra", "rb", "zs").index(what)
        if t == 3:
            n = s.nz * s.f2; base = s.nz * s.f1 + s.f1; k = split(n)
            a, m, c = [(0, n, 0), (0, n, 1), (0, k, 2), (k, n - k, 2), (0, n, 3)][i]
            return v.gp.at[pl.ds(base + a, m), pl.ds(c * s.fc, s.fc)]
        if t == 5:
            return [v.vs.at[4], v.vs.at[5], v.vs.at[6, pl.ds(0, 8)], v.vs.at[6, pl.ds(8, 8)], v.vs.at[7]][i]
        if t == 4: ref, base, n = v.m, 12 * s.p1, s.p1
        elif t == 2: ref, base, n = v.A, 0, s.orr
        else: ref, base, n = v.n1, t * 3 * s.qi[0][1], s.qi[t][1]
        k = split(n)
        a, m = [(0, n), (n, n), (2 * n, k), (2 * n + k, n - k)][i]
        return ref.at[pl.ds(base + a, m), pl.ds(2 * s.pc, s.pc)] if t == 4 else ref.at[pl.ds(base + a, m)]
    def half(s, ref, h):
        n = ref.shape[0]; k = split(n)
        return ref.at[pl.ds(0, k)] if h == 0 else ref.at[pl.ds(k, n - k)]
    def load_own(s, t):
        for i in range(4):
            sem = s.v.lsem.at[t * 8 + i]
            if t == 3:
                for z in range(s.nz):
                    pltpu.make_async_copy(s.fpart(s.chips[i], z, s.f1, s.f2), s.own(3, i).at[pl.ds(z * s.f2, s.f2)], sem).start()
            elif t == 2:
                pltpu.make_async_copy(s.rows(s.hbm[1], s.chips[i], s.orr), s.own(2, i), sem).start()
            else:
                pltpu.make_async_copy(s.rows(s.hbm[0], s.chips[i], s.qr, *s.qi[t]), s.own(t, i), sem).start()
    def near_of(s, t, i):
        if t < 2: return s.near[0].at[i, pl.ds(*s.qi[t])]
        return s.near[t - 1].at[i]
    def load_sib(s, t):
        for i in range(4):
            if t != 1: s.s0all(max(t - 1, 0), i).wait_recv()
            pltpu.make_async_copy(s.near_of(t, i), s.sb(t, i), s.v.lsem.at[t * 8 + 4 + i]).start()
    def slot_p(s, k): return s.v.PT.at[pl.ds(k * s.p2, s.p2)]
    def slot_f(s, k): return s.v.F.at[pl.ds(0, s.nz * s.f1), pl.ds(k * s.fc, s.fc)]
    def slot_z(s, j): return s.v.m.at[pl.ds(j // 3 * 8 * s.p1, 8 * s.p1), pl.ds(j % 3 * s.pc, s.pc)]
    def load_p(s):
        pltpu.make_async_copy(s.rows(s.hbm[3], s.d, s.pr, s.p1, s.p2), s.slot_p(0), s.v.lsem.at[32]).start()
        for k in range(1, 8):
            s.pp(k).wait_recv()
            pltpu.make_async_copy(s.pP.at[k - 1], s.slot_p(k), s.v.lsem.at[32 + k]).start()
    def load_f(s):
        for z in range(s.nz):
            pltpu.make_async_copy(s.fpart(s.d, z, 0, s.f1), s.slot_f(0).at[pl.ds(z * s.f1, s.f1)], s.v.lsem.at[40]).start()
        for k in range(1, 8):
            s.pf_all(k).wait_recv()
            pltpu.make_async_copy(s.pF.at[k - 1], s.slot_f(k), s.v.lsem.at[40 + k]).start()
    def load_z(s):
        for d in range(8):
            pltpu.make_async_copy(s.zpart(s.z, d), s.slot_z(0).at[pl.ds(d * s.p1, s.p1)], s.v.lsem.at[48]).start()
        for j in range(1, s.nz):
            s.pz_all(j).wait_recv()
            pltpu.make_async_copy(s.pZ.at[j - 1], s.slot_z(j), s.v.lsem.at[48 + j]).start()
    def loaded(s, ref, sem): pltpu.make_async_copy(ref, ref, s.v.lsem.at[sem]).wait()
    def cc(s, i): return s.cp(s.v.cs.at[0], s.v.cs.at[1 + i], "c", i, s.peers[i])
    def factors(s, c):
        s.v.cs[0] = jnp.full(s.v.cs.shape[1:], c, f32)
        for i in range(len(s.peers)): s.cc(i).start()
    def wait_factors(s):
        for i in range(len(s.peers)): s.cc(i).wait_recv()
    def c(s, i): return s.v.cs[i, 0:1, 0:1]
    def sibv(s, t, i):
        d = s.chips[i] + s.sib - s.d
        src = s.v.gv.at[d] if t == 5 else s.v.m.at[pl.ds(pl.multiple_of(8 * s.p1 + d * s.p1, 16), s.p1), pl.ds(s.pc, s.pc)]
        return s.cp(src, s.sb(t, i), "n", t * 13 + i, (s.sib, s.z))
    def start_v(s, t):
        for i in range(4): s.sibv(t, i).start()
    def sum_p(s):
        for k in range(8): s.loaded(s.slot_p(k), 32 + k)
        for q in range(s.nz):
            cols = slice(q * s.pc, (q + 1) * s.pc)
            t = sum(s.c(k) * s.v.PT[k * s.p2:(k + 1) * s.p2, cols].astype(f32) for k in range(8))
            s.v.PT[8 * s.p2:9 * s.p2, cols] = t.astype(bf16)
        s.zfirst("p")
    def zpart_of(s, t, k):
        if t == "p": return s.v.PT.at[pl.ds(8 * s.p2, s.p2), pl.ds(pl.multiple_of(k * s.pc, 128), s.pc)]
        if t == "f": return s.v.n2.at[pl.ds(pl.multiple_of(k * s.f1, 16), s.f1), pl.ds(0, s.fc)]
        return s.zpiece(t, k)
    def zland_of(s, t, j):
        if t == "p": return s.v.PT.at[pl.ds(9 * s.p2, s.p2), pl.ds(j * s.pc, s.pc)]
        if t == "f": return s.v.n2.at[pl.ds((s.nz + j // 2) * s.f1, s.f1), pl.ds(j % 2 * s.fc, s.fc)]
        return s.zland(t, j)
    def zcp(s, t, j):
        a, b = s.z + 1 - 2 * (s.z % 2), (s.z + 2) % 4
        k, to = ((a, a), (3 - s.z, a), (b, b))[j]
        kind, i = ("z", "pf".index(t) * 3 + j) if t in ("p", "f") else ("n", t * 13 + 10 + j)
        return s.cp(s.zpart_of(t, k), s.zland_of(t, j), kind, i, (s.d, to))
    def zfirst(s, t):
        s.zcp(t, 1).start(); s.zcp(t, 0).start()
    def zsecond(s, t):
        s.zcp(t, 1).wait_recv()
        ref = s.zpart_of(t, (s.z + 2) % 4)
        ref[...] = (ref[...].astype(f32) + s.zland_of(t, 1)[...].astype(f32)).astype(bf16)
        s.zcp(t, 2).start()
    def zsum(s, t):
        s.zcp(t, 0).wait_recv(); s.zcp(t, 2).wait_recv()
        return s.zpart_of(t, s.z)[...].astype(f32) + s.zland_of(t, 0)[...].astype(f32) + s.zland_of(t, 2)[...].astype(f32)
    def zsent(s, t):
        for j in range(3): s.zcp(t, j).wait_send()
    def fin_p(s): s.v.out[3][s.p1:, :] = s.zsum("p")
    def sum_f(s):
        for k in range(8): s.loaded(s.slot_f(k), 40 + k)
        for q in range(s.nz):
            rows = slice(q * s.f1, (q + 1) * s.f1)
            t = sum(s.c(k) * s.v.F[rows, k * s.fc:(k + 1) * s.fc].astype(f32) for k in range(8))
            s.v.n2[rows, 0:s.fc] = t.astype(bf16)
        s.zfirst("f")
    def fin_f(s): s.v.out[2][0:s.f1, :] = s.zsum("f")
    def sum_z(s):
        for j in range(s.nz): s.loaded(s.slot_z(j), 48 + j)
        n = s.p1
        for d in range(8):
            t = s.c(0) * s.v.m[d * n:(d + 1) * n, 0:s.pc].astype(f32)
            for j in range(1, s.nz):
                a = j // 3 * 8 * n + d * n; b = j % 3 * s.pc
                t = t + s.c(7 + j) * s.v.m[a:a + n, b:b + s.pc].astype(f32)
            s.v.m[(8 + d) * n:(9 + d) * n, s.pc:2 * s.pc] = t.astype(bf16)
        s.start_v(4)
    def mixed(s, t, i):
        if t < 4:
            s.loaded(s.own(t, i), t * 8 + i); s.loaded(s.sb(t, i), t * 8 + 4 + i)
        else:
            s.sibv(t, i).wait_recv()
        a, b = s.own(t, i)[...].astype(f32), s.sb(t, i)[...].astype(f32)
        if t == 4: return a + b
        return s.c(0) * a + s.v.cs[(s.d - s.sib + 8) % 8, 0:1, 0:1] * b
    def nc(s, src, dst, t, slot, dev): return s.cp(src, dst, "n", t * 13 + slot, (dev, s.z))
    def ca(s, t): return s.nc(s.half(s.sb(t, 0), 0), s.land(t, "ra"), t, 4, s.xn)
    def cb(s, t): return s.nc(s.half(s.sb(t, 0), 1), s.land(t, "rb"), t, 5, s.yn)
    def cx(s, t, h): return s.nc(s.half(s.sb(t, 1), h), s.half(s.land(t, "rx"), h), t, 6 + h, s.xn)
    def cy(s, t, h): return s.nc(s.half(s.sb(t, 2), h), s.half(s.land(t, "ry"), h), t, 8 + h, s.yn)
    def a(s, t):
        def put(i):
            ref = s.sb(t, i)
            ref[...] = s.mixed(t, i).astype(ref.dtype)
        put(0); s.ca(t).start(); s.cb(t).start()
        put(1); s.cx(t, 0).start()
        put(2); s.cy(t, 1).start()
    def r(s, t):
        s.ca(t).wait_recv()
        x = s.half(s.sb(t, 2), 0)
        x[...] = (x[...].astype(f32) + s.land(t, "ra")[...].astype(f32)).astype(x.dtype)
        s.cy(t, 0).start()
        s.cb(t).wait_recv()
        x = s.half(s.sb(t, 1), 1)
        x[...] = (x[...].astype(f32) + s.land(t, "rb")[...].astype(f32)).astype(x.dtype)
        s.cx(t, 1).start()
    def packed(s, t):
        r0, n = s.qi[t] if t < 2 else (0, s.orr)
        return pl.ds(r0 * 3 // 2, n * 3 // 2)
    def zpiece(s, t, k):
        if t < 3: return (s.v.zq, s.v.zq, s.v.zo)[t].at[k, s.packed(t)]
        ref = s.land(t, "zs")
        return ref if t == 5 else ref.at[pl.ds(pl.multiple_of(k * s.f2, 16), s.f2)]
    def zland(s, t, j):
        if t < 3: return (s.v.zrq, s.v.zrq, s.v.zro)[t].at[j, s.packed(t)]
        if t == 5: return s.v.vs.at[8 + j]
        return s.v.gp.at[pl.ds(s.nz * s.f1 + s.f1 + j * s.f2, s.f2), pl.ds(4 * s.fc, s.fc)]
    def zc(s, t, j):
        dev = s.peers[6 + j]
        return s.cp(s.zpiece(t, dev[1]), s.zland(t, j - 1), "n", t * 13 + 9 + j, dev)
    def f(s, t):
        x = s.mixed(t, 3)
        for h in (0, 1):
            s.cx(t, h).wait_recv(); s.cy(t, h).wait_recv()
        x = x + s.land(t, "rx")[...].astype(f32) + s.land(t, "ry")[...].astype(f32)
        if t == 4:
            s.v.out[3][0:s.p1, :] = x
            return
        if t < 3:
            c = x.shape[1] // s.nz
            for k in range(s.nz): s.zpiece(t, k)[...] = pack(x[:, k * c:(k + 1) * c].astype(bf16))
        else:
            ref = s.land(t, "zs")
            ref[...] = x.astype(ref.dtype)
        if t == 5:
            for j in range(1, s.nz): s.zc(t, j).start()
        else:
            s.zfirst(t)
    def fin(s, t):
        if t == 5:
            for j in range(1, s.nz): s.zc(t, j).wait_recv()
            x = s.zpiece(t, s.z)[...]
            for j in range(s.nz - 1): x = x + s.zland(t, j)[...]
            s.v.out[4][...] = x
            return
        x = s.zsum(t)
        if t == 3: s.v.out[2][s.f1:, :] = x
        elif t == 2: s.v.out[1][...] = unpack(x)
        else: s.v.out[0][s.qi[t][0]:s.qi[t][0] + s.qi[t][1], :] = unpack(x)
    def finish(s):
        for k in range(1, 8): s.pp(k).wait_send(); s.pf_all(k).wait_send()
        for j in range(1, s.nz): s.pz_all(j).wait_send()
        for w in range(3):
            for i in range(4): s.s0all(w, i).wait_send()
        for i in range(len(s.peers)): s.cc(i).wait_send()
        for t in range(6):
            if t > 3:
                for i in range(4): s.sibv(t, i).wait_send()
            s.ca(t).wait_send(); s.cb(t).wait_send()
            for h in (0, 1): s.cx(t, h).wait_send(); s.cy(t, h).wait_send()
            if t == 5:
                for j in range(1, s.nz): s.zc(t, j).wait_send()
            elif t != 4: s.zsent(t)
        s.zsent("p"); s.zsent("f")


def block_kernel(names, remote, length, tok, cot, *refs):
    refs = list(refs)
    take = lambda n: [refs.pop(0) for _ in range(n)]
    if remote:
        clip, *raw = take(7)
        y, gx, ratio, *outs = take(8)
        gq, go, gf, gp, sQ, sO, sF, pP, pF, pZ = take(10)
        QT, OT, F, PT, V, sq, so, sf, sp, sv, zq, zo, send, recv = take(14)
        gv, vs, cs, zrq, zro, lsem, *rsem = take(20)
    else:
        QT, OT, F, PT, vec, bf = take(6)
        y, gx, gq, go, gf, gp, col, dbf, ss = take(9)
        V = None
    s = Block(length=length[0], QT=QT, OT=OT, F=F, PT=PT, V=V, **dict(zip(names, refs)))
    D = s.x.shape[1]; FF = s.u.shape[1]
    cx = pltpu.make_async_copy(tok, s.x, s.isem.at[0]); cx.start()
    ce = pltpu.make_async_copy(cot, s.ey, s.isem.at[1]); ce.start()
    if remote:
        places = types.SimpleNamespace(QT=QT, OT=OT, F=F, PT=PT, m=s.m, gp=s.gp, n1=s.n1, n2=s.n2, A=s.A, gv=gv, vs=vs, cs=cs, zq=zq, zo=zo, zrq=zrq, zro=zro, lsem=lsem, out=outs)
        red = Reduce((gq, go, gf, gp), (pP, pF, pZ), (sQ, sO, sF), places, {k: (rsem[2 * i], rsem[2 * i + 1]) for i, k in enumerate("pfysczn")})
        greet(g_peers := Comm().peers)
        qn = raw[0].shape[1]
        cuts = [0, 64, 128, 192, qn]
        fc = F.shape[1] // 8; pr = sp.shape[0]
        p0 = pr // 48 * 32
        items = [(4, 0, 16, False)] + [(0, a, b - a, False) for a, b in zip(cuts, cuts[1:])] + [(1, 0, raw[1].shape[1], False),
            (2, 0, fc, False), (3, 0, p0, False), (3, p0, pr - p0, True)]
        g = Gather(items, (sq, so, sf, sp, sv), (zq, zo), (QT, OT, F, PT, V), send, recv)
        q = raw[0][...].astype(bf16).T
        for a, b in zip(cuts, cuts[1:]): sq[a * 3 // 2:b * 3 // 2, :] = pack(q[a:b])
        so[...] = pack(raw[1][...].astype(bf16).T)
        sf[...] = raw[2][...].astype(bf16)
        sp[...] = raw[3][...].astype(bf16)
        sv[...] = jnp.zeros_like(sv)
        sv[0:8, 0:raw[5].shape[1]] = raw[5][...]
        nb = raw[4].shape[0] // 128
        for j in range(nb): sv[8 + j:9 + j, :] = raw[4][j * 128:(j + 1) * 128].reshape(1, 128)
        pl.semaphore_wait(pltpu.get_barrier_semaphore(), len(g_peers))
        v, q1, q2, q3, q4, o, f, p, p2 = range(9)
        qs = (q1, q2, q3, q4)
        for i in qs + (o, v, p2): g.start(i)
        g.e1(v); g.e2(v); g.e3(v); g.e2(p2); g.e3(p2); g.e4(v); g.e1(q1); g.e5(v); s.unpack(); cx.wait(); s.ln1(); ce.wait(); s.ey_mask(); s.turn(s.ey, 0)
        g.e1(q2); g.start(f); g.e2(q1); g.e3(q1); g.e1(q3); g.e2(q2); g.e3(q2); g.e4(q1); g.e1(q4); g.e2(q3); g.e3(q3); g.e4(q2)
        g.e1(o); g.start(p); g.e2(q4); g.e3(q4); g.e4(q3); g.e4(p2); g.z1(p2); g.e4(q4)
        for i in qs: g.e5(i)
        s.qkv({2: lambda: (g.e2(o), g.e3(o))})
        g.e1(f)
        loop(D // 128, s.attend, {1: lambda: g.e4(o), 3: lambda: g.e1(p)})
        g.e5(o); g.e2(f); g.e3(f)
        s.out(); s.ln2(); g.e5(f, (0, 1, 2))
        s.fc({6: lambda: (g.e2(p), g.e3(p)), 9: lambda: (g.e4(f), g.e5(f, (3,)))}, g.order)
    else:
        s.vec[...] = vec[...]; s.bf[...] = bf[...]
        s.clear(); cx.wait()
        s.ln1(); ce.wait(); s.ey_mask(); s.turn(s.ey, 0); s.qkv()
        loop(D // 128, s.attend)
        s.out(); s.ln2(); s.fc()
    s.wgrad(s.ey, s.u, gp, FF, 512, {3: lambda: g.e4(p), 5: lambda: g.z2(p2)} if remote else {}, True)
    if remote: red.start_p(); g.e5(p); g.e5(p2)
    s.ef_y(); s.wgrad(s.n2, s.gp, gf, FF, 512)
    cy = pltpu.make_async_copy(s.er, y, s.isem.at[2]); cy.start()
    if remote: red.start_f(); red.start_s(2)
    s.gn2()
    cy.wait()
    s.ln2b(); s.wgrad(s.er, s.A, go, D, 256)
    if remote: red.start_s(1)
    s.eA()
    loop(D // 128, s.attend_back)
    cx = pltpu.make_async_copy(tok, s.A, s.isem.at[0]); cx.start()
    s.wgrad(s.u, s.n1, gq, D, 256)
    if remote:
        for i in range(len(items)): g.finish(i)
        red.start_s(0); red.load_own(2); red.load_own(3); red.load_p()
    s.bias_cols(); s.gn1()
    if remote: red.load_own(0); red.load_own(1); red.load_z()
    cx.wait(); s.ln1b()
    cg = pltpu.make_async_copy(s.er, gx, s.isem.at[3]); cg.start()
    norm2 = s.norm()
    if not remote:
        ss[0] = norm2
        cg.wait()
        col[...] = s.col[...]; dbf[...] = s.dbf[...]
        return
    norm = jnp.sqrt(jnp.full((8, 128), norm2, f32))
    ratio[...] = norm / clip[0]
    red.factors(jnp.minimum(1.0, clip[0] / norm))
    w = D // 8
    for d in range(8):
        gv[d, 0:8, 0:w] = s.col[:, d * w:(d + 1) * w]
        gv[d, 0:8, w:128] = jnp.zeros((8, 128 - w), f32)
        for j in range(8):
            k = d * nb + j
            gv[d, 8 + j:9 + j, :] = s.dbf[:, k * 128:(k + 1) * 128] if j < nb else jnp.zeros((1, 128), f32)
    q1, q2, o, f, h, v = range(6)
    for t in (q1, q2, o, f): red.load_sib(t)
    red.load_f()
    red.wait_factors()
    red.start_v(v)
    red.a(q1); red.a(q2); red.sum_p(); red.r(q1); red.a(f); red.sum_f(); red.a(v); red.r(q2); red.f(q1); red.zsecond("p"); red.sum_z(); red.a(o); red.r(v)
    red.r(f); red.zsecond("f"); red.f(q2); red.zsecond(q1); red.a(h); red.r(o); red.f(v); red.f(f); red.zsecond(q2); red.r(h); red.fin_p(); red.fin_f()
    red.f(o); red.zsecond(f); red.fin(q1); red.f(h); red.zsecond(o); red.fin(q2); red.fin(v); red.fin(f); red.fin(o)
    red.finish()
    cg.wait()


def run_block(remote, length, tok, cot, *ws):
    L, D = tok.shape
    sd = jax.ShapeDtypeStruct
    dma = pltpu.SemaphoreType.DMA
    V = pltpu.VMEM
    vm = pl.BlockSpec(memory_space=pltpu.VMEM); an = pl.BlockSpec(memory_space=pl.ANY); sm = pl.BlockSpec(memory_space=pltpu.SMEM)
    extra = []
    if remote:
        nz = lax.axis_size("fsdp")
        clip, q, o, f, p, b, v = ws
        FF = f.shape[1] * 8
        qt, ot, pt = q.shape[::-1], o.shape[::-1], p.shape
        qp, op = (qt[0] * 3 // 2, 128), (ot[0] * 3 // 2, 128)
        fr = D // nz; f1 = fr // 96 * 80; fc = FF // 8; pr = D // 8; p1 = pr // 32 * 16; pc = FF // nz
        extra = [V((3 * D, D), bf16), V((D, D), bf16), V((D, FF), bf16), V((D, FF), bf16), V((8, 16, 128), f32),
            V(qp, bf16), V(op, bf16), V(f.shape, bf16), V(pt, bf16), V((16, 128), f32),
            V((nz,) + qp, bf16), V((nz,) + op, bf16), dma((9, 11)), dma((9, 11)),
            V((8, 16, 128), f32), V((12, 16, 128), f32), V((8 + nz - 1, 8, 128), f32), V((nz - 1,) + qp, bf16), V((nz - 1,) + op, bf16), dma((52,))]
        for n in (7, 7, 3, 12, 10, 6, 78): extra += [dma((n,)), dma((n,))]
        outs = [sd((8, 128), f32), sd(qt, f32), sd(ot, f32), sd(f.shape, f32), sd(pt, f32), sd((16, 128), f32)]
        hbm = [sd((4, 3 * D // 8, D), bf16), sd((4, pr, D), bf16), sd((4, nz * (fr - f1), fc), bf16),
            sd((7, pr - p1, FF), bf16), sd((7, nz * f1, fc), bf16), sd((nz - 1, 8 * p1, pc), bf16)]
        ins = [sm] + [vm] * 6
    else:
        FF = ws[2].shape[1]
        ins = [vm] * len(ws)
    acts = [sd((L, D), bf16), sd((L, D), bf16)]
    grads = [sd((3 * D, D), bf16), sd((D, D), bf16), sd((D, FF), bf16), sd((D, FF), bf16)]
    scr = scratch(L, D, FF)
    params = dict(collective_id=0, has_side_effects=True) if remote else {}
    if remote:
        shapes = acts + outs + grads + hbm
        specs = [an] * 2 + [vm] * 6 + [an] * 10
    else:
        shapes = acts + grads + [sd((8, D), f32), sd((1, FF), f32), sd((1,), f32)]
        specs = [an] * 6 + [vm, vm, sm]
    return pl.pallas_call(functools.partial(block_kernel, list(scr), remote), out_shape=shapes,
        in_specs=[sm, an, an] + ins, out_specs=specs, scratch_shapes=extra + list(scr.values()),
        compiler_params=pltpu.CompilerParams(vmem_limit_bytes=VLIM, **params))(length, tok, cot, *ws)


VLIM = (63 << 20) + (900 << 10)


def last_kernel(examples, ratio, sq, so, sf, sp, sv, nq, no, nf, np_, nb, nv, oratio, oq, oo, of, op, ob, ov):
    oratio[0] = jnp.sum(ratio[0:1, 0:1])
    e = 1.0 / examples
    oq[...] = sq[...].T * e + nq[...]
    oo[...] = so[...].T * e + no[...]
    of[...] = sf[...] * e + nf[...]
    op[...] = sp[...] * e + np_[...]
    for j in range(ob.shape[0] // 128):
        ob[j * 128:(j + 1) * 128] = sv[8 + j:9 + j, :].reshape(128) * e + nb[j * 128:(j + 1) * 128]
    ov[...] = sv[0:8, 0:ov.shape[1]] * e + nv[...]


def shards(tokens, qkv_weight, out_weight, fc_weight, proj_weight, fc_bias, vectors, cotangent, lengths, clip_norm,
           noise_qkv, noise_out, noise_fc, noise_proj, noise_fc_bias, noise_vectors):
    ndp, nz = lax.axis_size("dp"), lax.axis_size("fsdp")
    examples = ndp * nz
    noises = (noise_qkv, noise_out, noise_fc, noise_proj, noise_fc_bias, noise_vectors)
    if ndp == 8:
        y, gx, ratio, sq, so, sf, sp, sv, *_ = run_block(True, lengths, tokens, cotangent, clip_norm.reshape(1), qkv_weight, out_weight, fc_weight, proj_weight.T, fc_bias, vectors)
        sd = jax.ShapeDtypeStruct
        vm = pl.BlockSpec(memory_space=pltpu.VMEM); sm = pl.BlockSpec(memory_space=pltpu.SMEM)
        pt = proj_weight.shape[::-1]
        ratio, gq, go, gf, gp, gb, gv = pl.pallas_call(functools.partial(last_kernel, examples),
            out_shape=[sd((1,), f32), sd(qkv_weight.shape, f32), sd(out_weight.shape, f32), sd(fc_weight.shape, f32), sd(pt, f32), sd(fc_bias.shape, f32), sd(vectors.shape, f32)],
            in_specs=[vm] * 12, out_specs=[sm] + [vm] * 6)(
            ratio, sq, so, sf, sp, sv, noise_qkv, noise_out, noise_fc, noise_proj.T, noise_fc_bias, noise_vectors)
        return y, gx, ratio, gq, go, gf, gp.T, gb, gv
    g = lambda a: lax.all_gather(lax.all_gather(a.astype(bf16), "dp", axis=1, tiled=True), "fsdp", axis=0, tiled=True)
    vec = lax.all_gather(vectors.astype(bf16), "dp", axis=1, tiled=True).astype(f32)
    bf = lax.all_gather(fc_bias.astype(bf16), "dp", axis=0, tiled=True).astype(f32).reshape(1, -1)
    y, gx, gq, go, gf, gp, col, dbf, ss = run_block(False, lengths, tokens, cotangent, g(qkv_weight).T, g(out_weight).T, g(fc_weight), g(proj_weight).T, vec, bf)
    norm = jnp.sqrt(ss)
    factor = jnp.minimum(1.0, clip_norm / norm)
    ps = lambda a, dim: lax.psum_scatter(factor * a.astype(f32), "dp", scatter_dimension=dim, tiled=True)
    pz = lambda a: lax.psum_scatter(a.astype(bf16), "fsdp", scatter_dimension=0, tiled=True).astype(f32)
    finals = tuple(pz(ps(a, 1)) for a in (gq.T, go.T, gf, gp.T)) + lax.psum((ps(dbf[0], 0), ps(col, 1)), "fsdp")
    return (y, gx, norm / clip_norm) + tuple(a / examples + n for a, n in zip(finals, noises))


def solution(mesh):
    both, cut = P(("dp", "fsdp"), None), P("fsdp", "dp")
    weights = (cut, cut, cut, cut, P("dp"), P(None, "dp"))
    return jax.shard_map(shards, mesh=mesh, in_specs=(both,) + weights + (both, P(("dp", "fsdp")), P()) + weights,
        out_specs=(both, both, P(("dp", "fsdp"))) + weights, check_vma=False)
```

```python
import functools
import types
import jax
import jax.numpy as jnp
from jax import lax
from jax.experimental import pallas as pl
from jax.experimental.pallas import tpu as pltpu
from jax.sharding import PartitionSpec as P

MESH = pl.DeviceIdType.MESH
f32 = jnp.float32
bf16 = jnp.bfloat16
HD=64; T=256; QB=256; C=768
EPS=1e-05
GC=0.7978845608028654
GA=0.044715

def nn(a, b): return lax.dot_general(a, b, (((1,), (0,)), ((), ())), preferred_element_type=f32)
def nt(a, b): return lax.dot_general(a, b, (((1,), (1,)), ((), ())), preferred_element_type=f32)
def at(i, n): return pl.ds(pl.multiple_of(i * n, n), n)
def loop(n, body, hooks={}):
    def step(i, c):
        for k, fn in hooks.items():
            @pl.when(i == k)
            def _(): fn()
        body(i)
        return c
    lax.fori_loop(0, n, step, 0)

class Block:
    def __init__(s, **refs):
        s.__dict__.update(refs)
        s.x = s.er
    def unpack(s):
        V = s.V
        n = V.shape[0]; w = s.x.shape[1] // n; k = s.bf.shape[1] // n // 128
        s.vec[...] = jnp.concatenate([V[d][0:8, 0:w] for d in range(n)], axis=1).astype(bf16).astype(f32)
        s.bf[...] = jnp.concatenate([V[d][8 + j:9 + j, :] for d in range(n) for j in range(k)], axis=1).astype(bf16).astype(f32)
        s.clear()
    def clear(s):
        s.col[...] = jnp.zeros_like(s.col); s.ssq[...] = jnp.zeros_like(s.ssq)
    def row(s, i): return s.vec[i:i + 1, :]
    def ln1(s):
        def body(i):
            x = s.x[at(i, T), :].astype(f32)
            c = x - jnp.mean(x, axis=1, keepdims=True)
            v = jnp.mean(c * c, axis=1, keepdims=True)
            s.n1[at(i, T), :] = (c * lax.rsqrt(v + EPS) * s.row(0) + s.row(1)).astype(bf16)
        loop(s.x.shape[0] // T, body)
    def qkv(s, hooks={}):
        D = s.n1.shape[1]
        for part, b in ((0, 2), (1, None), (2, 3)):
            if part in hooks: hooks[part]()
            o = nt(s.n1[...], s.QT[part * D:(part + 1) * D, :])
            if b is not None: o = o + s.row(b)
            s.m[:, part * D:(part + 1) * D] = o.astype(bf16)
    def heads(s, hp):
        D = s.x.shape[1]
        q = s.m[:, at(hp, 128)] * bf16(HD ** -0.5)
        k = s.m[:, pl.ds(pl.multiple_of(D + hp * 128, 128), 128)]
        v = s.m[:, pl.ds(pl.multiple_of(2 * D + hp * 128, 128), 128)]
        return q, k, v
    def masked(s, q, k, h):
        lane = lax.broadcasted_iota(jnp.int32, q.shape, 1)
        mine = (lane // HD) == h
        free = lane == (1 - h) * HD
        zero = jnp.zeros_like(q)
        bias = jnp.where(lax.broadcasted_iota(jnp.int32, q.shape, 0) < s.length, 0.0, -1e30).astype(bf16)
        return jnp.where(mine, q, jnp.where(free, jnp.ones_like(q), zero)), jnp.where(mine, k, jnp.where(free, bias, zero))
    def scores(s, kh, qh, b):
        n = (b + 1) * QB
        o = nt(kh[:n], qh[n - QB:n])
        r = lax.broadcasted_iota(jnp.int32, (QB, QB), 0); c = lax.broadcasted_iota(jnp.int32, (QB, QB), 1)
        d = jnp.where(r <= c, o[n - QB:], -1e30)
        return jnp.concatenate([o[:n - QB], d], axis=0) if b else d
    def attend(s, hp):
        L = s.x.shape[0]; nb = L // QB
        q, k, v = s.heads(hp)
        vt = v.T
        ones = jnp.ones((16, L), bf16)
        qk = [s.masked(q, k, h) for h in (0, 1)]
        ve = [jnp.concatenate([vt[h * HD:(h + 1) * HD], ones], axis=0) for h in (0, 1)]
        units = [(h, b) for h in (0, 1) for b in range(nb)]
        S = {}
        def first(u):
            h, b = units[u]
            o = s.scores(qk[h][1], qk[h][0], b)
            S[u] = o, jnp.max(o, axis=0, keepdims=True)
        first(0)
        for u, (h, b) in enumerate(units):
            if u + 1 < len(units): first(u + 1)
            p, mx = S.pop(u)
            o = nn(ve[h][:, :(b + 1) * QB], jnp.exp(p - mx).astype(bf16))
            l = o[HD:HD + 1]
            s.lse[hp, h:h + 1, b * QB:(b + 1) * QB] = mx + jnp.log(l)
            s.ot[h * HD:(h + 1) * HD, b * QB:(b + 1) * QB] = o[:HD] / l
        s.A[:, at(hp, 128)] = s.ot[...].T.astype(bf16)
    def out(s):
        s.r[...] = s.x[...].astype(f32) + nt(s.A[...], s.OT[...]) + s.row(4)
    def ln2(s):
        def body(i):
            x = s.r[at(i, T), :]
            c = x - jnp.mean(x, axis=1, keepdims=True)
            v = jnp.mean(c * c, axis=1, keepdims=True)
            s.n2[at(i, T), :] = (c * lax.rsqrt(v + EPS) * s.row(5) + s.row(6)).astype(bf16)
        loop(s.x.shape[0] // T, body)
    def fc(s, hooks={}, order=lambda i: i):
        n = s.u.shape[1] // 4 // T
        def body(i):
            c = at(order(i // n) * n + i % n, T)
            f = nn(s.n2[...], s.F[:, c]) + s.bf[:, c]
            f2 = f * f
            t = jnp.tanh(f * (GC + GC * GA * f2))
            p = 0.5 * t + 0.5
            u = f * p
            s.u[:, c] = u.astype(bf16)
            s.gp[:, c] = (p + u * (1.0 - p) * (2 * GC + 6 * GC * GA * f2)).astype(bf16)
        loop(4 * n, body, hooks)
    def ey_mask(s):
        def body(i):
            rp = i * T + lax.broadcasted_iota(jnp.int32, (T, s.x.shape[1]), 0)
            e = jnp.where(rp < s.length, s.ey[at(i, T), :].astype(f32), 0.0)
            s.ey[at(i, T), :] = e.astype(bf16)
            s.col[7:8, :] += jnp.sum(e, axis=0, keepdims=True)
        loop(s.x.shape[0] // T, body)
    def turn(s, lhs, c):
        R = s.lt.shape[0]
        def tr(i): s.lt[at(i, T), :] = lhs[:, pl.ds(pl.multiple_of(c * R + i * T, T), T)].T
        loop(R // T, tr)
    def wgrad(s, lhs, rhs, out, cols, nw, hooks={}, turned=False):
        n = cols // nw; R = s.lt.shape[0]; m = out.shape[0] // R
        def cp(t):
            slot = t % 2
            return pltpu.make_async_copy(s.stage.at[slot, :, pl.ds(0, nw)], out.at[at(t // n, R), at(t % n, nw)], s.dsem.at[slot])
        for c in range(m):
            if not turned: s.turn(lhs, c)
            def inner(j):
                t = c * n + j
                o = nn(s.lt[...], rhs[:, at(j, nw)])
                @pl.when(t >= 2)
                def _(): cp(t - 2).wait()
                s.ssq[:, 0:nw] += jnp.sum(o * o, axis=0, keepdims=True)
                s.stage[t % 2, :, 0:nw] = o.astype(bf16)
                cp(t).start()
            loop(n, inner, hooks)
        cp(m * n - 2).wait(); cp(m * n - 1).wait()
    def y(s):
        s.er[...] = (s.r[...] + nt(s.u[...], s.PT[...]) + s.row(7)).astype(bf16)
    def ef(s):
        def body(i):
            e = (nn(s.ey[...], s.PT[:, at(i, C)]) * s.gp[:, at(i, C)].astype(f32)).astype(bf16)
            s.gp[:, at(i, C)] = e
            s.dbf[:, at(i, C)] = jnp.sum(e.astype(f32), axis=0, keepdims=True)
        loop(s.u.shape[1] // C, body)
    def ef_y(s):
        s.ef(); s.y()
    def gn2(s):
        s.G[...] = nt(s.gp[...], s.F[...])
    def lnb(s, x, gn, gain):
        c = x - jnp.mean(x, axis=1, keepdims=True)
        v = jnp.mean(c * c, axis=1, keepdims=True)
        rs = lax.rsqrt(v + EPS)
        h = c * rs
        a = gn * gain
        return h, rs * (a - jnp.mean(a, axis=1, keepdims=True) - h * jnp.mean(a * h, axis=1, keepdims=True))
    def ln2b(s):
        def body(i):
            gn = s.G[at(i, T), :]
            h, g = s.lnb(s.r[at(i, T), :], gn, s.row(5))
            s.col[5:6, :] += jnp.sum(gn * h, axis=0, keepdims=True)
            s.col[6:7, :] += jnp.sum(gn, axis=0, keepdims=True)
            g = g + s.ey[at(i, T), :].astype(f32)
            s.r[at(i, T), :] = g
            e = g.astype(bf16)
            s.er[at(i, T), :] = e
            s.col[4:5, :] += jnp.sum(e.astype(f32), axis=0, keepdims=True)
        loop(s.x.shape[0] // T, body)
    def eA(s):
        s.n2[...] = nn(s.er[...], s.OT[...]).astype(bf16)
    def attend_back(s, hp):
        L, D = s.x.shape; nb = L // QB
        q, k, v = s.heads(hp)
        e = s.n2[:, at(hp, 128)]
        kt = k.T
        ea = (e.astype(f32) * s.A[:, at(hp, 128)].astype(f32)).T
        lane = lax.broadcasted_iota(jnp.int32, e.shape, 1)
        s.dk[...] = jnp.zeros_like(s.dk); s.dv[...] = jnp.zeros_like(s.dv)
        heads = []
        for h in (0, 1):
            mine = (lane // HD) == h
            zero = jnp.zeros_like(e)
            heads.append((*s.masked(q, k, h), jnp.where(mine, e, zero), jnp.where(mine, q, zero), jnp.sum(ea[h * HD:(h + 1) * HD, :], axis=0, keepdims=True)))
        units = [(h, b) for h in (0, 1) for b in range(nb)]
        st = {}
        def one(u):
            h, b = units[u]; qh, kh, eh, qz, delta = heads[h]
            st[u] = s.scores(kh, qh, b), nt(v[:(b + 1) * QB], eh[b * QB:(b + 1) * QB])
        def two(u):
            h, b = units[u]; S, dP = st[u]
            cols = slice(b * QB, (b + 1) * QB)
            p = jnp.exp(S - s.lse[hp, h:h + 1, cols])
            st[u] = p.astype(bf16), (p * (dP - heads[h][4][:, cols])).astype(bf16)
        def three(u):
            h, b = units[u]; qh, kh, eh, qz, delta = heads[h]; p, ds = st.pop(u)
            rows = slice(0, (b + 1) * QB); cols = slice(b * QB, (b + 1) * QB)
            s.dv[rows] += nn(p, eh[cols]); s.dk[rows] += nn(ds, qz[cols])
            s.ot[h * HD:(h + 1) * HD, cols] = nn(kt[h * HD:(h + 1) * HD, rows], ds) * (HD ** -0.5)
        n = len(units)
        for u in range(-1, n + 1):
            if u + 1 < n: one(u + 1)
            if 0 <= u < n: two(u)
            if u >= 1: three(u - 1)
        s.u[:, at(hp, 128)] = s.ot[...].T.astype(bf16)
        s.u[:, pl.ds(pl.multiple_of(D + hp * 128, 128), 128)] = s.dk[...].astype(bf16)
        s.u[:, pl.ds(pl.multiple_of(2 * D + hp * 128, 128), 128)] = s.dv[...].astype(bf16)
    def bias_cols(s):
        D = s.x.shape[1]
        def body(i):
            s.col[2:3, :] += jnp.sum(s.u[at(i, T), 0:D].astype(f32), axis=0, keepdims=True)
            s.col[3:4, :] += jnp.sum(s.u[at(i, T), 2 * D:3 * D].astype(f32), axis=0, keepdims=True)
        loop(s.x.shape[0] // T, body)
    def gn1(s):
        s.G[...] = nn(s.u[:, 0:s.QT.shape[0]], s.QT[...])
    def ln1b(s):
        def body(i):
            gn = s.G[at(i, T), :]
            h, g = s.lnb(s.A[at(i, T), :].astype(f32), gn, s.row(0))
            s.col[0:1, :] += jnp.sum(gn * h, axis=0, keepdims=True)
            s.col[1:2, :] += jnp.sum(gn, axis=0, keepdims=True)
            s.er[at(i, T), :] = (s.r[at(i, T), :] + g).astype(bf16)
        loop(s.x.shape[0] // T, body)
    def norm(s):
        t = jnp.sum(s.ssq[...]) + jnp.sum(s.dbf[...] * s.dbf[...]) + jnp.sum(s.col[...] * s.col[...])
        return t

def scratch(L, D, FF, rows=None):
    return dict(
        vec=pltpu.VMEM((8, D), f32), bf=pltpu.VMEM((1, FF), f32), col=pltpu.VMEM((8, D), f32), dbf=pltpu.VMEM((1, FF), f32),
        ssq=pltpu.VMEM((1, 512), f32),
        n1=pltpu.VMEM((L, D), bf16), m=pltpu.VMEM((L, 3 * D), bf16), A=pltpu.VMEM((L, D), bf16), r=pltpu.VMEM((L, D), f32),
        n2=pltpu.VMEM((L, D), bf16), u=pltpu.VMEM((L, FF), bf16), gp=pltpu.VMEM((L, FF), bf16), er=pltpu.VMEM((L, D), bf16),
        G=pltpu.VMEM((L, D), f32), stage=pltpu.VMEM((2, D, 512), bf16), lt=pltpu.VMEM((D, L), bf16),
        lse=pltpu.VMEM((D // 128, 2, L), f32), ot=pltpu.VMEM((128, L), f32), dk=pltpu.VMEM((L, 128), f32), dv=pltpu.VMEM((L, 128), f32),
        ey=pltpu.VMEM((L, D), bf16),
        dsem=pltpu.SemaphoreType.DMA((2,)), isem=pltpu.SemaphoreType.DMA((4,)))


def place():
    d = lax.axis_index("dp"); z = lax.axis_index("fsdp")
    core = d % 2; xx = (d // 2) % 2; yy = d // 4
    return d, z, d + 1 - 2 * core, d + 2 - 4 * xx, d + 4 - 8 * yy


def greet(partners):
    for dev in partners:
        pl.semaphore_signal(pltpu.get_barrier_semaphore(), inc=1, device_id=dev, device_id_type=MESH)


def split(n):
    return n // 32 * 16 if n >= 32 else n // 2


def pack(x):
    n = x.shape[0]
    return jnp.concatenate([x[:, :128], jnp.concatenate([x[:n // 2, 128:], x[n // 2:, 128:]], axis=1)], axis=0)


def unpack(x):
    n = x.shape[0] * 2 // 3
    return jnp.concatenate([x[:n], jnp.concatenate([x[n:, :64], x[n:, 64:]], axis=0)], axis=1)


class Comm:
    def __init__(s):
        s.d, s.z, s.sib, s.xn, s.yn = place()
        s.dg = s.xn + s.yn - s.d
        s.nz = lax.axis_size("fsdp")
        s.peers = [((s.d + k) % 8, s.z) for k in range(1, 8)] + [(s.d, (s.z + j) % s.nz) for j in range(1, s.nz)]


class Gather(Comm):
    def __init__(s, items, shards, zb, full, send, recv):
        super().__init__()
        s.items = items; s.sh = shards; s.zb = zb; s.full = full; s.send = send; s.recv = recv
        s.chips = (s.d, s.xn, s.yn, s.dg)
    def cp(s, src, dst, i, slot, dev):
        return pltpu.make_async_remote_copy(src_ref=src, dst_ref=dst, send_sem=s.send.at[i, slot], recv_sem=s.recv.at[i, slot], device_id=dev, device_id_type=MESH)
    def part(s, i, d, z=None):
        w, r0, n, _ = s.items[i]
        ref = s.full[w]
        if w == 4:
            return ref.at[d, pl.ds(r0, n)]
        if w == 2:
            rows = pl.ds(0, ref.shape[0]) if z is None else pl.ds(pl.multiple_of(z * (ref.shape[0] // s.nz), 16), ref.shape[0] // s.nz)
            return ref.at[rows, pl.ds(pl.multiple_of(d * (ref.shape[1] // 8) + r0, 128), n)]
        rows = pl.ds(pl.multiple_of(d * (ref.shape[0] // 8) + r0, 16), n)
        if z is None:
            return ref.at[rows, :]
        return ref.at[rows, pl.ds(pl.multiple_of(z * (ref.shape[1] // s.nz), 128), ref.shape[1] // s.nz)]
    def block(s, i, d, half=None):
        ref = s.part(i, d, s.z if s.items[i][3] else None)
        if half is None: return ref
        n = ref.shape[0]; k = split(n)
        return ref.at[pl.ds(0, k)] if half == 0 else ref.at[pl.ds(k, n - k)]
    def rows(s, w, r0, n): return pl.ds(r0 * 3 // 2, n * 3 // 2) if w < 2 else pl.ds(r0, n)
    def shard(s, i):
        w, r0, n, _ = s.items[i]
        if w == 4: return s.sh[w]
        return s.sh[w].at[:, pl.ds(r0, n)] if w == 2 else s.sh[w].at[s.rows(w, r0, n)]
    def zslot(s, i, z):
        w, r0, n, _ = s.items[i]
        return s.zb[w].at[z, s.rows(w, r0, n)] if w < 2 else s.part(i, s.d, z)
    def zc(s, i, j, recv=False):
        other = (s.z - j + s.nz) % s.nz if recv else (s.z + j) % s.nz
        return s.cp(s.shard(i), s.zslot(i, other if recv else s.z), i, j - 1, (s.d, other))
    def start(s, i):
        if s.items[i][0] == 4:
            s.block(i, s.d)[...] = s.shard(i)[...]
            return
        s.zslot(i, s.z)[...] = s.shard(i)[...]
        if s.items[i][3]:
            s.bx(i, s.d, s.xn, 3).start()
            s.bx(i, s.d, s.yn, 4).start()
            return
        for j in range(1, s.nz):
            s.zc(i, j).start()
    def sibc(s, i, k, d):
        return s.cp(s.part(i, d), s.part(i, d), i, 7 + k, (s.sib, s.z))
    def bx(s, i, b, dev, slot, half=None):
        return s.cp(s.block(i, b, half), s.block(i, b, half), i, slot, (dev, s.z))
    def e1(s, i):
        w = s.items[i][0]
        if w < 4:
            for j in range(1, s.nz):
                s.zc(i, j, True).wait_recv()
        if w < 2:
            s.block(i, s.d)[...] = jnp.concatenate([unpack(s.zslot(i, k)[...]) for k in range(s.nz)], axis=1)
        s.bx(i, s.d, s.xn, 3).start()
        s.bx(i, s.d, s.yn, 4).start()
        s.sibc(i, 0, s.d).start()
    def e2(s, i):
        s.bx(i, s.xn, s.xn, 3).wait_recv()
        s.bx(i, s.xn, s.yn, 5, 0).start()
        if not s.items[i][3]: s.sibc(i, 1, s.xn).start()
    def e3(s, i):
        s.bx(i, s.yn, s.yn, 4).wait_recv()
        s.bx(i, s.yn, s.xn, 6, 1).start()
        if not s.items[i][3]: s.sibc(i, 2, s.yn).start()
    def e4(s, i):
        s.bx(i, s.dg, s.yn, 5, 0).wait_recv()
        s.bx(i, s.dg, s.xn, 6, 1).wait_recv()
        if not s.items[i][3]: s.sibc(i, 3, s.dg).start()
    def z1(s, i):
        for j in range(1, s.nz):
            for d in s.chips:
                s.cp(s.part(i, d, s.z), s.part(i, d, s.z), i, j - 1, (s.d, (s.z + j) % s.nz)).start()
    def zall(s, i, j):
        w, r0, n, _ = s.items[i]
        ref = s.full[w]
        ref = ref.at[pl.ds(0, ref.shape[0] // s.nz), pl.ds(0, 4 * n)] if w == 2 else ref.at[pl.ds(0, 4 * n), pl.ds(0, ref.shape[1] // s.nz)]
        return s.cp(ref, ref, i, j - 1, (s.d, (s.z + j) % s.nz))
    def z2(s, i):
        for j in range(1, s.nz): s.zall(i, j).wait_recv()
        for k, d in enumerate(s.chips): s.sibc(i, k, d).start()
    def e5(s, i, ks=(0, 1, 2, 3)):
        for k in ks:
            s.sibc(i, k, s.chips[k] + s.sib - s.d).wait_recv()
    def order(s, i):
        return (i // 2 + s.d // 4) % 2 * 2 + (i + s.d // 2) % 2
    def finish(s, i):
        if s.items[i][0] < 4:
            for j in range(1, s.nz):
                (s.zall(i, j) if s.items[i][3] else s.zc(i, j)).wait_send()
        s.bx(i, s.d, s.xn, 3).wait_send()
        s.bx(i, s.d, s.yn, 4).wait_send()
        s.bx(i, s.xn, s.yn, 5, 0).wait_send()
        s.bx(i, s.yn, s.xn, 6, 1).wait_send()
        for k, b in enumerate(s.chips):
            s.sibc(i, k, b).wait_send()


class Reduce(Comm):
    def __init__(s, hbm, far, near, v, sems):
        super().__init__()
        s.hbm = hbm; s.v = v; s.near = near
        s.pP, s.pF, s.pZ = far
        s.sems = sems
        s.chips = (s.dg, s.xn, s.yn, s.d)
        s.fr = hbm[2].shape[0] // s.nz; s.fc = hbm[2].shape[1] // 8
        s.f1 = s.pF.shape[1] // s.nz; s.f2 = s.fr - s.f1
        s.qr = hbm[0].shape[0] // 8; s.orr = hbm[1].shape[0] // 8
        s.pr = hbm[3].shape[0] // 8; s.pc = hbm[3].shape[1] // s.nz
        s.p1 = s.pZ.shape[1] // 8; s.p2 = s.pr - s.p1
        q1 = s.qr // 32 * 16 // 32 * 32
        s.qi = ((0, q1), (q1, s.qr - q1))
    def cp(s, src, dst, kind, i, dev):
        a, b = s.sems[kind]
        return pltpu.make_async_remote_copy(src_ref=src, dst_ref=dst, send_sem=a.at[i], recv_sem=b.at[i], device_id=dev, device_id_type=MESH)
    def rows(s, ref, d, n, a=0, m=None): return ref.at[pl.ds(pl.multiple_of(d * n + a, 16), n if m is None else m), :]
    def pp(s, k):
        dev = s.peers[k - 1]
        return s.cp(s.rows(s.hbm[3], dev[0], s.pr, s.p1, s.p2), s.pP.at[k - 1], "p", k - 1, dev)
    def zpart(s, z, d): return s.hbm[3].at[pl.ds(d * s.pr, s.p1), pl.ds(pl.multiple_of(z * s.pc, 128), s.pc)]
    def pz(s, j, d):
        dev = s.peers[6 + j]
        return s.cp(s.zpart(dev[1], d), s.pZ.at[j - 1, pl.ds(d * s.p1, s.p1)], "y", j - 1, dev)
    def pz_all(s, j): return s.cp(s.pZ.at[j - 1], s.pZ.at[j - 1], "y", j - 1, s.peers[6 + j])
    def start_p(s):
        for j in range(1, s.nz):
            for d in range(8): s.pz(j, d).start()
        for k in range(1, 8): s.pp(k).start()
    def fpart(s, d, z, a, n): return s.hbm[2].at[pl.ds(z * s.fr + a, n), pl.ds(pl.multiple_of(d * s.fc, 128), s.fc)]
    def pf_all(s, k): return s.cp(s.pF.at[k - 1], s.pF.at[k - 1], "f", k - 1, s.peers[k - 1])
    def start_f(s):
        for k in range(1, 8):
            dev = s.peers[k - 1]
            for z in range(s.nz):
                s.cp(s.fpart(dev[0], z, 0, s.f1), s.pF.at[k - 1, pl.ds(z * s.f1, s.f1)], "f", k - 1, dev).start()
    def s0all(s, w, i): return s.cp(s.near[w].at[i], s.near[w].at[i], "s", w * 4 + i, (s.sib, s.z))
    def start_s(s, w):
        for i in range(4):
            d = s.chips[i] + s.sib - s.d
            if w == 2:
                for z in range(s.nz):
                    s.cp(s.fpart(d, z, s.f1, s.f2), s.near[2].at[i, pl.ds(z * s.f2, s.f2)], "s", w * 4 + i, (s.sib, s.z)).start()
            else:
                s.cp(s.rows(s.hbm[w], d, s.qr if w == 0 else s.orr), s.near[w].at[i], "s", w * 4 + i, (s.sib, s.z)).start()
    def own(s, t, i):
        v = s.v
        if t < 2: return v.QT.at[pl.ds(i * s.qr + s.qi[t][0], s.qi[t][1])]
        if t == 2: return v.OT.at[pl.ds(i * s.orr, s.orr)]
        if t == 3: return v.F.at[pl.ds(s.nz * s.f1, s.nz * s.f2), pl.ds(i * s.fc, s.fc)]
        if t == 4: return v.m.at[pl.ds(pl.multiple_of(8 * s.p1 + s.chips[i] * s.p1, 16), s.p1), pl.ds(s.pc, s.pc)]
        return v.gv.at[s.chips[i]]
    def sb(s, t, i):
        v = s.v
        if t < 2: return v.QT.at[pl.ds((4 + i) * s.qr + s.qi[t][0], s.qi[t][1])]
        if t == 2: return v.OT.at[pl.ds((4 + i) * s.orr, s.orr)]
        if t == 3: return v.F.at[pl.ds(s.nz * s.f1, s.nz * s.f2), pl.ds((4 + i) * s.fc, s.fc)]
        if t == 4: return v.m.at[pl.ds((8 + i) * s.p1, s.p1), pl.ds(2 * s.pc, s.pc)]
        return v.vs.at[i]
    def land(s, t, what):
        v = s.v
        i = ("rx", "ry", "ra", "rb", "zs").index(what)
        if t == 3:
            n = s.nz * s.f2; base = s.nz * s.f1 + s.f1; k = split(n)
            a, m, c = [(0, n, 0), (0, n, 1), (0, k, 2), (k, n - k, 2), (0, n, 3)][i]
            return v.gp.at[pl.ds(base + a, m), pl.ds(c * s.fc, s.fc)]
        if t == 5:
            return [v.vs.at[4], v.vs.at[5], v.vs.at[6, pl.ds(0, 8)], v.vs.at[6, pl.ds(8, 8)], v.vs.at[7]][i]
        if t == 4: ref, base, n = v.m, 12 * s.p1, s.p1
        elif t == 2: ref, base, n = v.A, 0, s.orr
        else: ref, base, n = v.n1, t * 3 * s.qi[0][1], s.qi[t][1]
        k = split(n)
        a, m = [(0, n), (n, n), (2 * n, k), (2 * n + k, n - k)][i]
        return ref.at[pl.ds(base + a, m), pl.ds(2 * s.pc, s.pc)] if t == 4 else ref.at[pl.ds(base + a, m)]
    def half(s, ref, h):
        n = ref.shape[0]; k = split(n)
        return ref.at[pl.ds(0, k)] if h == 0 else ref.at[pl.ds(k, n - k)]
    def load_own(s, t):
        for i in range(4):
            sem = s.v.lsem.at[t * 8 + i]
            if t == 3:
                for z in range(s.nz):
                    pltpu.make_async_copy(s.fpart(s.chips[i], z, s.f1, s.f2), s.own(3, i).at[pl.ds(z * s.f2, s.f2)], sem).start()
            elif t == 2:
                pltpu.make_async_copy(s.rows(s.hbm[1], s.chips[i], s.orr), s.own(2, i), sem).start()
            else:
                pltpu.make_async_copy(s.rows(s.hbm[0], s.chips[i], s.qr, *s.qi[t]), s.own(t, i), sem).start()
    def near_of(s, t, i):
        if t < 2: return s.near[0].at[i, pl.ds(*s.qi[t])]
        return s.near[t - 1].at[i]
    def load_sib(s, t):
        for i in range(4):
            if t != 1: s.s0all(max(t - 1, 0), i).wait_recv()
            pltpu.make_async_copy(s.near_of(t, i), s.sb(t, i), s.v.lsem.at[t * 8 + 4 + i]).start()
    def slot_p(s, k): return s.v.PT.at[pl.ds(k * s.p2, s.p2)]
    def slot_f(s, k): return s.v.F.at[pl.ds(0, s.nz * s.f1), pl.ds(k * s.fc, s.fc)]
    def slot_z(s, j): return s.v.m.at[pl.ds(j // 3 * 8 * s.p1, 8 * s.p1), pl.ds(j % 3 * s.pc, s.pc)]
    def load_p(s):
        pltpu.make_async_copy(s.rows(s.hbm[3], s.d, s.pr, s.p1, s.p2), s.slot_p(0), s.v.lsem.at[32]).start()
        for k in range(1, 8):
            s.pp(k).wait_recv()
            pltpu.make_async_copy(s.pP.at[k - 1], s.slot_p(k), s.v.lsem.at[32 + k]).start()
    def load_f(s):
        for z in range(s.nz):
            pltpu.make_async_copy(s.fpart(s.d, z, 0, s.f1), s.slot_f(0).at[pl.ds(z * s.f1, s.f1)], s.v.lsem.at[40]).start()
        for k in range(1, 8):
            s.pf_all(k).wait_recv()
            pltpu.make_async_copy(s.pF.at[k - 1], s.slot_f(k), s.v.lsem.at[40 + k]).start()
    def load_z(s):
        for d in range(8):
            pltpu.make_async_copy(s.zpart(s.z, d), s.slot_z(0).at[pl.ds(d * s.p1, s.p1)], s.v.lsem.at[48]).start()
        for j in range(1, s.nz):
            s.pz_all(j).wait_recv()
            pltpu.make_async_copy(s.pZ.at[j - 1], s.slot_z(j), s.v.lsem.at[48 + j]).start()
    def loaded(s, ref, sem): pltpu.make_async_copy(ref, ref, s.v.lsem.at[sem]).wait()
    def cc(s, i): return s.cp(s.v.cs.at[0], s.v.cs.at[1 + i], "c", i, s.peers[i])
    def factors(s, c):
        s.v.cs[0] = jnp.full(s.v.cs.shape[1:], c, f32)
        for i in range(len(s.peers)): s.cc(i).start()
    def wait_factors(s):
        for i in range(len(s.peers)): s.cc(i).wait_recv()
    def c(s, i): return s.v.cs[i, 0:1, 0:1]
    def sibv(s, t, i):
        d = s.chips[i] + s.sib - s.d
        src = s.v.gv.at[d] if t == 5 else s.v.m.at[pl.ds(pl.multiple_of(8 * s.p1 + d * s.p1, 16), s.p1), pl.ds(s.pc, s.pc)]
        return s.cp(src, s.sb(t, i), "n", t * 13 + i, (s.sib, s.z))
    def start_v(s, t):
        for i in range(4): s.sibv(t, i).start()
    def sum_p(s):
        for k in range(8): s.loaded(s.slot_p(k), 32 + k)
        for q in range(s.nz):
            cols = slice(q * s.pc, (q + 1) * s.pc)
            t = sum(s.c(k) * s.v.PT[k * s.p2:(k + 1) * s.p2, cols].astype(f32) for k in range(8))
            s.v.PT[8 * s.p2:9 * s.p2, cols] = t.astype(bf16)
        s.zfirst("p")
    def zpart_of(s, t, k):
        if t == "p": return s.v.PT.at[pl.ds(8 * s.p2, s.p2), pl.ds(pl.multiple_of(k * s.pc, 128), s.pc)]
        if t == "f": return s.v.n2.at[pl.ds(pl.multiple_of(k * s.f1, 16), s.f1), pl.ds(0, s.fc)]
        return s.zpiece(t, k)
    def zland_of(s, t, j):
        if t == "p": return s.v.PT.at[pl.ds(9 * s.p2, s.p2), pl.ds(j * s.pc, s.pc)]
        if t == "f": return s.v.n2.at[pl.ds((s.nz + j // 2) * s.f1, s.f1), pl.ds(j % 2 * s.fc, s.fc)]
        return s.zland(t, j)
    def zcp(s, t, j):
        a, b = s.z + 1 - 2 * (s.z % 2), (s.z + 2) % 4
        k, to = ((a, a), (3 - s.z, a), (b, b))[j]
        kind, i = ("z", "pf".index(t) * 3 + j) if t in ("p", "f") else ("n", t * 13 + 10 + j)
        return s.cp(s.zpart_of(t, k), s.zland_of(t, j), kind, i, (s.d, to))
    def zfirst(s, t):
        s.zcp(t, 1).start(); s.zcp(t, 0).start()
    def zsecond(s, t):
        s.zcp(t, 1).wait_recv()
        ref = s.zpart_of(t, (s.z + 2) % 4)
        ref[...] = (ref[...].astype(f32) + s.zland_of(t, 1)[...].astype(f32)).astype(bf16)
        s.zcp(t, 2).start()
    def zsum(s, t):
        s.zcp(t, 0).wait_recv(); s.zcp(t, 2).wait_recv()
        return s.zpart_of(t, s.z)[...].astype(f32) + s.zland_of(t, 0)[...].astype(f32) + s.zland_of(t, 2)[...].astype(f32)
    def zsent(s, t):
        for j in range(3): s.zcp(t, j).wait_send()
    def fin_p(s): s.v.out[3][s.p1:, :] = s.zsum("p")
    def sum_f(s):
        for k in range(8): s.loaded(s.slot_f(k), 40 + k)
        for q in range(s.nz):
            rows = slice(q * s.f1, (q + 1) * s.f1)
            t = sum(s.c(k) * s.v.F[rows, k * s.fc:(k + 1) * s.fc].astype(f32) for k in range(8))
            s.v.n2[rows, 0:s.fc] = t.astype(bf16)
        s.zfirst("f")
    def fin_f(s): s.v.out[2][0:s.f1, :] = s.zsum("f")
    def sum_z(s):
        for j in range(s.nz): s.loaded(s.slot_z(j), 48 + j)
        n = s.p1
        for d in range(8):
            t = s.c(0) * s.v.m[d * n:(d + 1) * n, 0:s.pc].astype(f32)
            for j in range(1, s.nz):
                a = j // 3 * 8 * n + d * n; b = j % 3 * s.pc
                t = t + s.c(7 + j) * s.v.m[a:a + n, b:b + s.pc].astype(f32)
            s.v.m[(8 + d) * n:(9 + d) * n, s.pc:2 * s.pc] = t.astype(bf16)
        s.start_v(4)
    def mixed(s, t, i):
        if t < 4:
            s.loaded(s.own(t, i), t * 8 + i); s.loaded(s.sb(t, i), t * 8 + 4 + i)
        else:
            s.sibv(t, i).wait_recv()
        a, b = s.own(t, i)[...].astype(f32), s.sb(t, i)[...].astype(f32)
        if t == 4: return a + b
        return s.c(0) * a + s.v.cs[(s.d - s.sib + 8) % 8, 0:1, 0:1] * b
    def nc(s, src, dst, t, slot, dev): return s.cp(src, dst, "n", t * 13 + slot, (dev, s.z))
    def ca(s, t): return s.nc(s.half(s.sb(t, 0), 0), s.land(t, "ra"), t, 4, s.xn)
    def cb(s, t): return s.nc(s.half(s.sb(t, 0), 1), s.land(t, "rb"), t, 5, s.yn)
    def cx(s, t, h): return s.nc(s.half(s.sb(t, 1), h), s.half(s.land(t, "rx"), h), t, 6 + h, s.xn)
    def cy(s, t, h): return s.nc(s.half(s.sb(t, 2), h), s.half(s.land(t, "ry"), h), t, 8 + h, s.yn)
    def a(s, t):
        def put(i):
            ref = s.sb(t, i)
            ref[...] = s.mixed(t, i).astype(ref.dtype)
        put(0); s.ca(t).start(); s.cb(t).start()
        put(1); s.cx(t, 0).start()
        put(2); s.cy(t, 1).start()
    def r(s, t):
        s.ca(t).wait_recv()
        x = s.half(s.sb(t, 2), 0)
        x[...] = (x[...].astype(f32) + s.land(t, "ra")[...].astype(f32)).astype(x.dtype)
        s.cy(t, 0).start()
        s.cb(t).wait_recv()
        x = s.half(s.sb(t, 1), 1)
        x[...] = (x[...].astype(f32) + s.land(t, "rb")[...].astype(f32)).astype(x.dtype)
        s.cx(t, 1).start()
    def packed(s, t):
        r0, n = s.qi[t] if t < 2 else (0, s.orr)
        return pl.ds(r0 * 3 // 2, n * 3 // 2)
    def zpiece(s, t, k):
        if t < 3: return (s.v.zq, s.v.zq, s.v.zo)[t].at[k, s.packed(t)]
        ref = s.land(t, "zs")
        return ref if t == 5 else ref.at[pl.ds(pl.multiple_of(k * s.f2, 16), s.f2)]
    def zland(s, t, j):
        if t < 3: return (s.v.zrq, s.v.zrq, s.v.zro)[t].at[j, s.packed(t)]
        if t == 5: return s.v.vs.at[8 + j]
        return s.v.gp.at[pl.ds(s.nz * s.f1 + s.f1 + j * s.f2, s.f2), pl.ds(4 * s.fc, s.fc)]
    def zc(s, t, j):
        dev = s.peers[6 + j]
        return s.cp(s.zpiece(t, dev[1]), s.zland(t, j - 1), "n", t * 13 + 9 + j, dev)
    def f(s, t):
        x = s.mixed(t, 3)
        for h in (0, 1):
            s.cx(t, h).wait_recv(); s.cy(t, h).wait_recv()
        x = x + s.land(t, "rx")[...].astype(f32) + s.land(t, "ry")[...].astype(f32)
        if t == 4:
            s.v.out[3][0:s.p1, :] = x
            return
        if t < 3:
            c = x.shape[1] // s.nz
            for k in range(s.nz): s.zpiece(t, k)[...] = pack(x[:, k * c:(k + 1) * c].astype(bf16))
        else:
            ref = s.land(t, "zs")
            ref[...] = x.astype(ref.dtype)
        if t == 5:
            for j in range(1, s.nz): s.zc(t, j).start()
        else:
            s.zfirst(t)
    def fin(s, t):
        if t == 5:
            for j in range(1, s.nz): s.zc(t, j).wait_recv()
            x = s.zpiece(t, s.z)[...]
            for j in range(s.nz - 1): x = x + s.zland(t, j)[...]
            s.v.out[4][...] = x
            return
        x = s.zsum(t)
        if t == 3: s.v.out[2][s.f1:, :] = x
        elif t == 2: s.v.out[1][...] = unpack(x)
        else: s.v.out[0][s.qi[t][0]:s.qi[t][0] + s.qi[t][1], :] = unpack(x)
    def finish(s):
        for k in range(1, 8): s.pp(k).wait_send(); s.pf_all(k).wait_send()
        for j in range(1, s.nz): s.pz_all(j).wait_send()
        for w in range(3):
            for i in range(4): s.s0all(w, i).wait_send()
        for i in range(len(s.peers)): s.cc(i).wait_send()
        for t in range(6):
            if t > 3:
                for i in range(4): s.sibv(t, i).wait_send()
            s.ca(t).wait_send(); s.cb(t).wait_send()
            for h in (0, 1): s.cx(t, h).wait_send(); s.cy(t, h).wait_send()
            if t == 5:
                for j in range(1, s.nz): s.zc(t, j).wait_send()
            elif t != 4: s.zsent(t)
        s.zsent("p"); s.zsent("f")


def block_kernel(names, remote, length, tok, cot, *refs):
    refs = list(refs)
    take = lambda n: [refs.pop(0) for _ in range(n)]
    if remote:
        clip, *raw = take(7)
        y, gx, ratio, *outs = take(8)
        gq, go, gf, gp, sQ, sO, sF, pP, pF, pZ = take(10)
        QT, OT, F, PT, V, sq, so, sf, sp, sv, zq, zo, send, recv = take(14)
        gv, vs, cs, zrq, zro, lsem, *rsem = take(20)
    else:
        QT, OT, F, PT, vec, bf = take(6)
        y, gx, gq, go, gf, gp, col, dbf, ss = take(9)
        V = None
    s = Block(length=length[0], QT=QT, OT=OT, F=F, PT=PT, V=V, **dict(zip(names, refs)))
    D = s.x.shape[1]; FF = s.u.shape[1]
    cx = pltpu.make_async_copy(tok, s.x, s.isem.at[0]); cx.start()
    ce = pltpu.make_async_copy(cot, s.ey, s.isem.at[1]); ce.start()
    if remote:
        places = types.SimpleNamespace(QT=QT, OT=OT, F=F, PT=PT, m=s.m, gp=s.gp, n1=s.n1, n2=s.n2, A=s.A, gv=gv, vs=vs, cs=cs, zq=zq, zo=zo, zrq=zrq, zro=zro, lsem=lsem, out=outs)
        red = Reduce((gq, go, gf, gp), (pP, pF, pZ), (sQ, sO, sF), places, {k: (rsem[2 * i], rsem[2 * i + 1]) for i, k in enumerate("pfysczn")})
        greet(g_peers := Comm().peers)
        qn = raw[0].shape[1]
        cuts = [0, 64, 128, 192, qn]
        fc = F.shape[1] // 8; pr = sp.shape[0]
        p0 = pr // 48 * 32
        items = [(4, 0, 16, False)] + [(0, a, b - a, False) for a, b in zip(cuts, cuts[1:])] + [(1, 0, raw[1].shape[1], False),
            (2, 0, fc, False), (3, 0, p0, False), (3, p0, pr - p0, True)]
        g = Gather(items, (sq, so, sf, sp, sv), (zq, zo), (QT, OT, F, PT, V), send, recv)
        q = raw[0][...].astype(bf16).T
        for a, b in zip(cuts, cuts[1:]): sq[a * 3 // 2:b * 3 // 2, :] = pack(q[a:b])
        so[...] = pack(raw[1][...].astype(bf16).T)
        sf[...] = raw[2][...].astype(bf16)
        sp[...] = raw[3][...].astype(bf16)
        sv[...] = jnp.zeros_like(sv)
        sv[0:8, 0:raw[5].shape[1]] = raw[5][...]
        nb = raw[4].shape[0] // 128
        for j in range(nb): sv[8 + j:9 + j, :] = raw[4][j * 128:(j + 1) * 128].reshape(1, 128)
        pl.semaphore_wait(pltpu.get_barrier_semaphore(), len(g_peers))
        v, q1, q2, q3, q4, o, f, p, p2 = range(9)
        qs = (q1, q2, q3, q4)
        for i in qs + (o, v, p2): g.start(i)
        g.e1(v); g.e2(v); g.e3(v); g.e2(p2); g.e3(p2); g.e4(v); g.e1(q1); g.e5(v); s.unpack(); cx.wait(); s.ln1(); ce.wait(); s.ey_mask(); s.turn(s.ey, 0)
        g.e1(q2); g.start(f); g.e2(q1); g.e3(q1); g.e1(q3); g.e2(q2); g.e3(q2); g.e4(q1); g.e1(q4); g.e2(q3); g.e3(q3); g.e4(q2)
        g.e1(o); g.start(p); g.e2(q4); g.e3(q4); g.e4(q3); g.e4(p2); g.z1(p2); g.e4(q4)
        for i in qs: g.e5(i)
        s.qkv({2: lambda: (g.e2(o), g.e3(o))})
        g.e1(f)
        loop(D // 128, s.attend, {1: lambda: g.e4(o), 3: lambda: g.e1(p)})
        g.e5(o); g.e2(f); g.e3(f)
        s.out(); s.ln2(); g.e5(f, (0, 1, 2))
        s.fc({6: lambda: (g.e2(p), g.e3(p)), 9: lambda: (g.e4(f), g.e5(f, (3,)))}, g.order)
    else:
        s.vec[...] = vec[...]; s.bf[...] = bf[...]
        s.clear(); cx.wait()
        s.ln1(); ce.wait(); s.ey_mask(); s.turn(s.ey, 0); s.qkv()
        loop(D // 128, s.attend)
        s.out(); s.ln2(); s.fc()
    s.wgrad(s.ey, s.u, gp, FF, 512, {3: lambda: g.e4(p), 5: lambda: g.z2(p2)} if remote else {}, True)
    if remote: red.start_p(); g.e5(p); g.e5(p2)
    s.ef_y(); s.wgrad(s.n2, s.gp, gf, FF, 512)
    cy = pltpu.make_async_copy(s.er, y, s.isem.at[2]); cy.start()
    if remote: red.start_f(); red.start_s(2)
    s.gn2()
    cy.wait()
    s.ln2b(); s.wgrad(s.er, s.A, go, D, 256)
    if remote: red.start_s(1)
    s.eA()
    loop(D // 128, s.attend_back)
    cx = pltpu.make_async_copy(tok, s.A, s.isem.at[0]); cx.start()
    s.wgrad(s.u, s.n1, gq, D, 256)
    if remote:
        for i in range(len(items)): g.finish(i)
        red.start_s(0); red.load_own(2); red.load_own(3); red.load_sib(2); red.load_sib(3); red.load_p()
    s.bias_cols(); s.gn1()
    if remote: red.load_own(0); red.load_own(1); red.load_z()
    cx.wait(); s.ln1b()
    cg = pltpu.make_async_copy(s.er, gx, s.isem.at[3]); cg.start()
    if remote: red.load_sib(0); red.load_sib(1)
    norm2 = s.norm()
    if not remote:
        ss[0] = norm2
        cg.wait()
        col[...] = s.col[...]; dbf[...] = s.dbf[...]
        return
    norm = jnp.sqrt(jnp.full((8, 128), norm2, f32))
    ratio[...] = norm / clip[0]
    red.factors(jnp.minimum(1.0, clip[0] / norm))
    w = D // 8
    for d in range(8):
        gv[d, 0:8, 0:w] = s.col[:, d * w:(d + 1) * w]
        gv[d, 0:8, w:128] = jnp.zeros((8, 128 - w), f32)
        for j in range(8):
            k = d * nb + j
            gv[d, 8 + j:9 + j, :] = s.dbf[:, k * 128:(k + 1) * 128] if j < nb else jnp.zeros((1, 128), f32)
    q1, q2, o, f, h, v = range(6)
    red.load_f()
    red.wait_factors()
    red.start_v(v)
    red.a(q1); red.a(q2); red.sum_p(); red.r(q1); red.a(f); red.sum_f(); red.a(v); red.r(q2); red.f(q1); red.zsecond("p"); red.sum_z(); red.a(o); red.r(v)
    red.r(f); red.zsecond("f"); red.f(q2); red.zsecond(q1); red.a(h); red.r(o); red.f(v); red.f(f); red.zsecond(q2); red.r(h); red.fin_p(); red.fin_f()
    red.f(o); red.zsecond(f); red.fin(q1); red.f(h); red.zsecond(o); red.fin(q2); red.fin(v); red.fin(f); red.fin(o)
    red.finish()
    cg.wait()


def run_block(remote, length, tok, cot, *ws):
    L, D = tok.shape
    sd = jax.ShapeDtypeStruct
    dma = pltpu.SemaphoreType.DMA
    V = pltpu.VMEM
    vm = pl.BlockSpec(memory_space=pltpu.VMEM); an = pl.BlockSpec(memory_space=pl.ANY); sm = pl.BlockSpec(memory_space=pltpu.SMEM)
    extra = []
    if remote:
        nz = lax.axis_size("fsdp")
        clip, q, o, f, p, b, v = ws
        FF = f.shape[1] * 8
        qt, ot, pt = q.shape[::-1], o.shape[::-1], p.shape
        qp, op = (qt[0] * 3 // 2, 128), (ot[0] * 3 // 2, 128)
        fr = D // nz; f1 = fr // 96 * 80; fc = FF // 8; pr = D // 8; p1 = pr // 32 * 16; pc = FF // nz
        extra = [V((3 * D, D), bf16), V((D, D), bf16), V((D, FF), bf16), V((D, FF), bf16), V((8, 16, 128), f32),
            V(qp, bf16), V(op, bf16), V(f.shape, bf16), V(pt, bf16), V((16, 128), f32),
            V((nz,) + qp, bf16), V((nz,) + op, bf16), dma((9, 11)), dma((9, 11)),
            V((8, 16, 128), f32), V((12, 16, 128), f32), V((8 + nz - 1, 8, 128), f32), V((nz - 1,) + qp, bf16), V((nz - 1,) + op, bf16), dma((52,))]
        for n in (7, 7, 3, 12, 10, 6, 78): extra += [dma((n,)), dma((n,))]
        outs = [sd((8, 128), f32), sd(qt, f32), sd(ot, f32), sd(f.shape, f32), sd(pt, f32), sd((16, 128), f32)]
        hbm = [sd((4, 3 * D // 8, D), bf16), sd((4, pr, D), bf16), sd((4, nz * (fr - f1), fc), bf16),
            sd((7, pr - p1, FF), bf16), sd((7, nz * f1, fc), bf16), sd((nz - 1, 8 * p1, pc), bf16)]
        ins = [sm] + [vm] * 6
    else:
        FF = ws[2].shape[1]
        ins = [vm] * len(ws)
    acts = [sd((L, D), bf16), sd((L, D), bf16)]
    grads = [sd((3 * D, D), bf16), sd((D, D), bf16), sd((D, FF), bf16), sd((D, FF), bf16)]
    scr = scratch(L, D, FF)
    params = dict(collective_id=0, has_side_effects=True) if remote else {}
    if remote:
        shapes = acts + outs + grads + hbm
        specs = [an] * 2 + [vm] * 6 + [an] * 10
    else:
        shapes = acts + grads + [sd((8, D), f32), sd((1, FF), f32), sd((1,), f32)]
        specs = [an] * 6 + [vm, vm, sm]
    return pl.pallas_call(functools.partial(block_kernel, list(scr), remote), out_shape=shapes,
        in_specs=[sm, an, an] + ins, out_specs=specs, scratch_shapes=extra + list(scr.values()),
        compiler_params=pltpu.CompilerParams(vmem_limit_bytes=VLIM, **params))(length, tok, cot, *ws)


VLIM = (63 << 20) + (900 << 10)


def last_kernel(examples, ratio, sq, so, sf, sp, sv, nq, no, nf, np_, nb, nv, oratio, oq, oo, of, op, ob, ov):
    oratio[0] = jnp.sum(ratio[0:1, 0:1])
    e = 1.0 / examples
    oq[...] = sq[...].T * e + nq[...]
    oo[...] = so[...].T * e + no[...]
    of[...] = sf[...] * e + nf[...]
    op[...] = sp[...] * e + np_[...]
    for j in range(ob.shape[0] // 128):
        ob[j * 128:(j + 1) * 128] = sv[8 + j:9 + j, :].reshape(128) * e + nb[j * 128:(j + 1) * 128]
    ov[...] = sv[0:8, 0:ov.shape[1]] * e + nv[...]


def shards(tokens, qkv_weight, out_weight, fc_weight, proj_weight, fc_bias, vectors, cotangent, lengths, clip_norm,
           noise_qkv, noise_out, noise_fc, noise_proj, noise_fc_bias, noise_vectors):
    ndp, nz = lax.axis_size("dp"), lax.axis_size("fsdp")
    examples = ndp * nz
    noises = (noise_qkv, noise_out, noise_fc, noise_proj, noise_fc_bias, noise_vectors)
    if ndp == 8:
        y, gx, ratio, sq, so, sf, sp, sv, *_ = run_block(True, lengths, tokens, cotangent, clip_norm.reshape(1), qkv_weight, out_weight, fc_weight, proj_weight.T, fc_bias, vectors)
        sd = jax.ShapeDtypeStruct
        vm = pl.BlockSpec(memory_space=pltpu.VMEM); sm = pl.BlockSpec(memory_space=pltpu.SMEM)
        pt = proj_weight.shape[::-1]
        ratio, gq, go, gf, gp, gb, gv = pl.pallas_call(functools.partial(last_kernel, examples),
            out_shape=[sd((1,), f32), sd(qkv_weight.shape, f32), sd(out_weight.shape, f32), sd(fc_weight.shape, f32), sd(pt, f32), sd(fc_bias.shape, f32), sd(vectors.shape, f32)],
            in_specs=[vm] * 12, out_specs=[sm] + [vm] * 6)(
            ratio, sq, so, sf, sp, sv, noise_qkv, noise_out, noise_fc, noise_proj.T, noise_fc_bias, noise_vectors)
        return y, gx, ratio, gq, go, gf, gp.T, gb, gv
    g = lambda a: lax.all_gather(lax.all_gather(a.astype(bf16), "dp", axis=1, tiled=True), "fsdp", axis=0, tiled=True)
    vec = lax.all_gather(vectors.astype(bf16), "dp", axis=1, tiled=True).astype(f32)
    bf = lax.all_gather(fc_bias.astype(bf16), "dp", axis=0, tiled=True).astype(f32).reshape(1, -1)
    y, gx, gq, go, gf, gp, col, dbf, ss = run_block(False, lengths, tokens, cotangent, g(qkv_weight).T, g(out_weight).T, g(fc_weight), g(proj_weight).T, vec, bf)
    norm = jnp.sqrt(ss)
    factor = jnp.minimum(1.0, clip_norm / norm)
    ps = lambda a, dim: lax.psum_scatter(factor * a.astype(f32), "dp", scatter_dimension=dim, tiled=True)
    pz = lambda a: lax.psum_scatter(a.astype(bf16), "fsdp", scatter_dimension=0, tiled=True).astype(f32)
    finals = tuple(pz(ps(a, 1)) for a in (gq.T, go.T, gf, gp.T)) + lax.psum((ps(dbf[0], 0), ps(col, 1)), "fsdp")
    return (y, gx, norm / clip_norm) + tuple(a / examples + n for a, n in zip(finals, noises))


def solution(mesh):
    both, cut = P(("dp", "fsdp"), None), P("fsdp", "dp")
    weights = (cut, cut, cut, cut, P("dp"), P(None, "dp"))
    return jax.shard_map(shards, mesh=mesh, in_specs=(both,) + weights + (both, P(("dp", "fsdp")), P()) + weights,
        out_specs=(both, both, P(("dp", "fsdp"))) + weights, check_vma=False)
```
